512 devices in a mesh: group: 2 (over core), dp: 16 (over z, y_hi), mp: 16 (over y_lo, x).
Axes of the slice: x: 4, y: 8 (y_hi: 2, y_lo: 4; y = y_hi * 4 + y_lo), z: 8, core: 2. Of those that a mesh axis runs over, the one named last changes fastest.
Arguments:
- queries: bfloat16 [1024, 4, 16384], P('dp', None, 'mp'), may hold values from -160 to 160
- cache_keys: bfloat16 [1024, 64, 1024], P(('dp', 'mp')), may hold values from -6 to 6
- cache_values: bfloat16 [1024, 64, 1024], P(('dp', 'mp')), may hold values from -6 to 6
- slot_keys: bfloat16 [1024, 4, 1024], P(('dp', 'mp')), may hold values from -6 to 6
- slot_values: bfloat16 [1024, 4, 1024], P(('dp', 'mp')), may hold values from -6 to 6
- cache_lengths: int32 [1024], P(('dp', 'mp')), may hold values from 2 to 64, as said below
- embeddings: bfloat16 [1024, 4, 16384], P('dp', None, 'mp'), may hold values from -160 to 160
- layer_low: bfloat16 [1024, 4, 16384], P('dp', None, 'mp'), may hold values from -160 to 160
- layer_mid: bfloat16 [1024, 4, 16384], P('dp', None, 'mp'), may hold values from -160 to 160
- accepted: int32 [1024], P('dp'), may hold values from 0 to 4
- join_gain: float32 [3, 16384], P(None, 'mp'), may hold values from 0.5 to 2
- norm_gain: float32 [2, 16384], P(None, 'mp'), may hold values from 0.5 to 2
- key_cotangent: bfloat16 [1024, 4, 1024], P('dp', None, 'mp'), may hold values from -64 to 64
- key_weight: float32 [1024, 2, 16384], P(('group', 'dp'), None, 'mp'), may hold values from -5 to 5
- moment_first: float32 [1024, 2, 16384], P(('group', 'dp'), None, 'mp'), may hold values from -4 to 4
- moment_second: float32 [1024, 2, 16384], P(('group', 'dp'), None, 'mp'), may hold values from 0.5 to 5
Outputs:
- key_weight_new: float32 [1024, 2, 16384], P(('group', 'dp'), None, 'mp')
- moment_first_new: float32 [1024, 2, 16384], P(('group', 'dp'), None, 'mp')
- moment_second_new: float32 [1024, 2, 16384], P(('group', 'dp'), None, 'mp')
- gain_grad: float32 [2, 16384], P(None, 'mp')
The draws below stay inside these ranges and needn't reach their ends.
Inputs may be any that keep to these rules, and one draw needn't show every extreme that they name: `cache_lengths`: some row has exactly 64.
All inputs are finite; a program needn't handle non-finite values.
Results may differ from the reference program's by a relative error of at most 0.017.
Values may be sent and summed in bfloat16 or wider, within the bound.
A program may use at most 128 MiB of HBM per device.

```python
import math
import jax
import jax.numpy as jnp
from jax import lax

D = 16384
HEADS = 128
KVH = 8
HD = 128
KVD = 1024
SLOTS = 4
ROWS_DEV = 64
CACHE = 64
ROWS = 1024
N_DP = 16


def drawn_pair(key):
    keys_base = jnp.clip(jax.random.normal(jax.random.fold_in(key, 11), (ROWS, CACHE, KVD), jnp.float32), -6.0, 6.0)
    return keys_base


def draw_cache_keys(key, part):
    keys_base = drawn_pair(key)
    return keys_base.astype(jnp.bfloat16)


def draw_queries(key, part):
    key = jax.random.fold_in(key, 2)
    base_values = jnp.clip(jax.random.normal(key, (ROWS, SLOTS, D), jnp.float32), -6.0, 6.0)
    return base_values.astype(jnp.bfloat16)


def profile_rows(key, noise):
    column_scale = 3.0 ** (jnp.arange(D, dtype=jnp.float32) / D)
    row_scale = 10.0 ** jax.random.uniform(jax.random.fold_in(key, 99), (ROWS, SLOTS, 1), jnp.float32)
    return noise * column_scale * row_scale


def draw_embeddings(key, part):
    key = jax.random.fold_in(key, 3)
    noise = jnp.clip(jax.random.normal(key, (ROWS, SLOTS, D), jnp.float32), -4.0, 4.0)
    return profile_rows(key, noise).astype(jnp.bfloat16)


def draw_layer_low(key, part):
    key = jax.random.fold_in(key, 4)
    noise = jnp.clip(jax.random.normal(key, (ROWS, SLOTS, D), jnp.float32), -4.0, 4.0)
    return profile_rows(key, noise).astype(jnp.bfloat16)


def draw_layer_mid(key, part):
    key = jax.random.fold_in(key, 5)
    noise = jnp.clip(jax.random.normal(key, (ROWS, SLOTS, D), jnp.float32), -4.0, 4.0)
    return profile_rows(key, noise).astype(jnp.bfloat16)


def draw_cache_lengths(key, part):
    key = jax.random.fold_in(key, 7)
    lengths = jax.random.randint(key, (ROWS,), 2, CACHE + 1)
    longest = jax.random.randint(jax.random.fold_in(key, 8), (), 0, ROWS)
    return jnp.where(jnp.arange(ROWS) == longest, CACHE, lengths).astype(jnp.int32)


def with_ends(values, key, low, largest):
    index_at = [jax.random.randint(jax.random.fold_in(key, axis), (), 0, length) for axis, length in enumerate(values.shape)]
    main_axis = values.shape.index(max(values.shape))
    beside = index_at[:main_axis] + [(index_at[main_axis] + 1) % values.shape[main_axis]] + index_at[main_axis + 1:]
    return values.at[tuple(index_at)].set(low).at[tuple(beside)].set(largest)


def block_levels(key, dims, cuts, least, largest):
    def one(position, parts):
        draws = jax.random.uniform(jax.random.fold_in(jax.random.fold_in(key, 6), position), (parts,), jnp.float32, least / len(cuts), largest / len(cuts))
        return jnp.repeat(jnp.exp(draws), dims[position] // parts).reshape((-1,) + (1,) * (len(dims) - position - 1))

    factor_of = one(*cuts[0])
    for cut in cuts[1:]:
        factor_of = factor_of * one(*cut)
    return factor_of


def gaussian(rng, shape, spread, bound, shards=(), held_as=jnp.bfloat16):
    drawn = jax.random.normal(rng, shape, jnp.float32) * spread
    if len(shards) > 0:
        drawn = block_levels(rng, shape, shards, -0.22, 0.18) * drawn
    return jnp.clip(drawn, min=-bound, max=bound).astype(held_as)


def setup_inputs(seed: int = 0) -> dict:
    keys = jax.random.split(jax.random.key(seed), 17)
    queries = draw_queries(jax.random.fold_in(keys[16], 71), 0)
    cache_keys = draw_cache_keys(jax.random.fold_in(keys[16], 71), 0)
    cache_values = gaussian(keys[2], (ROWS, CACHE, KVD), 1.0, 6.0, ((0, 256),))
    slot_keys = gaussian(keys[3], (ROWS, SLOTS, KVD), 1.0, 6.0, ((0, 256),))
    slot_values = gaussian(keys[4], (ROWS, SLOTS, KVD), 1.0, 6.0, ((0, 256),))
    cache_lengths = draw_cache_lengths(jax.random.fold_in(keys[16], 71), 0)
    embeddings = draw_embeddings(jax.random.fold_in(keys[16], 71), 0)
    layer_low = draw_layer_low(jax.random.fold_in(keys[16], 71), 0)
    layer_mid = draw_layer_mid(jax.random.fold_in(keys[16], 71), 0)
    accepted = with_ends(jax.random.randint(keys[9], (ROWS,), 0, 5), jax.random.fold_in(keys[9], 1), 0, 4).astype(jnp.int32)
    join_gain = jnp.clip(jnp.exp(math.log(2.0) - 1.3862944 * jax.random.uniform(keys[10], (3, D), jnp.float32) ** block_levels(keys[10], (3, D), ((1, 16),), -0.2, 0.2)), 0.5, 2.0)
    norm_gain = jnp.clip(jnp.exp(math.log(2.0) - 1.3862944 * jax.random.uniform(keys[11], (2, D), jnp.float32) ** block_levels(keys[11], (2, D), ((1, 16),), -0.2, 0.2)), 0.5, 2.0)
    key_cotangent = gaussian(keys[12], (ROWS, SLOTS, KVD), (2 * (2 * D) ** 0.5 * ROWS ** -0.5), 64.0, ((0, 16), (2, 16)))
    key_weight = gaussian(keys[13], (KVD, 2, D), 1.0, 5.0, ((0, 32), (2, 16)), jnp.float32)
    moment_first = gaussian(keys[14], (KVD, 2, D), 0.3, 4.0, ((0, 32), (2, 16)), jnp.float32)
    moment_second = jnp.clip(jnp.exp(math.log(5.0) - 2.3025851 * jax.random.uniform(keys[15], (KVD, 2, D), jnp.float32) ** block_levels(keys[15], (KVD, 2, D), ((0, 32), (2, 16)), -0.2, 0.2)), 0.5, 5.0)
    return {"queries": queries, "cache_keys": cache_keys, "cache_values": cache_values, "slot_keys": slot_keys, "slot_values": slot_values, "cache_lengths": cache_lengths, "embeddings": embeddings, "layer_low": layer_low, "layer_mid": layer_mid, "accepted": accepted, "join_gain": join_gain, "norm_gain": norm_gain, "key_cotangent": key_cotangent, "key_weight": key_weight, "moment_first": moment_first, "moment_second": moment_second}


first_beta = 0.9
second_beta = 0.95
learn_rate = 0.05
decay_rate = 0.1
adam_steps = 3
slot_decay = 0.8

def attend_row(operands):
    query_row, keys_row, values_row, new_keys, new_values, length = operands
    group_count = HEADS // KVH
    query_heads = query_row.astype(jnp.float32).reshape(SLOTS, KVH, group_count, HD)
    key_heads = keys_row.astype(jnp.float32).reshape(CACHE, KVH, HD)
    value_heads = values_row.astype(jnp.float32).reshape(CACHE, KVH, HD)
    new_key_heads = new_keys.astype(jnp.float32).reshape(SLOTS, KVH, HD)
    new_value_heads = new_values.astype(jnp.float32).reshape(SLOTS, KVH, HD)
    factor = HD ** (-0.5)
    cache_scores = jnp.einsum('skgd,pkd->skgp', query_heads, key_heads) * factor
    slot_scores = jnp.einsum('skgd,ukd->skgu', query_heads, new_key_heads) * factor
    cache_live = (jnp.arange(CACHE) < length)[None, None, None, :]
    slot_live = (jnp.arange(SLOTS)[None, :] <= jnp.arange(SLOTS)[:, None])[:, None, None, :]
    lowest = jnp.float32(-1e+30)
    highest = jnp.maximum(lax.optimization_barrier(jnp.max(jnp.where(cache_live, cache_scores, lowest), axis=-1)), lax.optimization_barrier(jnp.max(jnp.where(slot_live, slot_scores, lowest), axis=-1)))[..., None]
    cache_exps = jnp.where(cache_live, jnp.exp(cache_scores - highest), jnp.float32(0.0))
    slot_exps = jnp.where(slot_live, jnp.exp(slot_scores - highest), jnp.float32(0.0))
    totals = lax.optimization_barrier(jnp.sum(cache_exps, axis=-1, keepdims=True)) + lax.optimization_barrier(jnp.sum(slot_exps, axis=-1, keepdims=True))
    cache_probs = (cache_exps / totals).astype(jnp.bfloat16).astype(jnp.float32)
    slot_probs = (slot_exps / totals).astype(jnp.bfloat16).astype(jnp.float32)
    mixed = jnp.einsum('skgp,pkd->skgd', cache_probs, value_heads) + jnp.einsum('skgu,ukd->skgd', slot_probs, new_value_heads)
    return mixed.reshape(SLOTS, D).astype(jnp.bfloat16)

def normal_form(values):
    floats = values.astype(jnp.float32)
    return floats * lax.rsqrt(lax.optimization_barrier(jnp.mean(floats * floats, axis=-1, keepdims=True)) + 1e-05)

def reference(queries, cache_keys, cache_values, slot_keys, slot_values, cache_lengths, embeddings, layer_low, layer_mid, accepted, join_gain, norm_gain, key_cotangent, key_weight, moment_first, moment_second):
    top_layer = lax.map(attend_row, (queries, cache_keys, cache_values, slot_keys, slot_values, cache_lengths))
    normal_embed = normal_form(embeddings)
    normal_low = normal_form(layer_low)
    normal_mid = normal_form(layer_mid)
    normal_top = normal_form(top_layer)
    joined = join_gain[0] * normal_low + join_gain[1] * normal_mid + join_gain[2] * normal_top
    normal_joined = normal_form(joined)
    token_total = ROWS * SLOTS
    draft_input = jnp.stack([norm_gain[0] * normal_embed, norm_gain[1] * normal_joined], axis=2).astype(jnp.bfloat16).reshape(token_total, 2 * D)
    normals = jnp.stack([normal_embed, normal_joined], axis=2).reshape(token_total, 2 * D)
    slot_index = jnp.arange(SLOTS, dtype=jnp.int32)
    slot_weight = jnp.where(slot_index[None, :] < accepted[:, None], jnp.float32(slot_decay) ** slot_index.astype(jnp.float32)[None, :], jnp.float32(0.0))
    scaled = (slot_weight[:, :, None] * key_cotangent.astype(jnp.float32)).astype(jnp.bfloat16).reshape(token_total, KVD)
    grad_scale = (2.0 * D) ** (-0.5)
    weight_copy = key_weight.astype(jnp.bfloat16).reshape(KVD, 2 * D)
    block_rows = ROWS_DEV * SLOTS

    def accumulate(running, index):
        grad_sum, gain_sum = running
        first_row = (index * block_rows).astype(jnp.int32)
        input_block = lax.dynamic_slice_in_dim(draft_input, first_row, block_rows, 0)
        scaled_block = lax.dynamic_slice_in_dim(scaled, first_row, block_rows, 0)
        normal_block = lax.dynamic_slice_in_dim(normals, first_row, block_rows, 0)
        partial_grad = lax.dot_general(scaled_block, input_block, (((0,), (0,)), ((), ())), preferred_element_type=jnp.float32) * grad_scale
        rounded = lax.optimization_barrier(partial_grad.astype(jnp.bfloat16))
        grad_sum = grad_sum + rounded.astype(jnp.float32)
        input_grad = jnp.dot(scaled_block, weight_copy, preferred_element_type=jnp.float32) * grad_scale
        gain_sum = gain_sum + lax.optimization_barrier(jnp.sum(input_grad * normal_block, axis=0))
        return ((grad_sum, gain_sum), None)
    start_state = (jnp.zeros((KVD, 2 * D), jnp.float32), jnp.zeros((2 * D,), jnp.float32))
    (grad_flat, gain_flat), _ = lax.scan(accumulate, start_state, jnp.arange(N_DP, dtype=jnp.int32))
    gradient = grad_flat.reshape(KVD, 2, D)
    gain_grad = gain_flat.reshape(2, D)
    moment_first_new = first_beta * moment_first + (1.0 - first_beta) * gradient
    moment_second_new = second_beta * moment_second + (1.0 - second_beta) * gradient * gradient
    corrected_first = moment_first_new / (1.0 - first_beta ** adam_steps)
    corrected_second = moment_second_new / (1.0 - second_beta ** adam_steps)
    direction = corrected_first / (jnp.sqrt(corrected_second) + 1e-08)
    key_weight_new = key_weight - learn_rate * (direction + decay_rate * key_weight)
    return (key_weight_new, moment_first_new, moment_second_new, gain_grad)
```

```python
import functools

import jax
import jax.numpy as jnp
from jax import lax
from jax.experimental import pallas as pl
from jax.experimental.pallas import tpu as pltpu
from jax.sharding import PartitionSpec as P

HD = 128
SUB = 8
EPS = 1e-05
first_beta = 0.9
second_beta = 0.95
learn_rate = 0.05
decay_rate = 0.1
adam_steps = 3
slot_decay = 0.8
MESH = pl.DeviceIdType.MESH
F32 = jnp.float32
BF16 = jnp.bfloat16


def native(x):
    rows, slots, width = x.shape
    x = x.reshape(rows, slots, width // HD, HD).transpose(0, 2, 1, 3)
    return x.reshape(rows * (width // HD) * slots, HD)


def from_native(y, rows, slots, width):
    y = y.reshape(rows, width // HD, slots, HD).transpose(0, 2, 1, 3)
    return y.reshape(rows, slots, width)


def dot_nt(a, b, **kw):
    return lax.dot_general(a, b, (((1,), (1,)), ((), ())), preferred_element_type=F32, **kw)


def swap_halves(x):
    return jnp.concatenate([x[:, 4:], x[:, :4]], axis=1)


def kernel(
    dims,
    q_hbm, ck_hbm, cv_hbm, sk_ref, sv_ref, len_ref, em_hbm, lo_hbm, mi_hbm, cot_hbm,
    jg_ref, ng_ref, ngn_ref, w_hbm, m1_hbm, m2_hbm,
    w_out, m1_out, m2_out, gain_out,
    rxq, kbuf, vbuf, outb, emb, lob, mib, topb, cbuf, wbuf, m1buf, m2buf,
    gpat, zbuf, ssend, srecv, red, vx, ax, tb, sring, rring, sy, ry, gs1, gr1, gs2, gr2,
    lsem, q_s, q_r, c_s, c_r, o_s, o_r, s_s, s_r, red_s, red_r, top_s, top_r,
    ring_s, ring_r, y_s, y_r, g1_s, g1_r, g2_s, g2_r,
):
    NZ, NY, MP, KVH, F, D, HC, SH = dims
    LT = F // HD
    T = MP * 4 * SUB // 2
    TH = T // 2
    H = NZ // 2
    RB = NY * SH
    g = lax.axis_index("group")
    d = lax.axis_index("dp")
    m = lax.axis_index("mp")
    z, y = d // NY, lax.rem(d, NY)

    def at(gg=None, dd=None, mm=None):
        return (g if gg is None else gg, d if dd is None else dd, m if mm is None else mm)

    def zdev(zz):
        return lax.rem(zz + NZ, NZ) * NY + y

    def remote(src, dst, s, r, dev):
        return pltpu.make_async_remote_copy(
            src_ref=src, dst_ref=dst, send_sem=s, recv_sem=r, device_id=dev, device_id_type=MESH
        )

    def rem_mp(j):
        return lax.rem(m + j, MP)

    loads = {
        "k": pltpu.make_async_copy(ck_hbm.at[pl.ds(2 * g, 2)], kbuf, lsem.at[0]),
        "v": pltpu.make_async_copy(cv_hbm.at[pl.ds(2 * g, 2)], vbuf, lsem.at[1]),
        "lo": pltpu.make_async_copy(lo_hbm, lob, lsem.at[2]),
        "mi": pltpu.make_async_copy(mi_hbm, mib, lsem.at[3]),
        "em": pltpu.make_async_copy(em_hbm, emb, lsem.at[4]),
        "w": pltpu.make_async_copy(w_hbm, wbuf, lsem.at[5]),
        "m1": pltpu.make_async_copy(m1_hbm, m1buf, lsem.at[6]),
        "m2": pltpu.make_async_copy(m2_hbm, m2buf, lsem.at[7]),
        "q": pltpu.make_async_copy(q_hbm.at[m, g], rxq.at[m], lsem.at[8]),
    }
    for key in ("lo", "mi", "em", "q", "k", "v", "w", "m1", "m2"):
        loads[key].start()

    bar = pltpu.get_barrier_semaphore()

    def greet(j, c):
        pl.semaphore_signal(bar, inc=1, device_id=at(mm=rem_mp(j)), device_id_type=MESH)
        return c

    lax.fori_loop(1, MP, greet, 0)

    def greet_z(j, c):
        pl.semaphore_signal(bar, inc=1, device_id=at(dd=zdev(z + j)), device_id_type=MESH)
        return c

    lax.fori_loop(1, NZ, greet_z, 0)
    pl.semaphore_signal(bar, inc=1, device_id=at(gg=1 - g), device_id_type=MESH)
    greeted = MP - 1 + NZ - 1 + 1
    if NY == 2:
        pl.semaphore_signal(bar, inc=1, device_id=at(dd=z * NY + 1 - y), device_id_type=MESH)
        pl.semaphore_signal(bar, inc=1, device_id=at(gg=1 - g, dd=z * NY + 1 - y), device_id_type=MESH)
        greeted += 2
    pl.semaphore_wait(bar, greeted)

    def q_copy(j):
        dst = rem_mp(j)
        return remote(q_hbm.at[dst, g], rxq.at[m], q_s.at[j], q_r.at[m], at(mm=dst))

    def q_start(j, c):
        q_copy(j).start()
        return c

    lax.fori_loop(1, MP, q_start, 0)

    half = MP // 2
    mine = lax.rem(m, half)
    sends_cot = (m // half) == g

    def c_copy(j):
        return remote(cot_hbm, cbuf.at[mine], c_s.at[j], c_r.at[mine], at(mm=rem_mp(j)))

    own_cot = pltpu.make_async_copy(cot_hbm, cbuf.at[mine], c_s.at[0])

    @pl.when(sends_cot)
    def _():
        own_cot.start()

        def c_start(j, c):
            c_copy(j).start()
            return c

        lax.fori_loop(1, MP, c_start, 0)

    sub8 = lax.broadcasted_iota(jnp.int32, (1, SUB, HD), 1) < 4
    for a in range(3):
        for lp in range(LT // 2):
            lower = jg_ref[a : a + 1, 2 * lp * HD : (2 * lp + 1) * HD]
            upper = jg_ref[a : a + 1, (2 * lp + 1) * HD : (2 * lp + 2) * HD]
            gpat[a, lp] = jnp.where(sub8[0], lower, upper)

    def native_block(ref, i):
        return ref.astype(F32).reshape(2, LT // 2, SUB, HD)

    def fold(p):
        t = jnp.sum(p, axis=1)
        t = t + swap_halves(t)
        return jnp.where(sub8[0], t[0], t[1])

    zbuf[...] = jnp.zeros_like(zbuf)
    loads["lo"].wait()
    loads["mi"].wait()
    loads["em"].wait()
    g0, g1, g2 = gpat[0], gpat[1], gpat[2]

    def stats0(i, c):
        e = native_block(emb[i, g], i)
        l = native_block(lob[i, g], i)
        v = native_block(mib[i, g], i)
        gl, gv = l * g0, v * g1
        rows = pl.ds(pl.multiple_of(i * SUB, SUB), SUB)
        for n, p in enumerate((e * e, l * l, v * v, gl * gl, gv * gv, gl * gv)):
            zbuf[n, rows, :] = fold(p)
        return c

    lax.fori_loop(0, MP, stats0, 0)

    def row_sums(count):
        total = jnp.zeros((SUB, TH), F32)
        for n in range(count):
            pick = (lax.broadcasted_iota(jnp.int32, (SUB, HD), 0) == n).astype(F32)
            total = total + dot_nt(pick, zbuf[n], precision=lax.Precision.HIGHEST)
        return total

    def s_copy(ph, j):
        return remote(ssend.at[ph], srecv.at[ph, m], s_s.at[ph, j], s_r.at[ph, m], at(mm=rem_mp(j)))

    def s_begin(ph, count):
        ssend[ph] = row_sums(count)

        def go(j, c):
            s_copy(ph, j).start()
            return c

        lax.fori_loop(1, MP, go, 0)

    def red_copy(ph):
        return remote(red.at[ph, g], red.at[ph, g], red_s.at[ph], red_r.at[ph], at(gg=1 - g))

    def s_reduce(ph):
        def add(j, total):
            src = rem_mp(j)
            remote(
                ssend.at[ph], srecv.at[ph, src], s_s.at[ph, j], s_r.at[ph, src], at(mm=src)
            ).wait_recv()
            return total + srecv[ph, src]

        red[ph, g] = lax.fori_loop(1, MP, add, ssend[ph])
        red_copy(ph).start()

    s_begin(0, 6)

    def relayout(x, col, gg, n):
        x = x.astype(F32).reshape(2, LT // 2, SUB, HD)
        a, b = x[0], x[1]
        even = jnp.where(sub8, a, swap_halves(b))
        odd = jnp.where(sub8, swap_halves(a), b)
        return even, odd

    def relayout_all(n, load, gg):
        def two(i, c):
            parts = [relayout(load(2 * i + h, gg), 0, gg, n) for h in range(2)]
            rows = pl.ds(pl.multiple_of(gg * TH + i * 2 * SUB, 2 * SUB), 2 * SUB)
            for lp in range(LT // 2):
                for k in range(2):
                    tile = jnp.concatenate([parts[0][k][lp], parts[1][k][lp]], axis=0)
                    lt = 2 * lp + k
                    vx[n, rows, lt * HD : (lt + 1) * HD] = tile.astype(BF16)
            return c

        lax.fori_loop(0, MP // 2, two, 0)

    for gg in range(2):
        relayout_all(0, lambda i, gg: emb[i, gg], gg)

    loads["k"].wait()
    loads["v"].wait()
    loads["q"].wait()

    def q_wait(j, c):
        src = rem_mp(j)
        remote(q_hbm.at[src, g], rxq.at[src], q_s.at[j], q_r.at[src], at(mm=src)).wait_recv()
        return c

    lax.fori_loop(1, MP, q_wait, 0)

    CP = 64
    SR = KVH * 4
    QR = 32
    rowi = lax.broadcasted_iota(jnp.int32, (2 * QR, HD), 0)
    coli = lax.broadcasted_iota(jnp.int32, (2 * QR, HD), 1)
    slot_of = lax.rem(rowi, 4)
    scol = coli - CP
    in_slots = (scol >= 0) & (scol < SR) & (lax.rem(scol, 4) <= slot_of)
    pad = jnp.zeros((HD - CP - SR, HD), BF16)

    def attend(r, c):
        length = len_ref[2 * g + r]
        srows = pl.ds(pl.multiple_of((2 * g + r) * SR, SR), SR)
        sk_r, sv_r = sk_ref[srows, :], sv_ref[srows, :]
        qrows = pl.ds(pl.multiple_of(r * QR, QR), QR)
        cached = coli < jnp.minimum(length, CP)
        for k in range(KVH):
            qk = jnp.concatenate([rxq[2 * k, qrows, :], rxq[2 * k + 1, qrows, :]], axis=0)
            cols = slice(k * HD, (k + 1) * HD)
            keys = jnp.concatenate([kbuf[r, :, cols], sk_r, pad], axis=0)
            vals = jnp.concatenate([vbuf[r, :, cols], sv_r, pad], axis=0)
            live = cached | (in_slots & (scol // 4 == k))
            s = dot_nt(qk, keys) * (HD**-0.5)
            s = jnp.where(live, s, -1e30)
            top = jnp.max(s, axis=-1, keepdims=True)
            e = jnp.where(live, jnp.exp(s - top), 0.0)
            p = (e / jnp.sum(e, axis=-1, keepdims=True)).astype(BF16)
            o = jnp.dot(p, vals, preferred_element_type=F32).astype(BF16)
            outb[2 * k, qrows, :] = o[:QR]
            outb[2 * k + 1, qrows, :] = o[QR:]
        return c

    lax.fori_loop(0, 2, attend, 0)

    def o_copy(j):
        dst = rem_mp(j)
        return remote(outb.at[dst], topb.at[g, m], o_s.at[j], o_r.at[m], at(mm=dst))

    def o_start(j, c):
        o_copy(j).start()
        return c

    lax.fori_loop(1, MP, o_start, 0)
    topb[g, m] = outb[m]

    s_reduce(0)

    def c_wait(b, c):
        src = half * g + b
        there = remote(cot_hbm, cbuf.at[b], c_s.at[b], c_r.at[b], at(mm=src))

        @pl.when(src != m)
        def _():
            there.wait_recv()

        return c

    lax.fori_loop(0, half, c_wait, 0)

    @pl.when(sends_cot)
    def _():
        own_cot.wait()

    remote(red.at[0, g], red.at[0, 1 - g], red_s.at[0], red_r.at[0], at(gg=1 - g)).wait_recv()

    def sums(ph, n):
        return jnp.concatenate([red[ph, 0, n : n + 1, :], red[ph, 1, n : n + 1, :]], axis=1)

    def inv(total):
        return lax.rsqrt(total * (1.0 / D) + EPS)

    def scale_cot(n, row):
        ax[n] = (cbuf[...].reshape(HC, T).astype(F32) * row).astype(BF16)

    scale = (2.0 * D) ** -0.5
    FB = min(F, 256)
    CB = min(HC, 256)

    scale_cot(0, inv(sums(0, 0)))

    def tiles(i, terms):
        def one(n, c):
            rows = pl.ds(pl.multiple_of((n % (HC // CB)) * CB, CB), CB)
            fb = n // (HC // CB)
            cols = pl.ds(pl.multiple_of(fb * FB, FB), FB)
            total = None
            for n_x, gain in terms:
                part = jnp.dot(ax[n_x, rows, :], vx[n_x, :, cols], preferred_element_type=F32)
                if gain is not None:
                    part = part * jg_ref[gain : gain + 1, cols]
                total = part if total is None else total + part
            tb[i, rows, cols] = (total * (ng_ref[i : i + 1, cols] * scale)).astype(BF16)
            return c

        lax.fori_loop(0, (HC // CB) * (F // FB), one, 0)

    FH = F // 2

    def zrows(zz):
        return pl.ds(pl.multiple_of(lax.rem(zz + NZ, NZ) * RB, RB), RB)

    def ring_cols(k, way):
        return slice(way * FH, (way + 1) * FH) if k == 1 else slice(0, F)

    def ring_copy(i, way, k):
        cols = ring_cols(k, way)
        step = 1 if way == 0 else -1
        if k == 1:
            src = tb.at[i, zrows(z + step * H), cols]
        else:
            src = sring.at[i, way, k - 2]
        dst = rring.at[i, way, k - 1, :, cols]
        return remote(src, dst, ring_s.at[i, way, k - 1], ring_r.at[i, way, k - 1], at(dd=zdev(z + step)))

    def ring_step(i, k):
        for way in range(2):
            if k > 1:
                step = 1 if way == 0 else -1
                ring_copy(i, way, k - 1).wait_recv()
                rows = zrows(z + step * (H + 1 - k))
                cols = ring_cols(k - 1, way)
                if k == 2:
                    sring[i, way, 0] = tb[i, rows, :]
                own = tb[i, rows, cols].astype(F32)
                sring[i, way, k - 2, :, cols] = (own + rring[i, way, k - 2, :, cols].astype(F32)).astype(BF16)
            ring_copy(i, way, k).start()

    def y_copy(i):
        return remote(sy.at[i], ry.at[i], y_s.at[i], y_r.at[i], at(dd=z * NY + 1 - y))

    def ring_end(i):
        for way in range(2):
            ring_copy(i, way, H).wait_recv()

        def total(yy):
            rows = pl.ds(pl.multiple_of(z * RB + yy * SH, SH), SH)
            here = pl.ds(pl.multiple_of(yy * SH, SH), SH)
            t = tb[i, rows, :].astype(F32)
            if H > 1:
                for way in range(2):
                    t = t + rring[i, way, H - 1, here, :].astype(F32)
            else:
                t = t + jnp.concatenate(
                    [rring[i, way, 0, here, ring_cols(1, way)].astype(F32) for way in range(2)], axis=1
                )
            return t

        if NY == 2:
            sy[i] = total(1 - y).astype(BF16)
            y_copy(i).start()
        return total(y)

    def grad_end(i, t):
        if NY == 2:
            y_copy(i).wait_recv()
            t = t + ry[i].astype(F32)
        return t.reshape(SH, LT, HD).reshape(SH * LT, HD)

    def gain_part(i, grad):
        w = wbuf[pl.ds(i, SH * LT, stride=2), :].astype(BF16).astype(F32)
        part = jnp.sum((w * grad).reshape(SH, LT, HD), axis=0)
        gs1[pl.ds(i * LT, LT), :] = part / ngn_ref[pl.ds(i, LT, stride=2), :]

    def adam(i, grad):
        rows = pl.ds(i, SH * LT, stride=2)
        w = wbuf[rows, :]
        a = first_beta * m1buf[rows, :] + (1.0 - first_beta) * grad
        b = second_beta * m2buf[rows, :] + (1.0 - second_beta) * grad * grad
        m1_out[rows, :] = a
        m2_out[rows, :] = b
        ca = a * (1.0 / (1.0 - first_beta**adam_steps))
        cb = b * (1.0 / (1.0 - second_beta**adam_steps))
        w_out[rows, :] = w - learn_rate * (ca / (jnp.sqrt(cb) + 1e-08) + decay_rate * w)

    tiles(0, ((0, None),))
    ring_step(0, 1)

    for gg in range(2):
        relayout_all(1, lambda i, gg: lob[i, gg], gg)
        relayout_all(2, lambda i, gg: mib[i, gg], gg)

    def o_wait(j, c):
        src = rem_mp(j)
        remote(outb.at[src], topb.at[g, src], o_s.at[j], o_r.at[src], at(mm=src)).wait_recv()
        return c

    lax.fori_loop(1, MP, o_wait, 0)
    top_copy = remote(topb.at[g], topb.at[g], top_s, top_r, at(gg=1 - g))
    top_copy.start()

    def stats1(i, c):
        l = native_block(lob[i, g], i)
        v = native_block(mib[i, g], i)
        t = native_block(topb[g, i], i)
        gl, gv, gt = l * g0, v * g1, t * g2
        rows = pl.ds(pl.multiple_of(i * SUB, SUB), SUB)
        for n, p in enumerate((t * t, gt * gt, gl * gt, gv * gt)):
            zbuf[n, rows, :] = fold(p)
        return c

    lax.fori_loop(0, MP, stats1, 0)
    s_begin(1, 4)
    if H >= 2:
        ring_step(0, 2)
    relayout_all(3, lambda i, gg: topb[gg, i], g)
    s_reduce(1)
    if H >= 3:
        ring_step(0, 3)
    remote(topb.at[g], topb.at[1 - g], top_s, top_r, at(gg=1 - g)).wait_recv()
    relayout_all(3, lambda i, gg: topb[gg, i], 1 - g)
    remote(red.at[1, g], red.at[1, 1 - g], red_s.at[1], red_r.at[1], at(gg=1 - g)).wait_recv()
    rl, rv, rt = inv(sums(0, 1)), inv(sums(0, 2)), inv(sums(1, 0))
    joined = (
        rl * rl * sums(0, 3)
        + rv * rv * sums(0, 4)
        + rt * rt * sums(1, 1)
        + 2.0 * (rl * rv * sums(0, 5) + rl * rt * sums(1, 2) + rv * rt * sums(1, 3))
    )
    rj = inv(jnp.maximum(joined, 0.0))
    scale_cot(1, rl * rj)
    scale_cot(2, rv * rj)
    scale_cot(3, rt * rj)
    tiles(1, ((1, 0), (2, 1), (3, 2)))
    ring_step(1, 1)
    if H >= 4:
        ring_step(0, 4)
    if H >= 2:
        ring_step(1, 2)
    part0 = ring_end(0)
    if H >= 3:
        ring_step(1, 3)
    loads["w"].wait()
    loads["m1"].wait()
    loads["m2"].wait()
    grad0 = grad_end(0, part0)
    gain_part(0, grad0)
    adam(0, grad0)
    if H >= 4:
        ring_step(1, 4)
    grad1 = grad_end(1, ring_end(1))
    gain_part(1, grad1)

    pairs = [(1 - g, z * NY + y)]
    if NY == 2:
        pairs += [(g, z * NY + 1 - y), (1 - g, z * NY + 1 - y)]
    g1_copies = [
        remote(gs1, gr1.at[n], g1_s.at[n], g1_r.at[n], at(gg=gg, dd=dd)) for n, (gg, dd) in enumerate(pairs)
    ]
    for copy in g1_copies:
        copy.start()
    adam(1, grad1)
    total = gs1[...]
    for n, copy in enumerate(g1_copies):
        copy.wait_recv()
        total = total + gr1[n]
    gs2[...] = total

    def g2_copy(j):
        return remote(gs2, gr2.at[z], g2_s.at[j], g2_r.at[z], at(dd=zdev(z + j)))

    for j in range(1, NZ):
        g2_copy(j).start()
    for j in range(1, NZ):
        src = lax.rem(z + j, NZ)
        remote(gs2, gr2.at[src], g2_s.at[j], g2_r.at[src], at(dd=zdev(z + j))).wait_recv()
        total = total + gr2[src]
    gain_out[pl.ds(0, LT, stride=2), :] = total[:LT]
    gain_out[pl.ds(1, LT, stride=2), :] = total[LT:]

    def drain(j, c):
        q_copy(j).wait_send()
        o_copy(j).wait_send()
        s_copy(0, j).wait_send()
        s_copy(1, j).wait_send()
        return c

    lax.fori_loop(1, MP, drain, 0)

    @pl.when(sends_cot)
    def _():
        def c_drain(j, c):
            c_copy(j).wait_send()
            return c

        lax.fori_loop(1, MP, c_drain, 0)

    for ph in range(2):
        red_copy(ph).wait_send()
    top_copy.wait_send()
    for i in range(2):
        for way in range(2):
            for k in range(1, H + 1):
                ring_copy(i, way, k).wait_send()
        if NY == 2:
            y_copy(i).wait_send()
    for copy in g1_copies:
        copy.wait_send()
    for j in range(1, NZ):
        g2_copy(j).wait_send()


def shards(
    NZ, NY, MP,
    queries, cache_keys, cache_values, slot_keys, slot_values, cache_lengths,
    embeddings, layer_low, layer_mid, accepted, join_gain, norm_gain,
    key_cotangent, key_weight, moment_first, moment_second,
):
    rows, slots, F = embeddings.shape
    D = F * MP
    KW = cache_keys.shape[2]
    KVH = KW // HD
    SH = key_weight.shape[0]
    HC = SH * NZ * NY
    T = rows * slots
    TH = T // 2
    LT = F // HD
    RB = NY * SH
    H = NZ // 2
    slot_index = jnp.arange(slots, dtype=jnp.int32)
    weight = jnp.where(
        slot_index[None, :] < accepted[:, None],
        jnp.float32(slot_decay) ** slot_index.astype(F32)[None, :],
        0.0,
    )
    scaled = (weight[:, :, None] * key_cotangent.astype(F32)).astype(BF16)
    cols = scaled.shape[2]
    scaled = scaled.reshape(MP, 2, 2, slots, cols).transpose(4, 1, 0, 2, 3).reshape(cols, T)

    def tokens(x):
        return native(x).reshape(MP, 2, 2 * LT * slots, HD)

    hbm = pl.BlockSpec(memory_space=pl.ANY)
    vmem = pl.BlockSpec(memory_space=pltpu.VMEM)
    smem = pl.BlockSpec(memory_space=pltpu.SMEM)
    dma = pltpu.SemaphoreType.DMA
    B = 2 * LT * slots
    shape = jax.ShapeDtypeStruct
    outs = pl.pallas_call(
        functools.partial(kernel, (NZ, NY, MP, KVH, F, D, HC, SH)),
        out_shape=(
            shape((SH * 2 * LT, HD), F32),
            shape((SH * 2 * LT, HD), F32),
            shape((SH * 2 * LT, HD), F32),
            shape((2 * LT, HD), F32),
        ),
        in_specs=[hbm, hbm, hbm, vmem, vmem, smem, hbm, hbm, hbm, hbm, vmem, vmem, vmem, hbm, hbm, hbm],
        out_specs=(vmem, vmem, vmem, vmem),
        scratch_shapes=[
            pltpu.VMEM((MP, B, HD), BF16),
            pltpu.VMEM((2, 64, KW), BF16),
            pltpu.VMEM((2, 64, KW), BF16),
            pltpu.VMEM((MP, B, HD), BF16),
            pltpu.VMEM((MP, 2, B, HD), BF16),
            pltpu.VMEM((MP, 2, B, HD), BF16),
            pltpu.VMEM((MP, 2, B, HD), BF16),
            pltpu.VMEM((2, MP, B, HD), BF16),
            pltpu.VMEM((MP // 2, cols, T), BF16),
            pltpu.VMEM((SH * 2 * LT, HD), F32),
            pltpu.VMEM((SH * 2 * LT, HD), F32),
            pltpu.VMEM((SH * 2 * LT, HD), F32),
            pltpu.VMEM((3, LT // 2, SUB, HD), F32),
            pltpu.VMEM((SUB, TH, HD), F32),
            pltpu.VMEM((2, SUB, TH), F32),
            pltpu.VMEM((2, MP, SUB, TH), F32),
            pltpu.VMEM((2, 2, SUB, TH), F32),
            pltpu.VMEM((4, T, F), BF16),
            pltpu.VMEM((4, HC, T), BF16),
            pltpu.VMEM((2, HC, F), BF16),
            pltpu.VMEM((2, 2, max(H - 1, 1), RB, F), BF16),
            pltpu.VMEM((2, 2, H, RB, F), BF16),
            pltpu.VMEM((2, SH, F), BF16),
            pltpu.VMEM((2, SH, F), BF16),
            pltpu.VMEM((2 * LT, HD), F32),
            pltpu.VMEM((3, 2 * LT, HD), F32),
            pltpu.VMEM((2 * LT, HD), F32),
            pltpu.VMEM((NZ, 2 * LT, HD), F32),
            dma((9,)),
            dma((MP,)), dma((MP,)),
            dma((MP,)), dma((MP // 2,)),
            dma((MP,)), dma((MP,)),
            dma((2, MP)), dma((2, MP)),
            dma((2,)), dma((2,)),
            dma, dma,
            dma((2, 2, H)), dma((2, 2, H)),
            dma((2,)), dma((2,)),
            dma((3,)), dma((3,)),
            dma((NZ,)), dma((NZ,)),
        ],
        compiler_params=pltpu.CompilerParams(
            collective_id=0, has_side_effects=True, vmem_limit_bytes=48 * 1024 * 1024
        ),
        cost_estimate=pl.CostEstimate(
            flops=2 * 4 * HC * T * F, bytes_accessed=6 * 1024 * 1024, transcendentals=0
        ),
        name="draft_step",
    )(
        tokens(queries), cache_keys, cache_values, native(slot_keys), native(slot_values), cache_lengths,
        tokens(embeddings), tokens(layer_low), tokens(layer_mid), scaled,
        join_gain, norm_gain, native(norm_gain[None]),
        native(key_weight), native(moment_first), native(moment_second),
    )
    new = [from_native(x, SH, 2, F) for x in outs[:3]]
    return (*new, from_native(outs[3], 1, 2, F)[0])


def solution(mesh, NY=2):
    NZ, MP = mesh.shape["dp"] // NY, mesh.shape["mp"]
    tokens, owners, moments = P("dp", None, "mp"), P(("dp", "mp"), None, None), P(("group", "dp"), None, "mp")
    return jax.shard_map(
        functools.partial(shards, NZ, NY, MP),
        mesh=mesh,
        in_specs=(
            tokens, owners, owners, owners, owners, P(("dp", "mp")), tokens, tokens, tokens, P("dp"),
            P(None, "mp"), P(None, "mp"), tokens, moments, moments, moments,
        ),
        out_specs=(moments, moments, moments, P(None, "mp")),
        check_vma=False,
    )
```

```python
import functools

import jax
import jax.numpy as jnp
from jax import lax
from jax.experimental import pallas as pl
from jax.experimental.pallas import tpu as pltpu
from jax.sharding import PartitionSpec as P

HD = 128
SUB = 8
VMEM_BYTES = 62 * 1024 * 1024
NQ = 4
EPS = 1e-05
first_beta = 0.9
second_beta = 0.95
learn_rate = 0.05
decay_rate = 0.1
adam_steps = 3
slot_decay = 0.8
MESH = pl.DeviceIdType.MESH
F32 = jnp.float32
BF16 = jnp.bfloat16


def native(x):
    rows, slots, width = x.shape
    x = x.reshape(rows, slots, width // HD, HD).transpose(0, 2, 1, 3)
    return x.reshape(rows * (width // HD) * slots, HD)


def from_native(y, rows, slots, width):
    y = y.reshape(rows, width // HD, slots, HD).transpose(0, 2, 1, 3)
    return y.reshape(rows, slots, width)


def dot_nt(a, b, **kw):
    return lax.dot_general(a, b, (((1,), (1,)), ((), ())), preferred_element_type=F32, **kw)


def swap_halves(x):
    return jnp.concatenate([x[:, 4:], x[:, :4]], axis=1)


def kernel(
    dims,
    q_hbm, ck_hbm, cv_hbm, sk_ref, sv_ref, len_ref, em_hbm, lo_hbm, mi_hbm, cot_ref, acc_ref,
    jg_ref, ng_ref, ngn_ref, w_hbm, m1_hbm, m2_hbm,
    w_out, m1_out, m2_out, gain_out,
    rxq, kbuf, vbuf, outb, emb, lob, mib, topb, csend, cbuf, wbuf, m1buf, m2buf,
    gpat, zbuf, ssend, srecv, red, vx, ax, tb, sring, rring, sy, ry, own_t,
    w_two, wsend, wpart, gsend, grecv, gsib_s, gsib_r,
    lsem, q_s, q_r, c_s, c_r, o_s, o_r, s_s, s_r, red_s, red_r, top_s, top_r,
    ring_s, ring_r, y_s, y_r, wx_s, wx_r, g_s, g_r, gx_s, gx_r,
):
    NZ, NY, MP, KVH, F, D, HC, SH = dims
    LT = F // HD
    T = MP * 4 * SUB // 2
    TH = T // 2
    H = NZ // 2
    DP = NZ * NY
    RB = NY * SH
    FQ = F // NQ
    g = lax.axis_index("group")
    d = lax.axis_index("dp")
    m = lax.axis_index("mp")
    z, y = d // NY, lax.rem(d, NY)

    def at(gg=None, dd=None, mm=None):
        return (g if gg is None else gg, d if dd is None else dd, m if mm is None else mm)

    def zdev(zz):
        return lax.rem(zz + NZ, NZ) * NY + y

    def remote(src, dst, s, r, dev):
        return pltpu.make_async_remote_copy(
            src_ref=src, dst_ref=dst, send_sem=s, recv_sem=r, device_id=dev, device_id_type=MESH
        )

    def flip(a, j, n):
        out, bit = 0, 1
        while bit < n:
            p, q = lax.rem(a // bit, 2), lax.rem(j // bit, 2)
            out = out + bit * (p + q - 2 * p * q)
            bit *= 2
        return out

    def peer(j):
        return flip(m, jnp.int32(j), MP)

    loads = {
        "lo": pltpu.make_async_copy(lo_hbm, lob, lsem.at[0]),
        "mi": pltpu.make_async_copy(mi_hbm, mib, lsem.at[1]),
        "em": pltpu.make_async_copy(em_hbm, emb, lsem.at[2]),
        "q": pltpu.make_async_copy(q_hbm.at[m, g], rxq.at[m], lsem.at[3]),
        "k": pltpu.make_async_copy(ck_hbm.at[pl.ds(2 * g, 2)], kbuf, lsem.at[4]),
        "v": pltpu.make_async_copy(cv_hbm.at[pl.ds(2 * g, 2)], vbuf, lsem.at[5]),
        "w": pltpu.make_async_copy(w_hbm, wbuf, lsem.at[6]),
        "m1": pltpu.make_async_copy(m1_hbm, m1buf, lsem.at[7]),
        "m2": pltpu.make_async_copy(m2_hbm, m2buf, lsem.at[8]),
    }
    for load in loads.values():
        load.start()

    bar = pltpu.get_barrier_semaphore()

    def greet_dp(j, c):
        pl.semaphore_signal(bar, inc=1, device_id=at(dd=lax.rem(d + j, DP)), device_id_type=MESH)
        return c

    lax.fori_loop(1, DP, greet_dp, 0)

    def greet_mp(j, c):
        pl.semaphore_signal(bar, inc=1, device_id=at(mm=peer(MP - j)), device_id_type=MESH)
        return c

    lax.fori_loop(1, MP, greet_mp, 0)
    pl.semaphore_signal(bar, inc=1, device_id=at(gg=1 - g), device_id_type=MESH)

    RD = 4 * MP
    ct = cot_ref[...].astype(F32).reshape(RD // 2, 2, 4, cot_ref.shape[2])
    ct = jnp.concatenate([ct[:, 0], ct[:, 1]], axis=1).reshape(MP, 2, SUB, cot_ref.shape[2])
    ct = jnp.concatenate([ct[:, 0], ct[:, 1]], axis=0).reshape(T, cot_ref.shape[2])
    token = lax.broadcasted_iota(jnp.int32, (RD, T), 1)
    quad = token // 4
    part = lax.rem(quad, RD // 2)
    row = (part // 2) * 4 + (quad // (RD // 2)) * 2 + lax.rem(part, 2)
    pick = (lax.broadcasted_iota(jnp.int32, (RD, T), 0) == row).astype(BF16)
    lengths = jnp.broadcast_to(acc_ref[...].astype(F32), (SUB, RD)).astype(BF16)
    taken = jnp.dot(lengths, pick, preferred_element_type=F32)[:1]
    slot = lax.rem(lax.broadcasted_iota(jnp.int32, (1, T), 1), 4)
    weight = jnp.zeros((1, T), F32)
    for s in range(4):
        weight = jnp.where((slot == s) & (taken > s + 0.5), jnp.float32(slot_decay**s), weight)
    csend[...] = (ct.T * weight).astype(BF16)

    sub8 = lax.broadcasted_iota(jnp.int32, (1, SUB, HD), 1) < 4
    for a in range(3):
        for lp in range(LT // 2):
            lower = jg_ref[a : a + 1, 2 * lp * HD : (2 * lp + 1) * HD]
            upper = jg_ref[a : a + 1, (2 * lp + 1) * HD : (2 * lp + 2) * HD]
            gpat[a, lp] = jnp.where(sub8[0], lower, upper)

    def native_block(x):
        return x.astype(F32).reshape(2, LT // 2, SUB, HD)

    def fold(p):
        t = jnp.sum(p, axis=1)
        t = t + swap_halves(t)
        return jnp.where(sub8[0], t[0], t[1])

    loads["lo"].wait()
    loads["mi"].wait()
    loads["em"].wait()
    g0, g1, g2 = gpat[0], gpat[1], gpat[2]

    def stats0(i, c):
        e, l, v = native_block(emb[i, g]), native_block(lob[i, g]), native_block(mib[i, g])
        gl, gv = l * g0, v * g1
        rows = pl.ds(pl.multiple_of(i * SUB, SUB), SUB)
        for n, p in enumerate((e * e, l * l, v * v, gl * gl, gv * gv, gl * gv)):
            zbuf[n, rows, :] = fold(p)
        return c

    lax.fori_loop(0, MP, stats0, 0)

    def row_sums(count):
        total = jnp.zeros((SUB, TH), F32)
        for n in range(count):
            pick = (lax.broadcasted_iota(jnp.int32, (SUB, HD), 0) == n).astype(F32)
            total = total + dot_nt(pick, zbuf[n], precision=lax.Precision.HIGHEST)
        return total

    ssend[0] = row_sums(6)

    def relayout(x):
        x = native_block(x)
        a, b = x[0], x[1]
        return jnp.where(sub8, a, swap_halves(b)), jnp.where(sub8, swap_halves(a), b)

    def relayout_all(n, load, gg):
        def two(i, c):
            parts = [relayout(load(2 * i + h, gg)) for h in range(2)]
            rows = pl.ds(pl.multiple_of(gg * TH + i * 2 * SUB, 2 * SUB), 2 * SUB)
            for lp in range(LT // 2):
                for k in range(2):
                    tile = jnp.concatenate([parts[0][k][lp], parts[1][k][lp]], axis=0)
                    lt = 2 * lp + k
                    vx[n, rows, lt * HD : (lt + 1) * HD] = tile.astype(BF16)
            return c

        lax.fori_loop(0, MP // 2, two, 0)

    for gg in range(2):
        relayout_all(0, lambda i, gg: emb[i, gg], gg)
    loads["w"].wait()
    for i in range(2):
        w = wbuf[pl.ds(i, SH * LT, stride=2), :].astype(BF16).astype(F32)
        w_two[i] = w.reshape(SH, LT, HD).reshape(SH, F)
    wsend[...] = w_two[1].astype(BF16)

    pl.semaphore_wait(bar, DP - 1 + MP - 1 + 1)

    def q_copy(j):
        dst = peer(j)
        return remote(q_hbm.at[dst, g], rxq.at[m], q_s.at[j], q_r.at[m], at(mm=dst))

    def q_start(j, c):
        q_copy(MP - j).start()
        return c

    lax.fori_loop(1, MP, q_start, 0)

    half = MP // 2
    mine = lax.rem(m, half)
    sends_cot = (m // half) == g

    def c_copy(j):
        return remote(csend, cbuf.at[mine], c_s.at[j], c_r.at[mine], at(mm=peer(j)))

    @pl.when(sends_cot)
    def _():
        cbuf[mine] = csend[...]

        def c_start(j, c):
            c_copy(MP - j).start()
            return c

        lax.fori_loop(1, MP, c_start, 0)

    def s_copy(ph, j):
        return remote(ssend.at[ph], srecv.at[ph, m], s_s.at[ph, j], s_r.at[ph, m], at(mm=peer(j)))

    def s_begin(ph):
        def go(j, c):
            s_copy(ph, MP - j).start()
            return c

        lax.fori_loop(1, MP, go, 0)

    s_begin(0)

    def red_copy(ph):
        return remote(red.at[ph, g], red.at[ph, g], red_s.at[ph], red_r.at[ph], at(gg=1 - g))

    def s_reduce(ph):
        def add(j, total):
            src = peer(j)
            remote(
                ssend.at[ph], srecv.at[ph, src], s_s.at[ph, j], s_r.at[ph, src], at(mm=src)
            ).wait_recv()
            return total + srecv[ph, src]

        red[ph, g] = lax.fori_loop(1, MP, add, ssend[ph])
        red_copy(ph).start()

    def w_copy():
        return remote(wsend, wpart, wx_s, wx_r, at(dd=z * NY + 1 - y))

    for gg in range(2):
        relayout_all(1, lambda i, gg: lob[i, gg], gg)
        relayout_all(2, lambda i, gg: mib[i, gg], gg)

    loads["k"].wait()
    loads["v"].wait()
    loads["q"].wait()
    CP = 64
    SR = KVH * 4
    QR = 32
    rowi = lax.broadcasted_iota(jnp.int32, (2 * QR, HD), 0)
    coli = lax.broadcasted_iota(jnp.int32, (2 * QR, HD), 1)
    scol = coli - CP
    in_slots = (scol >= 0) & (scol < SR) & (lax.rem(scol, 4) <= lax.rem(rowi, 4))
    slot_head = scol // 4
    pad = jnp.zeros((HD - CP - SR, HD), BF16)
    slot_rows = [pl.ds(pl.multiple_of((2 * g + r) * SR, SR), SR) for r in range(2)]
    cached = [coli < jnp.minimum(len_ref[2 * g + r], CP) for r in range(2)]

    def o_copy(dst):
        return remote(outb.at[dst], topb.at[g, m], o_s.at[dst], o_r.at[m], at(mm=dst))

    def attend(j, c):
        k = flip(m // 2, j, KVH)
        for h in range(2):
            src = 2 * k + h

            @pl.when(src != m)
            def _():
                remote(q_hbm.at[src, g], rxq.at[src], q_s.at[src], q_r.at[src], at(mm=src)).wait_recv()

        cols = pl.ds(pl.multiple_of(k * HD, HD), HD)
        for r in range(2):
            qrows = slice(r * QR, (r + 1) * QR)
            qk = jnp.concatenate([rxq[2 * k, qrows, :], rxq[2 * k + 1, qrows, :]], axis=0)
            keys = jnp.concatenate([kbuf[r, :, cols], sk_ref[slot_rows[r], :], pad], axis=0)
            vals = jnp.concatenate([vbuf[r, :, cols], sv_ref[slot_rows[r], :], pad], axis=0)
            live = cached[r] | (in_slots & (slot_head == k))
            s = dot_nt(qk, keys) * (HD**-0.5)
            s = jnp.where(live, s, -1e30)
            top = jnp.max(s, axis=-1, keepdims=True)
            e = jnp.where(live, jnp.exp(s - top), 0.0)
            p = (e / jnp.sum(e, axis=-1, keepdims=True)).astype(BF16)
            o = jnp.dot(p, vals, preferred_element_type=F32).astype(BF16)
            outb[2 * k, qrows, :] = o[:QR]
            outb[2 * k + 1, qrows, :] = o[QR:]
        for h in range(2):
            dst = 2 * k + h

            @pl.when(dst != m)
            def _():
                o_copy(dst).start()

        return c

    lax.fori_loop(0, KVH, attend, 0)
    topb[g, m] = outb[m]

    s_reduce(0)

    def c_wait(b, c):
        src = half * g + b

        @pl.when(src != m)
        def _():
            remote(csend, cbuf.at[b], c_s.at[b], c_r.at[b], at(mm=src)).wait_recv()

        return c

    lax.fori_loop(0, half, c_wait, 0)
    remote(red.at[0, g], red.at[0, 1 - g], red_s.at[0], red_r.at[0], at(gg=1 - g)).wait_recv()

    def sums(ph, n):
        return jnp.concatenate([red[ph, 0, n : n + 1, :], red[ph, 1, n : n + 1, :]], axis=1)

    def inv(total):
        return lax.rsqrt(total * (1.0 / D) + EPS)

    def scale_cot(n, row):
        ax[n] = (cbuf[...].reshape(HC, T).astype(F32) * row).astype(BF16)

    scale = (2.0 * D) ** -0.5
    CB = min(HC, 256)

    def tile(i, q, terms):
        cols = slice(q * FQ, (q + 1) * FQ)

        def one(n, c):
            rows = pl.ds(pl.multiple_of(n * CB, CB), CB)
            total = None
            for n_x, gain in terms:
                part = jnp.dot(ax[n_x, rows, :], vx[n_x, :, cols], preferred_element_type=F32)
                if gain is not None:
                    part = part * jg_ref[gain : gain + 1, cols]
                total = part if total is None else total + part
            tb[i, q, rows, :] = (total * (ng_ref[i : i + 1, cols] * scale)).astype(BF16)
            return c

        lax.fori_loop(0, HC // CB, one, 0)

    ORDER = (0, 3, 1, 2)

    def length(way, q):
        return H if (way == 0) == (q < NQ // 2) else H - 1

    def zrows(zz):
        return pl.ds(pl.multiple_of(lax.rem(zz + NZ, NZ) * RB, RB), RB)

    def ring_copy(i, way, q, s):
        step = 1 if way == 0 else -1
        if s == 1:
            src = tb.at[i, q, zrows(z + step * length(way, q))]
        else:
            src = sring.at[i, way, q, s - 2]
        return remote(
            src, rring.at[i, way, q, s - 1], ring_s.at[i, way, q, s - 1], ring_r.at[i, way, q, s - 1],
            at(dd=zdev(z + step)),
        )

    def ring_step(i, s, q):
        for way in range(2):
            if s > length(way, q):
                continue
            if s > 1:
                ring_copy(i, way, q, s - 1).wait_recv()
                step = 1 if way == 0 else -1
                own = tb[i, q, zrows(z + step * (length(way, q) + 1 - s)), :].astype(F32)
                sring[i, way, q, s - 2] = (own + rring[i, way, q, s - 2].astype(F32)).astype(BF16)
            ring_copy(i, way, q, s).start()

    def ring_steps(i, s):
        for q in ORDER:
            ring_step(i, s, q)

    def gradient(i, terms):
        for q in ORDER:
            tile(i, q, terms)
            ring_step(i, 1, q)

    def y_copy(i, q):
        return remote(sy.at[i, q], ry.at[i, q], y_s.at[i, q], y_r.at[i, q], at(dd=z * NY + 1 - y))

    def ring_end(i):
        for q in ORDER:
            for way in range(2):
                if length(way, q) > 0:
                    ring_copy(i, way, q, length(way, q)).wait_recv()
            cols = slice(q * FQ, (q + 1) * FQ)

            def total(yy):
                t = tb[i, q, pl.ds(pl.multiple_of(z * RB + yy * SH, SH), SH), :].astype(F32)
                for way in range(2):
                    if length(way, q) > 0:
                        here = pl.ds(pl.multiple_of(yy * SH, SH), SH)
                        t = t + rring[i, way, q, length(way, q) - 1, here, :].astype(F32)
                return t

            if NY == 2:
                other = total(1 - y)
                sy[i, q] = other.astype(BF16)
                y_copy(i, q).start()
            here = total(y)
            own_t[i, :, cols] = here
            if i == 1:
                part = here * w_two[1, :, cols]
                if NY == 2:
                    part = part + other * wpart[:, cols].astype(F32)
                w_two[0, 0:1, cols] = jnp.sum(part, axis=0, keepdims=True)

    def grad_end(i):
        for q in range(NQ):
            if NY == 2:
                cols = slice(q * FQ, (q + 1) * FQ)
                y_copy(i, q).wait_recv()
                own_t[i, :, cols] = own_t[i, :, cols] + ry[i, q].astype(F32)

    def g_copy(i, j):
        return remote(gsend.at[i], grecv.at[i, d], g_s.at[i, j], g_r.at[i, d], at(dd=lax.rem(d + j, DP)))

    def gain_send(i, row):
        tiles = jnp.concatenate([row[:, t * HD : (t + 1) * HD] for t in range(LT)], axis=0)
        gsend[i] = tiles / ngn_ref[pl.ds(i, LT, stride=2), :]

        def go(j, c):
            g_copy(i, j).start()
            return c

        lax.fori_loop(1, DP, go, 0)

    def gain_total(i):
        def add(j, total):
            src = lax.rem(d + j, DP)
            remote(gsend.at[i], grecv.at[i, src], g_s.at[i, j], g_r.at[i, src], at(dd=src)).wait_recv()
            return total + grecv[i, src]

        return lax.fori_loop(1, DP, add, gsend[i])

    def adam(i):
        rows = pl.ds(i, SH * LT, stride=2)
        grad = own_t[i].reshape(SH, LT, HD).reshape(SH * LT, HD)
        w = wbuf[rows, :]
        a = first_beta * m1buf[rows, :] + (1.0 - first_beta) * grad
        b = second_beta * m2buf[rows, :] + (1.0 - second_beta) * grad * grad
        m1_out[rows, :] = a
        m2_out[rows, :] = b
        ca = a * (1.0 / (1.0 - first_beta**adam_steps))
        cb = b * (1.0 / (1.0 - second_beta**adam_steps))
        w_out[rows, :] = w - learn_rate * (ca / (jnp.sqrt(cb) + 1e-08) + decay_rate * w)

    scale_cot(0, inv(sums(0, 0)))
    gradient(0, ((0, None),))

    def stats1(j, c):
        i = flip(m, j, MP)

        @pl.when(i != m)
        def _():
            remote(outb.at[i], topb.at[g, i], o_s.at[i], o_r.at[i], at(mm=i)).wait_recv()

        l, v, t = native_block(lob[i, g]), native_block(mib[i, g]), native_block(topb[g, i])
        gl, gv, gt = l * g0, v * g1, t * g2
        rows = pl.ds(pl.multiple_of(i * SUB, SUB), SUB)
        for n, p in enumerate((t * t, gt * gt, gl * gt, gv * gt)):
            zbuf[n, rows, :] = fold(p)
        return c

    lax.fori_loop(0, MP, stats1, 0)
    ssend[1] = row_sums(4)
    s_begin(1)
    top_copy = remote(topb.at[g], topb.at[g], top_s, top_r, at(gg=1 - g))
    top_copy.start()
    if NY == 2:
        w_copy().start()
    relayout_all(3, lambda i, gg: topb[gg, i], g)
    if H >= 2:
        ring_steps(0, 2)
    remote(topb.at[g], topb.at[1 - g], top_s, top_r, at(gg=1 - g)).wait_recv()
    relayout_all(3, lambda i, gg: topb[gg, i], 1 - g)
    if H >= 3:
        ring_steps(0, 3)
    s_reduce(1)
    remote(red.at[1, g], red.at[1, 1 - g], red_s.at[1], red_r.at[1], at(gg=1 - g)).wait_recv()

    rl, rv, rt = inv(sums(0, 1)), inv(sums(0, 2)), inv(sums(1, 0))
    joined = (
        rl * rl * sums(0, 3)
        + rv * rv * sums(0, 4)
        + rt * rt * sums(1, 1)
        + 2.0 * (rl * rv * sums(0, 5) + rl * rt * sums(1, 2) + rv * rt * sums(1, 3))
    )
    rj = inv(jnp.maximum(joined, 0.0))
    scale_cot(1, rl * rj)
    scale_cot(2, rv * rj)
    scale_cot(3, rt * rj)
    gradient(1, ((1, 0), (2, 1), (3, 2)))

    if H >= 4:
        ring_steps(0, 4)
    if H >= 2:
        ring_steps(1, 2)
    ring_end(0)
    if H >= 3:
        ring_steps(1, 3)
    loads["m1"].wait()
    loads["m2"].wait()
    grad_end(0)
    gain_send(0, jnp.sum(own_t[0] * w_two[0], axis=0, keepdims=True))
    adam(0)
    if NY == 2:
        w_copy().wait_recv()
    if H >= 4:
        ring_steps(1, 4)
    ring_end(1)
    gain_send(1, w_two[0, 0:1, :])
    grad_end(1)
    adam(1)

    for i in range(2):
        gsib_s[i] = gain_total(i)
    g_pair = remote(gsib_s, gsib_r, gx_s, gx_r, at(gg=1 - g))
    g_pair.start()
    g_pair.wait_recv()
    for i in range(2):
        gain_out[pl.ds(i, LT, stride=2), :] = gsib_s[i] + gsib_r[i]

    def drain(j, c):
        q_copy(j).wait_send()
        o_copy(peer(j)).wait_send()
        s_copy(0, j).wait_send()
        s_copy(1, j).wait_send()
        return c

    lax.fori_loop(1, MP, drain, 0)

    @pl.when(sends_cot)
    def _():
        def c_drain(j, c):
            c_copy(j).wait_send()
            return c

        lax.fori_loop(1, MP, c_drain, 0)

    for ph in range(2):
        red_copy(ph).wait_send()
    top_copy.wait_send()
    for i in range(2):
        for q in range(NQ):
            for way in range(2):
                for s in range(1, length(way, q) + 1):
                    ring_copy(i, way, q, s).wait_send()
            if NY == 2:
                y_copy(i, q).wait_send()

        def g_drain(j, c):
            g_copy(i, j).wait_send()
            return c

        lax.fori_loop(1, DP, g_drain, 0)
    if NY == 2:
        w_copy().wait_send()
    g_pair.wait_send()


def hand_on(*refs):
    n = len(refs) // 2
    sems = refs[-1]
    copies = [pltpu.make_async_copy(refs[i], refs[n + i], sems.at[i]) for i in range(n)]
    for copy in copies:
        copy.start()
    for copy in copies:
        copy.wait()


def shards(
    NZ, NY, MP,
    queries, cache_keys, cache_values, slot_keys, slot_values, cache_lengths,
    embeddings, layer_low, layer_mid, accepted, join_gain, norm_gain,
    key_cotangent, key_weight, moment_first, moment_second,
):
    rows, slots, F = embeddings.shape
    D = F * MP
    KW = cache_keys.shape[2]
    KVH = KW // HD
    SH = key_weight.shape[0]
    HC = SH * NZ * NY
    T = rows * slots
    TH = T // 2
    LT = F // HD
    RB = NY * SH
    H = NZ // 2
    cols = key_cotangent.shape[2]
    DP = NZ * NY
    FQ = F // NQ

    def tokens(x):
        return native(x).reshape(MP, 2, 2 * LT * slots, HD)

    hbm = pl.BlockSpec(memory_space=pl.ANY)
    vmem = pl.BlockSpec(memory_space=pltpu.VMEM)
    smem = pl.BlockSpec(memory_space=pltpu.SMEM)
    dma = pltpu.SemaphoreType.DMA
    B = 2 * LT * slots
    shape = jax.ShapeDtypeStruct
    outs = pl.pallas_call(
        functools.partial(kernel, (NZ, NY, MP, KVH, F, D, HC, SH)),
        out_shape=(
            shape((SH * 2 * LT, HD), F32),
            shape((SH * 2 * LT, HD), F32),
            shape((SH * 2 * LT, HD), F32),
            shape((2 * LT, HD), F32),
        ),
        in_specs=[hbm, hbm, hbm, vmem, vmem, smem, hbm, hbm, hbm] + [vmem] * 5 + [hbm, hbm, hbm],
        out_specs=(vmem, vmem, vmem, vmem),
        scratch_shapes=[
            pltpu.VMEM((MP, B, HD), BF16),
            pltpu.VMEM((2, 64, KW), BF16),
            pltpu.VMEM((2, 64, KW), BF16),
            pltpu.VMEM((MP, B, HD), BF16),
            pltpu.VMEM((MP, 2, B, HD), BF16),
            pltpu.VMEM((MP, 2, B, HD), BF16),
            pltpu.VMEM((MP, 2, B, HD), BF16),
            pltpu.VMEM((2, MP, B, HD), BF16),
            pltpu.VMEM((cols, T), BF16),
            pltpu.VMEM((MP // 2, cols, T), BF16),
            pltpu.VMEM((SH * 2 * LT, HD), F32),
            pltpu.VMEM((SH * 2 * LT, HD), F32),
            pltpu.VMEM((SH * 2 * LT, HD), F32),
            pltpu.VMEM((3, LT // 2, SUB, HD), F32),
            pltpu.VMEM((SUB, TH, HD), F32),
            pltpu.VMEM((2, SUB, TH), F32),
            pltpu.VMEM((2, MP, SUB, TH), F32),
            pltpu.VMEM((2, 2, SUB, TH), F32),
            pltpu.VMEM((4, T, F), BF16),
            pltpu.VMEM((4, HC, T), BF16),
            pltpu.VMEM((2, NQ, HC, FQ), BF16),
            pltpu.VMEM((2, 2, NQ, max(H - 1, 1), RB, FQ), BF16),
            pltpu.VMEM((2, 2, NQ, H, RB, FQ), BF16),
            pltpu.VMEM((2, NQ, SH, FQ), BF16),
            pltpu.VMEM((2, NQ, SH, FQ), BF16),
            pltpu.VMEM((2, SH, F), F32),
            pltpu.VMEM((2, SH, F), F32),
            pltpu.VMEM((SH, F), BF16),
            pltpu.VMEM((SH, F), BF16),
            pltpu.VMEM((2, LT, HD), F32),
            pltpu.VMEM((2, DP, LT, HD), F32),
            pltpu.VMEM((2, LT, HD), F32),
            pltpu.VMEM((2, LT, HD), F32),
            dma((9,)),
            dma((MP,)), dma((MP,)),
            dma((MP,)), dma((MP // 2,)),
            dma((MP,)), dma((MP,)),
            dma((2, MP)), dma((2, MP)),
            dma((2,)), dma((2,)),
            dma, dma,
            dma((2, 2, NQ, H)), dma((2, 2, NQ, H)),
            dma((2, NQ)), dma((2, NQ)),
            dma, dma,
            dma((2, DP)), dma((2, DP)),
            dma, dma,
        ],
        compiler_params=pltpu.CompilerParams(
            collective_id=0, has_side_effects=True, vmem_limit_bytes=VMEM_BYTES
        ),
        cost_estimate=pl.CostEstimate(
            flops=2 * 4 * HC * T * F, bytes_accessed=6 * 1024 * 1024, transcendentals=0
        ),
        name="draft_step",
    )(
        tokens(queries), cache_keys, cache_values, native(slot_keys), native(slot_values), cache_lengths,
        tokens(embeddings), tokens(layer_low), tokens(layer_mid), key_cotangent, accepted[None],
        join_gain, norm_gain, native(norm_gain[None]),
        native(key_weight), native(moment_first), native(moment_second),
    )
    outs = pl.pallas_call(
        hand_on,
        out_shape=[shape(x.shape, x.dtype) for x in outs],
        in_specs=[hbm] * 4,
        out_specs=[hbm] * 4,
        scratch_shapes=[dma((4,))],
        compiler_params=pltpu.CompilerParams(vmem_limit_bytes=VMEM_BYTES),
        name="hand_on",
    )(*outs)
    new = [from_native(x, SH, 2, F) for x in outs[:3]]
    return (*new, from_native(outs[3], 1, 2, F)[0])


def solution(mesh, NY=2):
    NZ, MP = mesh.shape["dp"] // NY, mesh.shape["mp"]
    tokens, owners, moments = P("dp", None, "mp"), P(("dp", "mp"), None, None), P(("group", "dp"), None, "mp")
    return jax.shard_map(
        functools.partial(shards, NZ, NY, MP),
        mesh=mesh,
        in_specs=(
            tokens, owners, owners, owners, owners, P(("dp", "mp")), tokens, tokens, tokens, P("dp"),
            P(None, "mp"), P(None, "mp"), tokens, moments, moments, moments,
        ),
        out_specs=(moments, moments, moments, P(None, "mp")),
        check_vma=False,
    )
```

```python
import functools

import jax
import jax.numpy as jnp
from jax import lax
from jax.experimental import pallas as pl
from jax.experimental.pallas import tpu as pltpu
from jax.sharding import PartitionSpec as P

HD = 128
SUB = 8
VMEM_BYTES = 62 * 1024 * 1024
NQ = 4
EPS = 1e-05
first_beta = 0.9
second_beta = 0.95
learn_rate = 0.05
decay_rate = 0.1
adam_steps = 3
slot_decay = 0.8
MESH = pl.DeviceIdType.MESH
F32 = jnp.float32
BF16 = jnp.bfloat16


def native(x):
    rows, slots, width = x.shape
    x = x.reshape(rows, slots, width // HD, HD).transpose(0, 2, 1, 3)
    return x.reshape(rows * (width // HD) * slots, HD)


def from_native(y, rows, slots, width):
    y = y.reshape(rows, width // HD, slots, HD).transpose(0, 2, 1, 3)
    return y.reshape(rows, slots, width)


def dot_nt(a, b, **kw):
    return lax.dot_general(a, b, (((1,), (1,)), ((), ())), preferred_element_type=F32, **kw)


def swap_halves(x):
    return jnp.concatenate([x[:, 4:], x[:, :4]], axis=1)


def kernel(
    dims,
    q_hbm, ck_hbm, cv_hbm, sk_ref, sv_ref, len_ref, em_hbm, lo_hbm, mi_hbm, cot_ref, acc_ref,
    jg_ref, ng_ref, ngn_ref, w_hbm, m1_hbm, m2_hbm,
    w_out, m1_out, m2_out, gain_out,
    rxq, kbuf, vbuf, outb, emb, lob, mib, topb, csend, cbuf, wbuf, m1buf, m2buf,
    gpat, zbuf, ssend, srecv, red, vx, ax, tb, sring, rring, sy, ry, own_t,
    w_two, wsend, wpart, gsend, grecv, gsib_s, gsib_r,
    lsem, q_s, q_r, c_s, c_r, c2_s, c2_r, o_s, o_r, s_s, s_r, red_s, red_r, top_s, top_r,
    ring_s, ring_r, y_s, y_r, wx_s, wx_r, g_s, g_r, gx_s, gx_r,
):
    NZ, NY, MP, MX, KVH, F, D, HC, SH = dims
    MY = MP // MX
    YH = MY // 2
    LT = F // HD
    T = MP * 4 * SUB // 2
    TH = T // 2
    H = NZ // 2
    DP = NZ * NY
    FH = F // 2
    g = lax.axis_index("group")
    d = lax.axis_index("dp")
    m = lax.axis_index("mp")
    z, y = d // NY, lax.rem(d, NY)
    ml, mx = m // MX, lax.rem(m, MX)

    def at(gg=None, dd=None, mm=None):
        return (g if gg is None else gg, d if dd is None else dd, m if mm is None else mm)

    def zdev(zz):
        return lax.rem(zz + NZ, NZ) * NY + y

    def remote(src, dst, s, r, dev):
        return pltpu.make_async_remote_copy(
            src_ref=src, dst_ref=dst, send_sem=s, recv_sem=r, device_id=dev, device_id_type=MESH
        )

    def flips(a, n):
        return [(b, b * (1 - 2 * lax.rem(a // b, 2))) for b in (1, 2, 4, 8) if b < n]

    def flipped(a, bits, j):
        for b, delta in bits:
            if j & b:
                a = a + delta
        return a

    m_bits, d_bits, x_bits, y_bits = flips(m, MP), flips(d, DP), flips(mx, MX), flips(ml, MY)

    def peer(j):
        return flipped(m, m_bits, j)

    def dpeer(j):
        return flipped(d, d_bits, j)

    loads = {
        "lo": pltpu.make_async_copy(lo_hbm, lob, lsem.at[0]),
        "mi": pltpu.make_async_copy(mi_hbm, mib, lsem.at[1]),
        "em": pltpu.make_async_copy(em_hbm, emb, lsem.at[2]),
        "q": pltpu.make_async_copy(q_hbm.at[m, g], rxq.at[m], lsem.at[3]),
        "k": pltpu.make_async_copy(ck_hbm.at[pl.ds(2 * g, 2)], kbuf, lsem.at[4]),
        "v": pltpu.make_async_copy(cv_hbm.at[pl.ds(2 * g, 2)], vbuf, lsem.at[5]),
        "w": pltpu.make_async_copy(w_hbm, wbuf, lsem.at[6]),
        "m1": pltpu.make_async_copy(m1_hbm, m1buf, lsem.at[7]),
        "m2": pltpu.make_async_copy(m2_hbm, m2buf, lsem.at[8]),
    }
    for load in loads.values():
        load.start()

    bar = pltpu.get_barrier_semaphore()

    for j in range(DP - 1, 0, -1):
        pl.semaphore_signal(bar, inc=1, device_id=at(dd=dpeer(j)), device_id_type=MESH)
    for j in range(MP - 1, 0, -1):
        pl.semaphore_signal(bar, inc=1, device_id=at(mm=peer(j)), device_id_type=MESH)
    pl.semaphore_signal(bar, inc=1, device_id=at(gg=1 - g), device_id_type=MESH)

    RD = 4 * MP
    ct = cot_ref[...].astype(F32).reshape(RD // 2, 2, 4, cot_ref.shape[2])
    ct = jnp.concatenate([ct[:, 0], ct[:, 1]], axis=1).reshape(MP, 2, SUB, cot_ref.shape[2])
    ct = jnp.concatenate([ct[:, 0], ct[:, 1]], axis=0).reshape(T, cot_ref.shape[2])
    token = lax.broadcasted_iota(jnp.int32, (RD, T), 1)
    quad = token // 4
    part = lax.rem(quad, RD // 2)
    row = (part // 2) * 4 + (quad // (RD // 2)) * 2 + lax.rem(part, 2)
    pick = (lax.broadcasted_iota(jnp.int32, (RD, T), 0) == row).astype(BF16)
    lengths = jnp.broadcast_to(acc_ref[...].astype(F32), (SUB, RD)).astype(BF16)
    taken = jnp.dot(lengths, pick, preferred_element_type=F32)[:1]
    slot = lax.rem(lax.broadcasted_iota(jnp.int32, (1, T), 1), 4)
    weight = jnp.zeros((1, T), F32)
    for s in range(4):
        weight = jnp.where((slot == s) & (taken > s + 0.5), jnp.float32(slot_decay**s), weight)
    csend[...] = (ct.T * weight).astype(BF16)

    sub8 = lax.broadcasted_iota(jnp.int32, (1, SUB, HD), 1) < 4
    for a in range(3):
        for lp in range(LT // 2):
            lower = jg_ref[a : a + 1, 2 * lp * HD : (2 * lp + 1) * HD]
            upper = jg_ref[a : a + 1, (2 * lp + 1) * HD : (2 * lp + 2) * HD]
            gpat[a, lp] = jnp.where(sub8[0], lower, upper)

    def native_block(x):
        return x.astype(F32).reshape(2, LT // 2, SUB, HD)

    def fold(p):
        t = jnp.sum(p, axis=1)
        t = t + swap_halves(t)
        return jnp.where(sub8[0], t[0], t[1])

    loads["lo"].wait()
    loads["mi"].wait()
    loads["em"].wait()
    g0, g1, g2 = gpat[0], gpat[1], gpat[2]

    def stats0(i, c):
        e, l, v = native_block(emb[i, g]), native_block(lob[i, g]), native_block(mib[i, g])
        gl, gv = l * g0, v * g1
        rows = pl.ds(pl.multiple_of(i * SUB, SUB), SUB)
        for n, p in enumerate((e * e, l * l, v * v, gl * gl, gv * gv, gl * gv)):
            zbuf[n, rows, :] = fold(p)
        return c

    lax.fori_loop(0, MP, stats0, 0)

    def row_sums(count):
        total = jnp.zeros((SUB, TH), F32)
        for n in range(count):
            pick = (lax.broadcasted_iota(jnp.int32, (SUB, HD), 0) == n).astype(F32)
            total = total + dot_nt(pick, zbuf[n], precision=lax.Precision.HIGHEST)
        return total

    ssend[0] = row_sums(6)

    def relayout(x):
        x = native_block(x)
        a, b = x[0], x[1]
        return jnp.where(sub8, a, swap_halves(b)), jnp.where(sub8, swap_halves(a), b)

    def relayout_all(n, load, gg):
        def two(i, c):
            parts = [relayout(load(2 * i + h, gg)) for h in range(2)]
            rows = pl.ds(pl.multiple_of(gg * TH + i * 2 * SUB, 2 * SUB), 2 * SUB)
            for lp in range(LT // 2):
                for k in range(2):
                    tile = jnp.concatenate([parts[0][k][lp], parts[1][k][lp]], axis=0)
                    lt = 2 * lp + k
                    vx[n, rows, lt * HD : (lt + 1) * HD] = tile.astype(BF16)
            return c

        lax.fori_loop(0, MP // 2, two, 0)

    for gg in range(2):
        relayout_all(0, lambda i, gg: emb[i, gg], gg)
    loads["w"].wait()
    for i in range(2):
        w = wbuf[pl.ds(i, SH * LT, stride=2), :].astype(BF16).astype(F32)
        w_two[i] = w.reshape(SH, LT, HD).reshape(SH, F)
    wsend[...] = w_two[1].astype(BF16)

    pl.semaphore_wait(bar, DP - 1 + MP - 1 + 1)

    def q_copy(j):
        dst = peer(j)
        return remote(q_hbm.at[dst, g], rxq.at[m], q_s, q_r.at[ml], at(mm=dst))

    for j in range(MP - 1, 0, -1):
        q_copy(j).start()

    sends_cot = (ml // YH) == g
    mine = lax.rem(ml, YH)

    def c_copy(j):
        to = flipped(ml, y_bits, j) * MX + mx
        return remote(csend, cbuf.at[mx, mine], c_s, c_r.at[mine], at(mm=to))

    @pl.when(sends_cot)
    def _():
        cbuf[mx, mine] = csend[...]
        for j in range(MY - 1, 0, -1):
            c_copy(j).start()

    def c_forward(j):
        to = ml * MX + flipped(mx, x_bits, j)
        return remote(cbuf.at[mx], cbuf.at[mx], c2_s, c2_r, at(mm=to))

    def c_turn():
        for b in range(YH):

            @pl.when((YH * g + b) != ml)
            def _():
                remote(csend, cbuf.at[mx, b], c_s, c_r.at[b], at(mm=(YH * g + b) * MX + mx)).wait_recv()

        for j in range(MX - 1, 0, -1):
            c_forward(j).start()

    def c_end():
        remote(cbuf.at[0 : MX - 1], cbuf.at[0 : MX - 1], c2_s, c2_r, at(mm=peer(1))).wait_recv()

    def s_copy(ph, j):
        return remote(ssend.at[ph], srecv.at[ph, m], s_s.at[ph], s_r.at[ph], at(mm=peer(j)))

    def s_begin(ph):
        for j in range(MP - 1, 0, -1):
            s_copy(ph, j).start()
        srecv[ph, m] = ssend[ph]

    s_begin(0)

    def s_all(ph):
        some = srecv.at[ph, 0 : MP - 1]
        return remote(some, some, s_s.at[ph], s_r.at[ph], at(mm=peer(1)))

    def red_copy(ph):
        return remote(red.at[ph, g], red.at[ph, g], red_s.at[ph], red_r.at[ph], at(gg=1 - g))

    def s_reduce(ph):
        s_all(ph).wait_recv()
        red[ph, g] = jnp.sum(srecv[ph], axis=0)
        red_copy(ph).start()

    def w_copy():
        return remote(wsend, wpart, wx_s, wx_r, at(dd=z * NY + 1 - y))

    for gg in range(2):
        relayout_all(1, lambda i, gg: lob[i, gg], gg)
        relayout_all(2, lambda i, gg: mib[i, gg], gg)

    loads["k"].wait()
    loads["v"].wait()
    loads["q"].wait()
    CP = 64
    SR = KVH * 4
    QR = 32
    rowi = lax.broadcasted_iota(jnp.int32, (2 * QR, HD), 0)
    coli = lax.broadcasted_iota(jnp.int32, (2 * QR, HD), 1)
    scol = coli - CP
    in_slots = (scol >= 0) & (scol < SR) & (lax.rem(scol, 4) <= lax.rem(rowi, 4))
    slot_head = scol // 4
    pad = jnp.zeros((HD - CP - SR, HD), BF16)
    slot_rows = [pl.ds(pl.multiple_of((2 * g + r) * SR, SR), SR) for r in range(2)]
    cached = [coli < jnp.minimum(len_ref[2 * g + r], CP) for r in range(2)]

    def o_copy(dst):
        return remote(outb.at[dst], topb.at[g, m], o_s, o_r.at[ml], at(mm=dst))

    def attend(k):
        cols = pl.ds(pl.multiple_of(k * HD, HD), HD)
        for r in range(2):
            qrows = slice(r * QR, (r + 1) * QR)
            qk = jnp.concatenate([rxq[2 * k, qrows, :], rxq[2 * k + 1, qrows, :]], axis=0)
            keys = jnp.concatenate([kbuf[r, :, cols], sk_ref[slot_rows[r], :], pad], axis=0)
            vals = jnp.concatenate([vbuf[r, :, cols], sv_ref[slot_rows[r], :], pad], axis=0)
            live = cached[r] | (in_slots & (slot_head == k))
            s = dot_nt(qk, keys) * (HD**-0.5)
            s = jnp.where(live, s, -1e30)
            top = jnp.max(s, axis=-1, keepdims=True)
            e = jnp.where(live, jnp.exp(s - top), 0.0)
            p = (e / jnp.sum(e, axis=-1, keepdims=True)).astype(BF16)
            o = jnp.dot(p, vals, preferred_element_type=F32).astype(BF16)
            yield 2 * k, qrows, o[:QR]
            yield 2 * k + 1, qrows, o[QR:]

    for jy in range(MY):
        yl = flipped(ml, y_bits, jy)
        count = MX - 1 if jy == 0 else MX
        some = rxq.at[0:count]
        remote(some, some, q_s, q_r.at[yl], at(mm=peer(1))).wait_recv()
        done = []
        for h in range(MX // 2):
            done += list(attend(yl * (MX // 2) + h))
        for dst, qrows, o in done:
            outb[dst, qrows, :] = o
        for jx in range(MX):
            if jx or jy:
                o_copy(yl * MX + flipped(mx, x_bits, jx)).start()
        if jy == min(1, MY - 1):
            c_turn()
    topb[g, m] = outb[m]

    s_reduce(0)

    c_end()
    remote(red.at[0, g], red.at[0, 1 - g], red_s.at[0], red_r.at[0], at(gg=1 - g)).wait_recv()

    def sums(ph, n):
        return jnp.concatenate([red[ph, 0, n : n + 1, :], red[ph, 1, n : n + 1, :]], axis=1)

    def inv(total):
        return lax.rsqrt(total * (1.0 / D) + EPS)

    def scale_cot(n, row):
        for b in range(YH):
            for x in range(MX):
                rows = slice((b * MX + x) * CW, (b * MX + x + 1) * CW)
                ax[n, rows, :] = (cbuf[x, b].astype(F32) * row).astype(BF16)

    CW = HC // (YH * MX)
    scale = (2.0 * D) ** -0.5
    CB = min(HC, 256)
    ZB = CB // (NY * SH)

    def tile(i, q, terms):
        cols = slice(q * FH // 2, (q + 1) * FH // 2)
        here = slice((q % 2) * FH // 2, (q % 2 + 1) * FH // 2)
        for n in range(HC // CB):
            total = None
            for n_x, gain in terms:
                part = jnp.dot(ax[n_x, n * CB : (n + 1) * CB, :], vx[n_x, :, cols], preferred_element_type=F32)
                if gain is not None:
                    part = part * jg_ref[gain : gain + 1, cols]
                total = part if total is None else total + part
            total = (total * (ng_ref[i : i + 1, cols] * scale)).astype(BF16)
            total = total.reshape(ZB, NY, SH, FH // 2)
            for yy in range(NY):
                tb[i, yy, q // 2, n * ZB : (n + 1) * ZB, :, here] = total[:, yy]

    CHUNKS = [q for q in range(NQ) if NY == 2 or q >= 2]

    def y_of(q):
        return 1 - y if q < 2 else y

    def length(way, q):
        return H if (way == 0) == (q % 2 == 0) else H - 1

    def term(i, q, zz):
        return tb.at[i, y_of(q), q % 2, lax.rem(zz + NZ, NZ)]

    def ring_copy(i, way, q, s):
        step = 1 if way == 0 else -1
        src = term(i, q, z + step * length(way, q)) if s == 1 else sring.at[i, way, q, s - 2]
        return remote(
            src, rring.at[i, way, q, s - 1], ring_s.at[i, int(s == H)], ring_r.at[i, way, q, s - 1],
            at(dd=zdev(z + step)),
        )

    def ring_step(i, s, q):
        for way in range(2):
            if s > length(way, q):
                continue
            if s > 1:
                ring_copy(i, way, q, s - 1).wait_recv()
                step = 1 if way == 0 else -1
                own = term(i, q, z + step * (length(way, q) + 1 - s))[...].astype(F32)
                sring[i, way, q, s - 2] = (own + rring[i, way, q, s - 2].astype(F32)).astype(BF16)
            ring_copy(i, way, q, s).start()

    def ring_steps(i, s):
        for q in CHUNKS:
            ring_step(i, s, q)

    def ring_sent(i):
        ways = len(CHUNKS) // 2
        if H > 1:
            some = rring.at[i, :, 0 : len(CHUNKS), 0 : H - 1]
            remote(some, some, ring_s.at[i, 0], ring_r.at[i, 0, 0, 0], at(dd=zdev(z + 1))).wait_send()
        some = rring.at[i, :, 0:ways, 0]
        remote(some, some, ring_s.at[i, 1], ring_r.at[i, 0, 0, 0], at(dd=zdev(z + 1))).wait_send()

    def gradient(i, terms):
        for ch in range(2):
            tile(i, 2 * ch, terms)
            tile(i, 2 * ch + 1, terms)
            for q in CHUNKS:
                if q % 2 == ch:
                    ring_step(i, 1, q)

    def y_copy(i, ch):
        return remote(sy.at[i, ch], ry.at[i, ch], y_s.at[i], y_r.at[i, ch], at(dd=z * NY + 1 - y))

    def y_sent(i):
        remote(sy.at[i], ry.at[i], y_s.at[i], y_r.at[i, 0], at(dd=z * NY + 1 - y)).wait_send()

    def ring_end(i):
        gain = [None, None]
        for q in CHUNKS:
            ch = q % 2
            cols = slice(ch * FH, (ch + 1) * FH)
            t = term(i, q, z)[...].astype(F32)
            for way in range(2):
                n = length(way, q)
                if n > 0:
                    ring_copy(i, way, q, n).wait_recv()
                    t = t + rring[i, way, q, n - 1].astype(F32)
            if q < 2:
                sy[i, ch] = t.astype(BF16)
                y_copy(i, ch).start()
                if i == 1:
                    gain[ch] = t * wpart[:, cols].astype(F32)
            else:
                own_t[i, :, cols] = t
                if i == 1:
                    part = t * w_two[1, :, cols]
                    gain[ch] = part if gain[ch] is None else gain[ch] + part
        if i == 1:
            gain_send(1, jnp.sum(jnp.concatenate(gain, axis=1), axis=0, keepdims=True))

    def grad_end(i):
        if NY == 2:
            for ch in range(2):
                cols = slice(ch * FH, (ch + 1) * FH)
                y_copy(i, ch).wait_recv()
                own_t[i, :, cols] = own_t[i, :, cols] + ry[i, ch].astype(F32)

    def g_copy(i, j):
        return remote(gsend.at[i], grecv.at[i, d], g_s.at[i], g_r.at[i], at(dd=dpeer(j)))

    def gain_send(i, row):
        tiles = jnp.concatenate([row[:, t * HD : (t + 1) * HD] for t in range(LT)], axis=0)
        gsend[i] = tiles / ngn_ref[pl.ds(i, LT, stride=2), :]
        for j in range(DP - 1, 0, -1):
            g_copy(i, j).start()
        grecv[i, d] = gsend[i]

    def g_all(i):
        some = grecv.at[i, 0 : DP - 1]
        return remote(some, some, g_s.at[i], g_r.at[i], at(dd=dpeer(1)))

    def gain_total(i):
        g_all(i).wait_recv()
        return jnp.sum(grecv[i], axis=0)

    def adam(i):
        rows = pl.ds(i, SH * LT, stride=2)
        grad = own_t[i].reshape(SH, LT, HD).reshape(SH * LT, HD)
        w = wbuf[rows, :]
        a = first_beta * m1buf[rows, :] + (1.0 - first_beta) * grad
        b = second_beta * m2buf[rows, :] + (1.0 - second_beta) * grad * grad
        m1_out[rows, :] = a
        m2_out[rows, :] = b
        ca = a * (1.0 / (1.0 - first_beta**adam_steps))
        cb = b * (1.0 / (1.0 - second_beta**adam_steps))
        w_out[rows, :] = w - learn_rate * (ca / (jnp.sqrt(cb) + 1e-08) + decay_rate * w)

    scale_cot(0, inv(sums(0, 0)))
    gradient(0, ((0, None),))

    for jy in range(MY):
        yl = flipped(ml, y_bits, jy)
        some = topb.at[0, 0 : MX - 1 if jy == 0 else MX]
        remote(some, some, o_s, o_r.at[yl], at(mm=peer(1))).wait_recv()

        def stats1(x, c):
            i = yl * MX + x
            l, v, t = native_block(lob[i, g]), native_block(mib[i, g]), native_block(topb[g, i])
            gl, gv, gt = l * g0, v * g1, t * g2
            rows = pl.ds(pl.multiple_of(i * SUB, SUB), SUB)
            for n, p in enumerate((t * t, gt * gt, gl * gt, gv * gt)):
                zbuf[n, rows, :] = fold(p)
            return c

        lax.fori_loop(0, MX, stats1, 0, unroll=2)
    ssend[1] = row_sums(4)
    s_begin(1)
    top_copy = remote(topb.at[g], topb.at[g], top_s, top_r, at(gg=1 - g))
    top_copy.start()
    if NY == 2:
        w_copy().start()
    relayout_all(3, lambda i, gg: topb[gg, i], g)
    if H >= 2:
        ring_steps(0, 2)
    remote(topb.at[g], topb.at[1 - g], top_s, top_r, at(gg=1 - g)).wait_recv()
    relayout_all(3, lambda i, gg: topb[gg, i], 1 - g)
    if H >= 3:
        ring_steps(0, 3)

    def sent(block, count, sem, r):
        some = block.at[0:count]
        remote(some, some, sem, r, at(mm=peer(1))).wait_send()

    sent(rxq, MP - 1, q_s, q_r.at[0])
    sent(outb, MP - 1, o_s, o_r.at[0])
    s_all(0).wait_send()
    sent(cbuf, MX - 1, c2_s, c2_r)

    @pl.when(sends_cot)
    def _():
        some = ax.at[0, 0 : (MY - 1) * CW]
        remote(some, some, c_s, c_r.at[0], at(mm=peer(1))).wait_send()

    s_reduce(1)
    remote(red.at[1, g], red.at[1, 1 - g], red_s.at[1], red_r.at[1], at(gg=1 - g)).wait_recv()

    rl, rv, rt = inv(sums(0, 1)), inv(sums(0, 2)), inv(sums(1, 0))
    joined = (
        rl * rl * sums(0, 3)
        + rv * rv * sums(0, 4)
        + rt * rt * sums(1, 1)
        + 2.0 * (rl * rv * sums(0, 5) + rl * rt * sums(1, 2) + rv * rt * sums(1, 3))
    )
    rj = inv(jnp.maximum(joined, 0.0))
    scale_cot(1, rl * rj)
    scale_cot(2, rv * rj)
    scale_cot(3, rt * rj)
    gradient(1, ((1, 0), (2, 1), (3, 2)))

    if H >= 4:
        ring_steps(0, 4)
    if H >= 2:
        ring_steps(1, 2)
    ring_end(0)
    if H >= 3:
        ring_steps(1, 3)
    loads["m1"].wait()
    loads["m2"].wait()
    grad_end(0)
    gain_send(0, jnp.sum(own_t[0] * w_two[0], axis=0, keepdims=True))
    adam(0)
    if NY == 2:
        w_copy().wait_recv()
    if H >= 4:
        ring_steps(1, 4)
    ring_end(1)
    grad_end(1)
    adam(1)

    for i in range(2):
        gsib_s[i] = gain_total(i)
    g_pair = remote(gsib_s, gsib_r, gx_s, gx_r, at(gg=1 - g))
    g_pair.start()
    g_pair.wait_recv()
    for i in range(2):
        gain_out[pl.ds(i, LT, stride=2), :] = gsib_s[i] + gsib_r[i]

    s_all(1).wait_send()
    for ph in range(2):
        red_copy(ph).wait_send()
    top_copy.wait_send()
    for i in range(2):
        ring_sent(i)
        if NY == 2:
            y_sent(i)
        g_all(i).wait_send()
    if NY == 2:
        w_copy().wait_send()
    g_pair.wait_send()


def hand_on(*refs):
    n = len(refs) // 3
    sems = refs[-1]
    ins = [pltpu.make_async_copy(refs[i], refs[2 * n + i], sems.at[0, i]) for i in range(n)]
    outs = [pltpu.make_async_copy(refs[2 * n + i], refs[n + i], sems.at[1, i]) for i in range(n)]
    for copy in ins:
        copy.start()
    for into, out in zip(ins, outs):
        into.wait()
        out.start()
    for out in outs:
        out.wait()


def shards(
    NZ, NY, MP,
    queries, cache_keys, cache_values, slot_keys, slot_values, cache_lengths,
    embeddings, layer_low, layer_mid, accepted, join_gain, norm_gain,
    key_cotangent, key_weight, moment_first, moment_second,
):
    rows, slots, F = embeddings.shape
    D = F * MP
    KW = cache_keys.shape[2]
    KVH = KW // HD
    SH = key_weight.shape[0]
    HC = SH * NZ * NY
    T = rows * slots
    TH = T // 2
    LT = F // HD
    H = NZ // 2
    MX = 4 if MP == 16 else 2
    YH = MP // MX // 2
    cols = key_cotangent.shape[2]
    DP = NZ * NY
    FH = F // 2

    def tokens(x):
        return native(x).reshape(MP, 2, 2 * LT * slots, HD)

    hbm = pl.BlockSpec(memory_space=pl.ANY)
    vmem = pl.BlockSpec(memory_space=pltpu.VMEM)
    smem = pl.BlockSpec(memory_space=pltpu.SMEM)
    dma = pltpu.SemaphoreType.DMA
    B = 2 * LT * slots
    shape = jax.ShapeDtypeStruct
    outs = pl.pallas_call(
        functools.partial(kernel, (NZ, NY, MP, MX, KVH, F, D, HC, SH)),
        out_shape=(
            shape((SH * 2 * LT, HD), F32),
            shape((SH * 2 * LT, HD), F32),
            shape((SH * 2 * LT, HD), F32),
            shape((2 * LT, HD), F32),
        ),
        in_specs=[hbm, hbm, hbm, vmem, vmem, smem, hbm, hbm, hbm] + [vmem] * 5 + [hbm, hbm, hbm],
        out_specs=(vmem, vmem, vmem, vmem),
        scratch_shapes=[
            pltpu.VMEM((MP, B, HD), BF16),
            pltpu.VMEM((2, 64, KW), BF16),
            pltpu.VMEM((2, 64, KW), BF16),
            pltpu.VMEM((MP, B, HD), BF16),
            pltpu.VMEM((MP, 2, B, HD), BF16),
            pltpu.VMEM((MP, 2, B, HD), BF16),
            pltpu.VMEM((MP, 2, B, HD), BF16),
            pltpu.VMEM((2, MP, B, HD), BF16),
            pltpu.VMEM((cols, T), BF16),
            pltpu.VMEM((MX, YH, cols, T), BF16),
            pltpu.VMEM((SH * 2 * LT, HD), F32),
            pltpu.VMEM((SH * 2 * LT, HD), F32),
            pltpu.VMEM((SH * 2 * LT, HD), F32),
            pltpu.VMEM((3, LT // 2, SUB, HD), F32),
            pltpu.VMEM((SUB, TH, HD), F32),
            pltpu.VMEM((2, SUB, TH), F32),
            pltpu.VMEM((2, MP, SUB, TH), F32),
            pltpu.VMEM((2, 2, SUB, TH), F32),
            pltpu.VMEM((4, T, F), BF16),
            pltpu.VMEM((4, HC, T), BF16),
            pltpu.VMEM((2, NY, 2, NZ, SH, FH), BF16),
            pltpu.VMEM((2, 2, NQ, max(H - 1, 1), SH, FH), BF16),
            pltpu.VMEM((2, 2, NQ, H, SH, FH), BF16),
            pltpu.VMEM((2, 2, SH, FH), BF16),
            pltpu.VMEM((2, 2, SH, FH), BF16),
            pltpu.VMEM((2, SH, F), F32),
            pltpu.VMEM((2, SH, F), F32),
            pltpu.VMEM((SH, F), BF16),
            pltpu.VMEM((SH, F), BF16),
            pltpu.VMEM((2, LT, HD), F32),
            pltpu.VMEM((2, DP, LT, HD), F32),
            pltpu.VMEM((2, LT, HD), F32),
            pltpu.VMEM((2, LT, HD), F32),
            dma((9,)),
            dma, dma((MP // MX,)),
            dma, dma((YH,)), dma, dma,
            dma, dma((MP // MX,)),
            dma((2,)), dma((2,)),
            dma((2,)), dma((2,)),
            dma, dma,
            dma((2, 2)), dma((2, 2, NQ, H)),
            dma((2,)), dma((2, 2)),
            dma, dma,
            dma((2,)), dma((2,)),
            dma, dma,
        ],
        compiler_params=pltpu.CompilerParams(
            collective_id=0, has_side_effects=True, vmem_limit_bytes=VMEM_BYTES
        ),
        cost_estimate=pl.CostEstimate(
            flops=2 * 4 * HC * T * F, bytes_accessed=6 * 1024 * 1024, transcendentals=0
        ),
        name="draft_step",
    )(
        tokens(queries), cache_keys, cache_values, native(slot_keys), native(slot_values), cache_lengths,
        tokens(embeddings), tokens(layer_low), tokens(layer_mid), key_cotangent, accepted[None],
        join_gain, norm_gain, native(norm_gain[None]),
        native(key_weight), native(moment_first), native(moment_second),
    )
    outs = pl.pallas_call(
        hand_on,
        out_shape=[shape(x.shape, x.dtype) for x in outs],
        in_specs=[hbm] * 4,
        out_specs=[hbm] * 4,
        scratch_shapes=[pltpu.VMEM(x.shape, x.dtype) for x in outs] + [dma((2, 4))],
        compiler_params=pltpu.CompilerParams(vmem_limit_bytes=VMEM_BYTES),
        name="hand_on",
    )(*outs)
    new = [from_native(x, SH, 2, F) for x in outs[:3]]
    return (*new, from_native(outs[3], 1, 2, F)[0])


def solution(mesh, NY=2):
    NZ, MP = mesh.shape["dp"] // NY, mesh.shape["mp"]
    tokens, owners, moments = P("dp", None, "mp"), P(("dp", "mp"), None, None), P(("group", "dp"), None, "mp")
    return jax.shard_map(
        functools.partial(shards, NZ, NY, MP),
        mesh=mesh,
        in_specs=(
            tokens, owners, owners, owners, owners, P(("dp", "mp")), tokens, tokens, tokens, P("dp"),
            P(None, "mp"), P(None, "mp"), tokens, moments, moments, moments,
        ),
        out_specs=(moments, moments, moments, P(None, "mp")),
        check_vma=False,
    )
```

```python
import functools

import jax
import jax.numpy as jnp
from jax import lax
from jax.experimental import pallas as pl
from jax.experimental.pallas import tpu as pltpu
from jax.sharding import PartitionSpec as P

HD = 128
SUB = 8
VMEM_BYTES = 62 * 1024 * 1024
NQ = 4
EPS = 1e-05
first_beta = 0.9
second_beta = 0.95
learn_rate = 0.05
decay_rate = 0.1
adam_steps = 3
slot_decay = 0.8
MESH = pl.DeviceIdType.MESH
F32 = jnp.float32
BF16 = jnp.bfloat16


def native(x):
    rows, slots, width = x.shape
    x = x.reshape(rows, slots, width // HD, HD).transpose(0, 2, 1, 3)
    return x.reshape(rows * (width // HD) * slots, HD)


def from_native(y, rows, slots, width):
    y = y.reshape(rows, width // HD, slots, HD).transpose(0, 2, 1, 3)
    return y.reshape(rows, slots, width)


def dot_nt(a, b, **kw):
    return lax.dot_general(a, b, (((1,), (1,)), ((), ())), preferred_element_type=F32, **kw)


def swap_halves(x):
    return jnp.concatenate([x[:, 4:], x[:, :4]], axis=1)


def kernel(
    dims,
    q_hbm, ck_hbm, cv_hbm, sk_hbm, sv_hbm, len_ref, em_hbm, lo_hbm, mi_hbm, cot_hbm, acc_hbm,
    jg_hbm, ng_hbm, ngn_hbm, w_hbm, m1_hbm, m2_hbm,
    w_out, m1_out, m2_out, gain_out,
    sk_ref, sv_ref, cot_ref, acc_ref, jg_ref, ng_ref, ngn_ref, rxq, kbuf, vbuf, outb, emb, lob, mib, topb, csend, cbuf, wbuf, m1buf, m2buf,
    gpat, zbuf, ssend, srecv, red, vx, ax, tb, sring, rring, sy, ry, own_t,
    w_two, wsend, wpart, gsend, grecv, gsib_s, gsib_r,
    lsem, q_s, q_r, c_s, c_r, c2_s, c2_r, o_s, o_r, s_s, s_r, red_s, red_r, top_s, top_r,
    ring_s, ring_r, y_s, y_r, wx_s, wx_r, g_s, g_r, gx_s, gx_r,
):
    NZ, NY, MP, MX, KVH, F, D, HC, SH = dims
    MY = MP // MX
    YH = MY // 2
    LT = F // HD
    T = MP * 4 * SUB // 2
    TH = T // 2
    H = NZ // 2
    DP = NZ * NY
    FH = F // 2
    g = lax.axis_index("group")
    d = lax.axis_index("dp")
    m = lax.axis_index("mp")
    z, y = d // NY, lax.rem(d, NY)
    ml, mx = m // MX, lax.rem(m, MX)

    def at(gg=None, dd=None, mm=None):
        return (g if gg is None else gg, d if dd is None else dd, m if mm is None else mm)

    def zdev(zz):
        return lax.rem(zz + NZ, NZ) * NY + y

    def remote(src, dst, s, r, dev):
        return pltpu.make_async_remote_copy(
            src_ref=src, dst_ref=dst, send_sem=s, recv_sem=r, device_id=dev, device_id_type=MESH
        )

    def flips(a, n):
        return [(b, b * (1 - 2 * lax.rem(a // b, 2))) for b in (1, 2, 4, 8) if b < n]

    def flipped(a, bits, j):
        for b, delta in bits:
            if j & b:
                a = a + delta
        return a

    m_bits, d_bits, x_bits, y_bits = flips(m, MP), flips(d, DP), flips(mx, MX), flips(ml, MY)

    def peer(j):
        return flipped(m, m_bits, j)

    def dpeer(j):
        return flipped(d, d_bits, j)

    loads = {
        "cot": pltpu.make_async_copy(cot_hbm, cot_ref, lsem.at[9]),
        "acc": pltpu.make_async_copy(acc_hbm, acc_ref, lsem.at[10]),
        "jg": pltpu.make_async_copy(jg_hbm, jg_ref, lsem.at[11]),
        "lo": pltpu.make_async_copy(lo_hbm, lob, lsem.at[0]),
        "mi": pltpu.make_async_copy(mi_hbm, mib, lsem.at[1]),
        "em": pltpu.make_async_copy(em_hbm, emb, lsem.at[2]),
        "q": pltpu.make_async_copy(q_hbm.at[m, g], rxq.at[m], lsem.at[3]),
        "k": pltpu.make_async_copy(ck_hbm.at[pl.ds(2 * g, 2)], kbuf, lsem.at[4]),
        "v": pltpu.make_async_copy(cv_hbm.at[pl.ds(2 * g, 2)], vbuf, lsem.at[5]),
        "sk": pltpu.make_async_copy(sk_hbm, sk_ref, lsem.at[12]),
        "sv": pltpu.make_async_copy(sv_hbm, sv_ref, lsem.at[13]),
        "ng": pltpu.make_async_copy(ng_hbm, ng_ref, lsem.at[14]),
        "ngn": pltpu.make_async_copy(ngn_hbm, ngn_ref, lsem.at[15]),
        "w": pltpu.make_async_copy(w_hbm, wbuf, lsem.at[6]),
        "m1": pltpu.make_async_copy(m1_hbm, m1buf, lsem.at[7]),
        "m2": pltpu.make_async_copy(m2_hbm, m2buf, lsem.at[8]),
    }
    bar = pltpu.get_barrier_semaphore()

    greeted = [at(mm=peer(j)) for j in range(MP - 1, 0, -1)]
    greeted += [at(dd=z * NY + 1 - y)] if NY == 2 else []
    greeted += [at(dd=zdev(z + 1))] + ([at(dd=zdev(z - 1))] if NZ > 2 else []) + [at(gg=1 - g)]
    for dev in greeted:
        pl.semaphore_signal(bar, inc=1, device_id=dev, device_id_type=MESH)
    for load in loads.values():
        load.start()

    RD = 4 * MP
    loads["cot"].wait()
    loads["acc"].wait()
    ct = cot_ref[...].astype(F32).reshape(RD // 2, 2, 4, cot_ref.shape[2])
    ct = jnp.concatenate([ct[:, 0], ct[:, 1]], axis=1).reshape(MP, 2, SUB, cot_ref.shape[2])
    ct = jnp.concatenate([ct[:, 0], ct[:, 1]], axis=0).reshape(T, cot_ref.shape[2])
    token = lax.broadcasted_iota(jnp.int32, (RD, T), 1)
    quad = token // 4
    part = lax.rem(quad, RD // 2)
    row = (part // 2) * 4 + (quad // (RD // 2)) * 2 + lax.rem(part, 2)
    pick = (lax.broadcasted_iota(jnp.int32, (RD, T), 0) == row).astype(BF16)
    lengths = jnp.broadcast_to(acc_ref[...].astype(F32), (SUB, RD)).astype(BF16)
    taken = jnp.dot(lengths, pick, preferred_element_type=F32)[:1]
    slot = lax.rem(lax.broadcasted_iota(jnp.int32, (1, T), 1), 4)
    weight = jnp.zeros((1, T), F32)
    for s in range(4):
        weight = jnp.where((slot == s) & (taken > s + 0.5), jnp.float32(slot_decay**s), weight)
    csend[...] = (ct.T * weight).astype(BF16)

    sub8 = lax.broadcasted_iota(jnp.int32, (1, SUB, HD), 1) < 4
    loads["jg"].wait()
    for a in range(3):
        for lp in range(LT // 2):
            lower = jg_ref[a : a + 1, 2 * lp * HD : (2 * lp + 1) * HD]
            upper = jg_ref[a : a + 1, (2 * lp + 1) * HD : (2 * lp + 2) * HD]
            gpat[a, lp] = jnp.where(sub8[0], lower, upper)

    def native_block(x):
        return x.astype(F32).reshape(2, LT // 2, SUB, HD)

    def fold(p):
        t = jnp.sum(p, axis=1)
        t = t + swap_halves(t)
        return jnp.where(sub8[0], t[0], t[1])

    loads["lo"].wait()
    loads["mi"].wait()
    loads["em"].wait()
    g0, g1, g2 = gpat[0], gpat[1], gpat[2]

    def stats0(i, c):
        e, l, v = native_block(emb[i, g]), native_block(lob[i, g]), native_block(mib[i, g])
        gl, gv = l * g0, v * g1
        rows = pl.ds(pl.multiple_of(i * SUB, SUB), SUB)
        for n, p in enumerate((e * e, l * l, v * v, gl * gl, gv * gv, gl * gv)):
            zbuf[n, rows, :] = fold(p)
        return c

    lax.fori_loop(0, MP, stats0, 0)

    def row_sums(count):
        total = jnp.zeros((SUB, TH), F32)
        for n in range(count):
            pick = (lax.broadcasted_iota(jnp.int32, (SUB, HD), 0) == n).astype(F32)
            total = total + dot_nt(pick, zbuf[n], precision=lax.Precision.HIGHEST)
        return total

    ssend[0] = row_sums(6)

    def relayout(x):
        x = native_block(x)
        a, b = x[0], x[1]
        return jnp.where(sub8, a, swap_halves(b)), jnp.where(sub8, swap_halves(a), b)

    def relayout_all(n, load, gg):
        def two(i, c):
            parts = [relayout(load(2 * i + h, gg)) for h in range(2)]
            rows = pl.ds(pl.multiple_of(gg * TH + i * 2 * SUB, 2 * SUB), 2 * SUB)
            for lp in range(LT // 2):
                for k in range(2):
                    tile = jnp.concatenate([parts[0][k][lp], parts[1][k][lp]], axis=0)
                    lt = 2 * lp + k
                    vx[n, rows, lt * HD : (lt + 1) * HD] = tile.astype(BF16)
            return c

        lax.fori_loop(0, MP // 2, two, 0)

    for gg in range(2):
        relayout_all(0, lambda i, gg: emb[i, gg], gg)
    loads["w"].wait()
    for i in range(2):
        w = wbuf[pl.ds(i, SH * LT, stride=2), :].astype(BF16).astype(F32)
        w_two[i] = w.reshape(SH, LT, HD).reshape(SH, F)
    wsend[...] = w_two[1].astype(BF16)

    pl.semaphore_wait(bar, len(greeted))

    def q_copy(j):
        dst = peer(j)
        return remote(q_hbm.at[dst, g], rxq.at[m], q_s, q_r.at[ml], at(mm=dst))

    for j in range(MP - 1, 0, -1):
        q_copy(j).start()

    sends_cot = (ml // YH) == g
    mine = lax.rem(ml, YH)

    def c_copy(j):
        to = flipped(ml, y_bits, j) * MX + mx
        return remote(csend, cbuf.at[mx, mine], c_s, c_r.at[mine], at(mm=to))

    @pl.when(sends_cot)
    def _():
        cbuf[mx, mine] = csend[...]
        for j in range(MY - 1, 0, -1):
            c_copy(j).start()

    def c_forward(j):
        to = ml * MX + flipped(mx, x_bits, j)
        return remote(cbuf.at[mx], cbuf.at[mx], c2_s, c2_r, at(mm=to))

    def c_turn():
        for b in range(YH):

            @pl.when((YH * g + b) != ml)
            def _():
                remote(csend, cbuf.at[mx, b], c_s, c_r.at[b], at(mm=(YH * g + b) * MX + mx)).wait_recv()

        for j in range(MX - 1, 0, -1):
            c_forward(j).start()

    def c_end():
        remote(cbuf.at[0 : MX - 1], cbuf.at[0 : MX - 1], c2_s, c2_r, at(mm=peer(1))).wait_recv()

    def s_copy(ph, j):
        return remote(ssend.at[ph], srecv.at[ph, m], s_s.at[ph], s_r.at[ph], at(mm=peer(j)))

    def s_begin(ph):
        for j in range(MP - 1, 0, -1):
            s_copy(ph, j).start()
        srecv[ph, m] = ssend[ph]

    s_begin(0)

    def s_all(ph):
        some = srecv.at[ph, 0 : MP - 1]
        return remote(some, some, s_s.at[ph], s_r.at[ph], at(mm=peer(1)))

    def red_copy(ph):
        return remote(red.at[ph, g], red.at[ph, g], red_s.at[ph], red_r.at[ph], at(gg=1 - g))

    def s_reduce(ph):
        s_all(ph).wait_recv()
        red[ph, g] = jnp.sum(srecv[ph], axis=0)
        red_copy(ph).start()

    def w_copy():
        return remote(wsend, wpart, wx_s, wx_r, at(dd=z * NY + 1 - y))

    for gg in range(2):
        relayout_all(1, lambda i, gg: lob[i, gg], gg)
        relayout_all(2, lambda i, gg: mib[i, gg], gg)

    loads["k"].wait()
    loads["v"].wait()
    loads["q"].wait()
    for key in ("sk", "sv", "ng", "ngn"):
        loads[key].wait()
    CP = 64
    SR = KVH * 4
    QR = 32
    rowi = lax.broadcasted_iota(jnp.int32, (2 * QR, HD), 0)
    coli = lax.broadcasted_iota(jnp.int32, (2 * QR, HD), 1)
    scol = coli - CP
    in_slots = (scol >= 0) & (scol < SR) & (lax.rem(scol, 4) <= lax.rem(rowi, 4))
    slot_head = scol // 4
    pad = jnp.zeros((HD - CP - SR, HD), BF16)
    slot_rows = [pl.ds(pl.multiple_of((2 * g + r) * SR, SR), SR) for r in range(2)]
    cached = [coli < jnp.minimum(len_ref[2 * g + r], CP) for r in range(2)]

    def o_copy(dst):
        return remote(outb.at[dst], topb.at[g, m], o_s, o_r.at[ml], at(mm=dst))

    def attend(k):
        cols = pl.ds(pl.multiple_of(k * HD, HD), HD)
        for r in range(2):
            qrows = slice(r * QR, (r + 1) * QR)
            qk = jnp.concatenate([rxq[2 * k, qrows, :], rxq[2 * k + 1, qrows, :]], axis=0)
            keys = jnp.concatenate([kbuf[r, :, cols], sk_ref[slot_rows[r], :], pad], axis=0)
            vals = jnp.concatenate([vbuf[r, :, cols], sv_ref[slot_rows[r], :], pad], axis=0)
            live = cached[r] | (in_slots & (slot_head == k))
            s = dot_nt(qk, keys) * (HD**-0.5)
            s = jnp.where(live, s, -1e30)
            top = jnp.max(s, axis=-1, keepdims=True)
            e = jnp.where(live, jnp.exp(s - top), 0.0)
            p = (e / jnp.sum(e, axis=-1, keepdims=True)).astype(BF16)
            o = jnp.dot(p, vals, preferred_element_type=F32).astype(BF16)
            yield 2 * k, qrows, o[:QR]
            yield 2 * k + 1, qrows, o[QR:]

    for jy in range(MY):
        yl = flipped(ml, y_bits, jy)
        count = MX - 1 if jy == 0 else MX
        some = rxq.at[0:count]
        remote(some, some, q_s, q_r.at[yl], at(mm=peer(1))).wait_recv()
        done = []
        for h in range(MX // 2):
            done += list(attend(yl * (MX // 2) + h))
        for dst, qrows, o in done:
            outb[dst, qrows, :] = o
        for jx in range(MX):
            if jx or jy:
                o_copy(yl * MX + flipped(mx, x_bits, jx)).start()
        if jy == min(1, MY - 1):
            c_turn()
    topb[g, m] = outb[m]

    s_reduce(0)

    c_end()
    remote(red.at[0, g], red.at[0, 1 - g], red_s.at[0], red_r.at[0], at(gg=1 - g)).wait_recv()

    def sums(ph, n):
        return jnp.concatenate([red[ph, 0, n : n + 1, :], red[ph, 1, n : n + 1, :]], axis=1)

    def inv(total):
        return lax.rsqrt(total * (1.0 / D) + EPS)

    CW = HC // (YH * MX)

    def scale_cot(n, row):
        for b in range(YH):
            for x in range(MX):
                scaled = (cbuf[x, b].astype(F32) * row).astype(BF16)
                for yy in range(NY):
                    ax[n, yy, b * MX + x] = scaled[yy * SH : (yy + 1) * SH]

    scale = (2.0 * D) ** -0.5

    def tile(i, yy, ch, terms):
        for h in range(2):
            cols = slice(ch * FH + h * FH // 2, ch * FH + (h + 1) * FH // 2)
            total = None
            for n_x, gain in terms:
                part = jnp.dot(
                    ax[n_x, yy].reshape(NZ * SH, T), vx[n_x, :, cols], preferred_element_type=F32
                )
                if gain is not None:
                    part = part * jg_ref[gain : gain + 1, cols]
                total = part if total is None else total + part
            total = (total * (ng_ref[i : i + 1, cols] * scale)).astype(BF16)
            tb[i, yy, ch, :, :, h * FH // 2 : (h + 1) * FH // 2] = total.reshape(NZ, SH, FH // 2)

    CHUNKS = [q for q in range(NQ) if NY == 2 or q >= 2]

    def y_of(q):
        return 1 - y if q < 2 else y

    def length(way, q):
        return H if (way == 0) == (q % 2 == 0) else H - 1

    def term(i, q, zz):
        return tb.at[i, y_of(q), q % 2, lax.rem(zz + NZ, NZ)]

    def ring_copy(i, way, q, s):
        step = 1 if way == 0 else -1
        src = term(i, q, z + step * length(way, q)) if s == 1 else sring.at[i, way, q, s - 2]
        return remote(
            src, rring.at[i, way, q, s - 1], ring_s.at[i, int(s == H)], ring_r.at[i, way, q, s - 1],
            at(dd=zdev(z + step)),
        )

    def ring_step(i, s, q):
        for way in range(2):
            if s > length(way, q):
                continue
            if s > 1:
                ring_copy(i, way, q, s - 1).wait_recv()
                step = 1 if way == 0 else -1
                own = term(i, q, z + step * (length(way, q) + 1 - s))[...].astype(F32)
                sring[i, way, q, s - 2] = (own + rring[i, way, q, s - 2].astype(F32)).astype(BF16)
            ring_copy(i, way, q, s).start()

    def ring_steps(i, s):
        for q in CHUNKS:
            ring_step(i, s, q)

    def ring_sent(i):
        ways = len(CHUNKS) // 2
        if H > 1:
            some = rring.at[i, :, 0 : len(CHUNKS), 0 : H - 1]
            remote(some, some, ring_s.at[i, 0], ring_r.at[i, 0, 0, 0], at(dd=zdev(z + 1))).wait_send()
        some = rring.at[i, :, 0:ways, 0]
        remote(some, some, ring_s.at[i, 1], ring_r.at[i, 0, 0, 0], at(dd=zdev(z + 1))).wait_send()

    def gradient(i, terms):
        for q in CHUNKS:
            tile(i, y_of(q), q % 2, terms)
            ring_step(i, 1, q)

    def y_copy(i, ch):
        return remote(sy.at[i, ch], ry.at[i, ch], y_s.at[i], y_r.at[i, ch], at(dd=z * NY + 1 - y))

    def y_sent(i):
        remote(sy.at[i], ry.at[i], y_s.at[i], y_r.at[i, 0], at(dd=z * NY + 1 - y)).wait_send()

    def ring_end(i):
        gain = [None, None]
        for q in CHUNKS:
            ch = q % 2
            cols = slice(ch * FH, (ch + 1) * FH)
            t = term(i, q, z)[...].astype(F32)
            for way in range(2):
                n = length(way, q)
                if n > 0:
                    ring_copy(i, way, q, n).wait_recv()
                    t = t + rring[i, way, q, n - 1].astype(F32)
            if q < 2:
                sy[i, ch] = t.astype(BF16)
                y_copy(i, ch).start()
                if i == 1:
                    gain[ch] = t * wpart[:, cols].astype(F32)
            else:
                own_t[i, :, cols] = t
                if i == 1:
                    part = t * w_two[1, :, cols]
                    gain[ch] = part if gain[ch] is None else gain[ch] + part
        if i == 1:
            gain_send(1, jnp.sum(jnp.concatenate(gain, axis=1), axis=0, keepdims=True))

    def grad_end(i):
        if NY == 2:
            for ch in range(2):
                cols = slice(ch * FH, (ch + 1) * FH)
                y_copy(i, ch).wait_recv()
                own_t[i, :, cols] = own_t[i, :, cols] + ry[i, ch].astype(F32)

    def g_copy(i, j):
        return remote(gsend.at[i], grecv.at[i, d], g_s.at[i], g_r.at[i], at(dd=dpeer(j)))

    def gain_send(i, row):
        tiles = jnp.concatenate([row[:, t * HD : (t + 1) * HD] for t in range(LT)], axis=0)
        gsend[i] = tiles / ngn_ref[pl.ds(i, LT, stride=2), :]
        for j in range(DP - 1, 0, -1):
            g_copy(i, j).start()
        grecv[i, d] = gsend[i]

    def g_all(i):
        some = grecv.at[i, 0 : DP - 1]
        return remote(some, some, g_s.at[i], g_r.at[i], at(dd=dpeer(1)))

    def gain_total(i):
        g_all(i).wait_recv()
        return jnp.sum(grecv[i], axis=0)

    def adam(i):
        rows = pl.ds(i, SH * LT, stride=2)
        grad = own_t[i].reshape(SH, LT, HD).reshape(SH * LT, HD)
        w = wbuf[rows, :]
        a = first_beta * m1buf[rows, :] + (1.0 - first_beta) * grad
        b = second_beta * m2buf[rows, :] + (1.0 - second_beta) * grad * grad
        m1_out[rows, :] = a
        m2_out[rows, :] = b
        ca = a * (1.0 / (1.0 - first_beta**adam_steps))
        cb = b * (1.0 / (1.0 - second_beta**adam_steps))
        w_out[rows, :] = w - learn_rate * (ca / (jnp.sqrt(cb) + 1e-08) + decay_rate * w)

    scale_cot(0, inv(sums(0, 0)))
    gradient(0, ((0, None),))

    for jy in range(MY):
        yl = flipped(ml, y_bits, jy)
        some = topb.at[0, 0 : MX - 1 if jy == 0 else MX]
        remote(some, some, o_s, o_r.at[yl], at(mm=peer(1))).wait_recv()

        def stats1(x, c):
            i = yl * MX + x
            l, v, t = native_block(lob[i, g]), native_block(mib[i, g]), native_block(topb[g, i])
            gl, gv, gt = l * g0, v * g1, t * g2
            rows = pl.ds(pl.multiple_of(i * SUB, SUB), SUB)
            for n, p in enumerate((t * t, gt * gt, gl * gt, gv * gt)):
                zbuf[n, rows, :] = fold(p)
            return c

        lax.fori_loop(0, MX, stats1, 0, unroll=2)
    ssend[1] = row_sums(4)
    s_begin(1)
    top_copy = remote(topb.at[g], topb.at[g], top_s, top_r, at(gg=1 - g))
    top_copy.start()
    relayout_all(3, lambda i, gg: topb[gg, i], g)
    if H >= 2:
        ring_steps(0, 2)
    remote(topb.at[g], topb.at[1 - g], top_s, top_r, at(gg=1 - g)).wait_recv()
    relayout_all(3, lambda i, gg: topb[gg, i], 1 - g)

    def sent(block, count, sem, r):
        some = block.at[0:count]
        remote(some, some, sem, r, at(mm=peer(1))).wait_send()

    sent(rxq, MP - 1, q_s, q_r.at[0])
    sent(outb, MP - 1, o_s, o_r.at[0])
    s_all(0).wait_send()
    sent(cbuf, MX - 1, c2_s, c2_r)

    @pl.when(sends_cot)
    def _():
        some = ax.at[0, 0, 0 : (MY - 1) * CW // SH]
        remote(some, some, c_s, c_r.at[0], at(mm=peer(1))).wait_send()

    s_reduce(1)
    if H >= 3:
        ring_steps(0, 3)
    remote(red.at[1, g], red.at[1, 1 - g], red_s.at[1], red_r.at[1], at(gg=1 - g)).wait_recv()

    rl, rv, rt = inv(sums(0, 1)), inv(sums(0, 2)), inv(sums(1, 0))
    joined = (
        rl * rl * sums(0, 3)
        + rv * rv * sums(0, 4)
        + rt * rt * sums(1, 1)
        + 2.0 * (rl * rv * sums(0, 5) + rl * rt * sums(1, 2) + rv * rt * sums(1, 3))
    )
    rj = inv(jnp.maximum(joined, 0.0))
    scale_cot(1, rl * rj)
    scale_cot(2, rv * rj)
    scale_cot(3, rt * rj)
    gradient(1, ((1, 0), (2, 1), (3, 2)))

    if NY == 2:
        w_copy().start()
    if H >= 4:
        ring_steps(0, 4)
    if H >= 2:
        ring_steps(1, 2)
    ring_end(0)
    if H >= 3:
        ring_steps(1, 3)
    if H >= 4:
        ring_steps(1, 4)
    loads["m1"].wait()
    loads["m2"].wait()
    grad_end(0)
    gain_send(0, jnp.sum(own_t[0] * w_two[0], axis=0, keepdims=True))
    adam(0)
    if NY == 2:
        w_copy().wait_recv()
    ring_end(1)
    grad_end(1)
    adam(1)

    for i in range(2):
        gsib_s[i] = gain_total(i)
    g_pair = remote(gsib_s, gsib_r, gx_s, gx_r, at(gg=1 - g))
    g_pair.start()
    g_pair.wait_recv()
    for i in range(2):
        gain_out[pl.ds(i, LT, stride=2), :] = gsib_s[i] + gsib_r[i]

    s_all(1).wait_send()
    for ph in range(2):
        red_copy(ph).wait_send()
    top_copy.wait_send()
    for i in range(2):
        ring_sent(i)
        if NY == 2:
            y_sent(i)
        g_all(i).wait_send()
    if NY == 2:
        w_copy().wait_send()
    g_pair.wait_send()


def hand_on(*refs):
    n = len(refs) // 2
    sems = refs[-1]
    copies = [pltpu.make_async_copy(refs[i], refs[n + i], sems.at[i]) for i in range(n)]
    for copy in copies:
        copy.start()
    for copy in copies:
        copy.wait()


def shards(
    NZ, NY, MP,
    queries, cache_keys, cache_values, slot_keys, slot_values, cache_lengths,
    embeddings, layer_low, layer_mid, accepted, join_gain, norm_gain,
    key_cotangent, key_weight, moment_first, moment_second,
):
    rows, slots, F = embeddings.shape
    D = F * MP
    KW = cache_keys.shape[2]
    KVH = KW // HD
    SH = key_weight.shape[0]
    HC = SH * NZ * NY
    T = rows * slots
    TH = T // 2
    LT = F // HD
    H = NZ // 2
    MX = 4 if MP == 16 else 2
    YH = MP // MX // 2
    cols = key_cotangent.shape[2]
    DP = NZ * NY
    FH = F // 2

    def tokens(x):
        return native(x).reshape(MP, 2, 2 * LT * slots, HD)

    hbm = pl.BlockSpec(memory_space=pl.ANY)
    vmem = pl.BlockSpec(memory_space=pltpu.VMEM)
    smem = pl.BlockSpec(memory_space=pltpu.SMEM)
    dma = pltpu.SemaphoreType.DMA
    B = 2 * LT * slots
    shape = jax.ShapeDtypeStruct
    outs = pl.pallas_call(
        functools.partial(kernel, (NZ, NY, MP, MX, KVH, F, D, HC, SH)),
        out_shape=(
            pltpu.VMEM((SH * 2 * LT, HD), F32),
            pltpu.VMEM((SH * 2 * LT, HD), F32),
            pltpu.VMEM((SH * 2 * LT, HD), F32),
            pltpu.VMEM((2 * LT, HD), F32),
        ),
        in_specs=[hbm] * 5 + [smem] + [hbm] * 11,
        out_specs=(vmem, vmem, vmem, vmem),
        scratch_shapes=[
            pltpu.VMEM((KVH * 16, HD), BF16),
            pltpu.VMEM((KVH * 16, HD), BF16),
            pltpu.VMEM(key_cotangent.shape, BF16),
            pltpu.VMEM((1, rows), jnp.int32),
            pltpu.VMEM((3, F), F32),
            pltpu.VMEM((2, F), F32),
            pltpu.VMEM((2 * LT, HD), F32),
            pltpu.VMEM((MP, B, HD), BF16),
            pltpu.VMEM((2, 64, KW), BF16),
            pltpu.VMEM((2, 64, KW), BF16),
            pltpu.VMEM((MP, B, HD), BF16),
            pltpu.VMEM((MP, 2, B, HD), BF16),
            pltpu.VMEM((MP, 2, B, HD), BF16),
            pltpu.VMEM((MP, 2, B, HD), BF16),
            pltpu.VMEM((2, MP, B, HD), BF16),
            pltpu.VMEM((cols, T), BF16),
            pltpu.VMEM((MX, YH, cols, T), BF16),
            pltpu.VMEM((SH * 2 * LT, HD), F32),
            pltpu.VMEM((SH * 2 * LT, HD), F32),
            pltpu.VMEM((SH * 2 * LT, HD), F32),
            pltpu.VMEM((3, LT // 2, SUB, HD), F32),
            pltpu.VMEM((SUB, TH, HD), F32),
            pltpu.VMEM((2, SUB, TH), F32),
            pltpu.VMEM((2, MP, SUB, TH), F32),
            pltpu.VMEM((2, 2, SUB, TH), F32),
            pltpu.VMEM((4, T, F), BF16),
            pltpu.VMEM((4, NY, NZ, SH, T), BF16),
            pltpu.VMEM((2, NY, 2, NZ, SH, FH), BF16),
            pltpu.VMEM((2, 2, NQ, max(H - 1, 1), SH, FH), BF16),
            pltpu.VMEM((2, 2, NQ, H, SH, FH), BF16),
            pltpu.VMEM((2, 2, SH, FH), BF16),
            pltpu.VMEM((2, 2, SH, FH), BF16),
            pltpu.VMEM((2, SH, F), F32),
            pltpu.VMEM((2, SH, F), F32),
            pltpu.VMEM((SH, F), BF16),
            pltpu.VMEM((SH, F), BF16),
            pltpu.VMEM((2, LT, HD), F32),
            pltpu.VMEM((2, DP, LT, HD), F32),
            pltpu.VMEM((2, LT, HD), F32),
            pltpu.VMEM((2, LT, HD), F32),
            dma((16,)),
            dma, dma((MP // MX,)),
            dma, dma((YH,)), dma, dma,
            dma, dma((MP // MX,)),
            dma((2,)), dma((2,)),
            dma((2,)), dma((2,)),
            dma, dma,
            dma((2, 2)), dma((2, 2, NQ, H)),
            dma((2,)), dma((2, 2)),
            dma, dma,
            dma((2,)), dma((2,)),
            dma, dma,
        ],
        compiler_params=pltpu.CompilerParams(
            collective_id=0, has_side_effects=True, vmem_limit_bytes=VMEM_BYTES
        ),
        cost_estimate=pl.CostEstimate(
            flops=2 * 4 * HC * T * F, bytes_accessed=6 * 1024 * 1024, transcendentals=0
        ),
        name="draft_step",
    )(
        tokens(queries), cache_keys, cache_values, native(slot_keys), native(slot_values), cache_lengths,
        tokens(embeddings), tokens(layer_low), tokens(layer_mid), key_cotangent, accepted[None],
        join_gain, norm_gain, native(norm_gain[None]),
        native(key_weight), native(moment_first), native(moment_second),
    )
    outs = pl.pallas_call(
        hand_on,
        out_shape=[shape(x.shape, x.dtype) for x in outs],
        in_specs=[vmem] * 4,
        out_specs=[hbm] * 4,
        scratch_shapes=[dma((4,))],
        compiler_params=pltpu.CompilerParams(vmem_limit_bytes=VMEM_BYTES // 8),
        name="hand_on",
    )(*outs)
    new = [from_native(x, SH, 2, F) for x in outs[:3]]
    return (*new, from_native(outs[3], 1, 2, F)[0])


def solution(mesh, NY=2):
    NZ, MP = mesh.shape["dp"] // NY, mesh.shape["mp"]
    tokens, owners, moments = P("dp", None, "mp"), P(("dp", "mp"), None, None), P(("group", "dp"), None, "mp")
    return jax.shard_map(
        functools.partial(shards, NZ, NY, MP),
        mesh=mesh,
        in_specs=(
            tokens, owners, owners, owners, owners, P(("dp", "mp")), tokens, tokens, tokens, P("dp"),
            P(None, "mp"), P(None, "mp"), tokens, moments, moments, moments,
        ),
        out_specs=(moments, moments, moments, P(None, "mp")),
        check_vma=False,
    )
```

```python
import functools

import jax
import jax.numpy as jnp
from jax import lax
from jax.experimental import pallas as pl
from jax.experimental.pallas import tpu as pltpu
from jax.sharding import PartitionSpec as P

HD = 128
SUB = 8
VMEM_BYTES = 62 * 1024 * 1024
NQ = 4
EPS = 1e-05
first_beta = 0.9
second_beta = 0.95
learn_rate = 0.05
decay_rate = 0.1
adam_steps = 3
slot_decay = 0.8
MESH = pl.DeviceIdType.MESH
F32 = jnp.float32
BF16 = jnp.bfloat16


def native(x):
    rows, slots, width = x.shape
    x = x.reshape(rows, slots, width // HD, HD).transpose(0, 2, 1, 3)
    return x.reshape(rows * (width // HD) * slots, HD)


def from_native(y, rows, slots, width):
    y = y.reshape(rows, width // HD, slots, HD).transpose(0, 2, 1, 3)
    return y.reshape(rows, slots, width)


def dot_nt(a, b, **kw):
    return lax.dot_general(a, b, (((1,), (1,)), ((), ())), preferred_element_type=F32, **kw)


def swap_halves(x):
    return jnp.concatenate([x[:, 4:], x[:, :4]], axis=1)


def kernel(
    dims,
    q_hbm, ck_hbm, cv_hbm, sk_hbm, sv_hbm, len_ref, em_hbm, lo_hbm, mi_hbm, cot_hbm, acc_hbm,
    jg_hbm, ng_hbm, ngn_hbm, w_hbm, m1_hbm, m2_hbm,
    w_out, m1_out, m2_out, gain_out,
    sk_ref, sv_ref, cot_ref, acc_ref, jg_ref, ng_ref, ngn_ref, rxq, kbuf, vbuf, outb, emb, lob, mib, topb, csend, cbuf, wbuf, m1buf, m2buf,
    gpat, zbuf, ssend, srecv, srecv2, red, vx, ax, tb, sring, rring, sy, ry, own_t,
    w_two, wz, gsend, grecv, gsib_s, gsib_r,
    lsem, q_s, q_r, c_s, c_r, c2_s, c2_r, o_s, o_r, s_s, s_r, red_s, red_r, top_s, top_r,
    ring_s, ring_r, y_s, y_r, wx_s, wx_r, wz_s, wz_r, g_s, g_r, gx_s, gx_r,
):
    NZ, NY, MP, MX, KVH, F, D, HC, SH = dims
    MY = MP // MX
    YH = MY // 2
    LT = F // HD
    T = MP * 4 * SUB // 2
    TH = T // 2
    H = NZ // 2
    DP = NZ * NY
    FH = F // 2
    g = lax.axis_index("group")
    d = lax.axis_index("dp")
    m = lax.axis_index("mp")
    z, y = d // NY, lax.rem(d, NY)
    ml, mx = m // MX, lax.rem(m, MX)

    def at(gg=None, dd=None, mm=None):
        return (g if gg is None else gg, d if dd is None else dd, m if mm is None else mm)

    def zdev(zz):
        return lax.rem(zz + NZ, NZ) * NY + y

    def remote(src, dst, s, r, dev):
        return pltpu.make_async_remote_copy(
            src_ref=src, dst_ref=dst, send_sem=s, recv_sem=r, device_id=dev, device_id_type=MESH
        )

    def flips(a, n):
        return [(b, b * (1 - 2 * lax.rem(a // b, 2))) for b in (1, 2, 4, 8) if b < n]

    def flipped(a, bits, j):
        for b, delta in bits:
            if j & b:
                a = a + delta
        return a

    m_bits, d_bits, x_bits, y_bits = flips(m, MP), flips(d, DP), flips(mx, MX), flips(ml, MY)

    def peer(j):
        return flipped(m, m_bits, j)

    def dpeer(j):
        return flipped(d, d_bits, j)

    loads = {
        "cot": pltpu.make_async_copy(cot_hbm, cot_ref, lsem.at[9]),
        "acc": pltpu.make_async_copy(acc_hbm, acc_ref, lsem.at[10]),
        "jg": pltpu.make_async_copy(jg_hbm, jg_ref, lsem.at[11]),
        "lo": pltpu.make_async_copy(lo_hbm, lob, lsem.at[0]),
        "mi": pltpu.make_async_copy(mi_hbm, mib, lsem.at[1]),
        "em": pltpu.make_async_copy(em_hbm, emb, lsem.at[2]),
        "q": pltpu.make_async_copy(q_hbm.at[m, g], rxq.at[m], lsem.at[3]),
        "k": pltpu.make_async_copy(ck_hbm.at[pl.ds(2 * g, 2)], kbuf, lsem.at[4]),
        "v": pltpu.make_async_copy(cv_hbm.at[pl.ds(2 * g, 2)], vbuf, lsem.at[5]),
        "sk": pltpu.make_async_copy(sk_hbm, sk_ref, lsem.at[12]),
        "sv": pltpu.make_async_copy(sv_hbm, sv_ref, lsem.at[13]),
        "ng": pltpu.make_async_copy(ng_hbm, ng_ref, lsem.at[14]),
        "ngn": pltpu.make_async_copy(ngn_hbm, ngn_ref, lsem.at[15]),
        "w": pltpu.make_async_copy(w_hbm, wbuf, lsem.at[6]),
        "m1": pltpu.make_async_copy(m1_hbm, m1buf, lsem.at[7]),
        "m2": pltpu.make_async_copy(m2_hbm, m2buf, lsem.at[8]),
    }
    bar = pltpu.get_barrier_semaphore()

    greeted = [at(mm=peer(j)) for j in range(MP - 1, 0, -1)]
    greeted += [at(dd=z * NY + 1 - y)] if NY == 2 else []
    greeted += [at(dd=zdev(z + 1))] + ([at(dd=zdev(z - 1))] if NZ > 2 else []) + [at(gg=1 - g)]
    for dev in greeted:
        pl.semaphore_signal(bar, inc=1, device_id=dev, device_id_type=MESH)
    for load in loads.values():
        load.start()

    RD = 4 * MP
    loads["cot"].wait()
    loads["acc"].wait()
    ct = cot_ref[...].astype(F32).reshape(RD // 2, 2, 4, cot_ref.shape[2])
    ct = jnp.concatenate([ct[:, 0], ct[:, 1]], axis=1).reshape(MP, 2, SUB, cot_ref.shape[2])
    ct = jnp.concatenate([ct[:, 0], ct[:, 1]], axis=0).reshape(T, cot_ref.shape[2])
    token = lax.broadcasted_iota(jnp.int32, (RD, T), 1)
    quad = token // 4
    part = lax.rem(quad, RD // 2)
    row = (part // 2) * 4 + (quad // (RD // 2)) * 2 + lax.rem(part, 2)
    pick = (lax.broadcasted_iota(jnp.int32, (RD, T), 0) == row).astype(BF16)
    lengths = jnp.broadcast_to(acc_ref[...].astype(F32), (SUB, RD)).astype(BF16)
    taken = jnp.dot(lengths, pick, preferred_element_type=F32)[:1]
    slot = lax.rem(lax.broadcasted_iota(jnp.int32, (1, T), 1), 4)
    weight = jnp.zeros((1, T), F32)
    for s in range(4):
        weight = jnp.where((slot == s) & (taken > s + 0.5), jnp.float32(slot_decay**s), weight)
    csend[...] = (ct.T * weight).astype(BF16)

    sub8 = lax.broadcasted_iota(jnp.int32, (1, SUB, HD), 1) < 4
    loads["jg"].wait()
    for a in range(3):
        for lp in range(LT // 2):
            lower = jg_ref[a : a + 1, 2 * lp * HD : (2 * lp + 1) * HD]
            upper = jg_ref[a : a + 1, (2 * lp + 1) * HD : (2 * lp + 2) * HD]
            gpat[a, lp] = jnp.where(sub8[0], lower, upper)

    def native_block(x):
        return x.astype(F32).reshape(2, LT // 2, SUB, HD)

    def fold(p):
        t = jnp.sum(p, axis=1)
        t = t + swap_halves(t)
        return jnp.where(sub8[0], t[0], t[1])

    loads["lo"].wait()
    loads["mi"].wait()
    loads["em"].wait()
    g0, g1, g2 = gpat[0], gpat[1], gpat[2]

    def stats0(i, c):
        e, l, v = native_block(emb[i, g]), native_block(lob[i, g]), native_block(mib[i, g])
        gl, gv = l * g0, v * g1
        rows = pl.ds(pl.multiple_of(i * SUB, SUB), SUB)
        for n, p in enumerate((e * e, l * l, v * v, gl * gl, gv * gv, gl * gv)):
            zbuf[n, rows, :] = fold(p)
        return c

    lax.fori_loop(0, MP, stats0, 0)

    def row_sums(count):
        total = jnp.zeros((SUB, TH), F32)
        for n in range(count):
            pick = (lax.broadcasted_iota(jnp.int32, (SUB, HD), 0) == n).astype(F32)
            total = total + dot_nt(pick, zbuf[n], precision=lax.Precision.HIGHEST)
        return total

    ssend[0] = row_sums(6)

    def relayout(x):
        x = native_block(x)
        a, b = x[0], x[1]
        return jnp.where(sub8, a, swap_halves(b)), jnp.where(sub8, swap_halves(a), b)

    def relayout_all(n, load, gg):
        def two(i, c):
            parts = [relayout(load(2 * i + h, gg)) for h in range(2)]
            rows = pl.ds(pl.multiple_of(gg * TH + i * 2 * SUB, 2 * SUB), 2 * SUB)
            for lp in range(LT // 2):
                for k in range(2):
                    tile = jnp.concatenate([parts[0][k][lp], parts[1][k][lp]], axis=0)
                    lt = 2 * lp + k
                    vx[n, rows, lt * HD : (lt + 1) * HD] = tile.astype(BF16)
            return c

        lax.fori_loop(0, MP // 2, two, 0)

    for gg in range(2):
        relayout_all(0, lambda i, gg: emb[i, gg], gg)
    loads["w"].wait()
    for i in range(2):
        w = wbuf[pl.ds(i, SH * LT, stride=2), :].astype(BF16).astype(F32)
        w = w.reshape(SH, LT, HD).reshape(SH, F)
        if i == 0:
            w_two[...] = w
        else:
            wz[0, 1] = w.astype(BF16)

    pl.semaphore_wait(bar, len(greeted))

    def q_copy(j):
        dst = peer(j)
        return remote(q_hbm.at[dst, g], rxq.at[m], q_s, q_r.at[ml], at(mm=dst))

    for j in range(MP - 1, 0, -1):
        q_copy(j).start()

    sends_cot = (ml // YH) == g
    mine = lax.rem(ml, YH)

    def c_copy(j):
        to = flipped(ml, y_bits, j) * MX + mx
        return remote(csend, cbuf.at[mx, mine], c_s, c_r.at[mine], at(mm=to))

    @pl.when(sends_cot)
    def _():
        cbuf[mx, mine] = csend[...]
        for j in range(MY - 1, 0, -1):
            c_copy(j).start()

    def c_forward(j):
        to = ml * MX + flipped(mx, x_bits, j)
        return remote(cbuf.at[mx], cbuf.at[mx], c2_s, c2_r, at(mm=to))

    def c_turn():
        for b in range(YH):

            @pl.when((YH * g + b) != ml)
            def _():
                remote(csend, cbuf.at[mx, b], c_s, c_r.at[b], at(mm=(YH * g + b) * MX + mx)).wait_recv()

        for j in range(MX - 1, 0, -1):
            c_forward(j).start()

    def c_end():
        remote(cbuf.at[0 : MX - 1], cbuf.at[0 : MX - 1], c2_s, c2_r, at(mm=peer(1))).wait_recv()

    for j in range(MP - 1, 0, -1):
        remote(ssend.at[0], srecv.at[m], s_s.at[0], s_r.at[0], at(mm=peer(j))).start()
    srecv[m] = ssend[0]

    def s_all():
        some = srecv.at[0 : MP - 1]
        return remote(some, some, s_s.at[0], s_r.at[0], at(mm=peer(1)))

    def red_copy():
        return remote(red.at[0, g], red.at[0, g], red_s, red_r, at(gg=1 - g))

    def w_copy():
        return remote(wz.at[0, 1], wz.at[0, 0], wx_s, wx_r, at(dd=z * NY + 1 - y))

    def wz_copy(way, yo):
        return remote(wz.at[0, yo], wz.at[1 + way, yo], wz_s, wz_r.at[way, yo], at(dd=zdev(z + 1 - 2 * way)))

    for way in range(2):
        wz_copy(way, 1).start()

    for gg in range(2):
        relayout_all(1, lambda i, gg: lob[i, gg], gg)
        relayout_all(2, lambda i, gg: mib[i, gg], gg)

    loads["k"].wait()
    loads["v"].wait()
    loads["q"].wait()
    for key in ("sk", "sv", "ng", "ngn"):
        loads[key].wait()
    CP = 64
    SR = KVH * 4
    QR = 32
    rowi = lax.broadcasted_iota(jnp.int32, (2 * QR, HD), 0)
    coli = lax.broadcasted_iota(jnp.int32, (2 * QR, HD), 1)
    scol = coli - CP
    in_slots = (scol >= 0) & (scol < SR) & (lax.rem(scol, 4) <= lax.rem(rowi, 4))
    slot_head = scol // 4
    pad = jnp.zeros((HD - CP - SR, HD), BF16)
    slot_rows = [pl.ds(pl.multiple_of((2 * g + r) * SR, SR), SR) for r in range(2)]
    cached = [coli < jnp.minimum(len_ref[2 * g + r], CP) for r in range(2)]

    def o_copy(dst):
        return remote(outb.at[dst], topb.at[g, m], o_s, o_r.at[ml], at(mm=dst))

    def attend(k):
        cols = pl.ds(pl.multiple_of(k * HD, HD), HD)
        for r in range(2):
            qrows = slice(r * QR, (r + 1) * QR)
            qk = jnp.concatenate([rxq[2 * k, qrows, :], rxq[2 * k + 1, qrows, :]], axis=0)
            keys = jnp.concatenate([kbuf[r, :, cols], sk_ref[slot_rows[r], :], pad], axis=0)
            vals = jnp.concatenate([vbuf[r, :, cols], sv_ref[slot_rows[r], :], pad], axis=0)
            live = cached[r] | (in_slots & (slot_head == k))
            s = dot_nt(qk, keys) * (HD**-0.5)
            s = jnp.where(live, s, -1e30)
            top = jnp.max(s, axis=-1, keepdims=True)
            e = jnp.exp(s - top)
            p = (e * (1.0 / jnp.sum(e, axis=-1, keepdims=True))).astype(BF16)
            o = jnp.dot(p, vals, preferred_element_type=F32).astype(BF16)
            yield 2 * k, qrows, o[:QR]
            yield 2 * k + 1, qrows, o[QR:]

    for jy in range(MY):
        yl = flipped(ml, y_bits, jy)
        count = MX - 1 if jy == 0 else MX
        some = rxq.at[0:count]
        remote(some, some, q_s, q_r.at[yl], at(mm=peer(1))).wait_recv()
        if jy == 1 and NY == 2:
            w_copy().start()
        done = []
        for h in range(MX // 2):
            done += list(attend(yl * (MX // 2) + h))
        for dst, qrows, o in done:
            outb[dst, qrows, :] = o
        for jx in range(MX):
            if jx or jy:
                o_copy(yl * MX + flipped(mx, x_bits, jx)).start()
        if jy == min(1, MY - 1):
            c_turn()
    topb[g, m] = outb[m]

    s_all().wait_recv()
    red[0, g] = jnp.sum(srecv[...], axis=0)
    red_copy().start()

    c_end()
    remote(red.at[0, g], red.at[0, 1 - g], red_s, red_r, at(gg=1 - g)).wait_recv()

    def sums(ph, n):
        return jnp.concatenate([red[ph, 0, n : n + 1, :], red[ph, 1, n : n + 1, :]], axis=1)

    def inv(total):
        return lax.rsqrt(total * (1.0 / D) + EPS)

    CW = HC // (YH * MX)

    def scale_cot(n, row):
        for b in range(YH):
            for x in range(MX):
                scaled = (cbuf[x, b].astype(F32) * row).astype(BF16)
                for yy in range(NY):
                    ax[n, yy, b * MX + x] = scaled[yy * SH : (yy + 1) * SH]

    scale = (2.0 * D) ** -0.5

    def tile(i, yy, ch, terms):
        for h in range(2):
            cols = slice(ch * FH + h * FH // 2, ch * FH + (h + 1) * FH // 2)
            total = None
            for n_x, gain in terms:
                part = jnp.dot(
                    ax[n_x, yy].reshape(NZ * SH, T), vx[n_x, :, cols], preferred_element_type=F32
                )
                if gain is not None:
                    part = part * jg_ref[gain : gain + 1, cols]
                total = part if total is None else total + part
            total = (total * (ng_ref[i : i + 1, cols] * scale)).astype(BF16)
            tb[i, yy, ch, :, :, h * FH // 2 : (h + 1) * FH // 2] = total.reshape(NZ, SH, FH // 2)

    CHUNKS = [q for q in range(NQ) if NY == 2 or q >= 2]

    def y_of(q):
        return 1 - y if q < 2 else y

    def length(way, q):
        return H if (way == 0) == (q % 2 == 0) else H - 1

    def term(i, q, zz):
        return tb.at[i, y_of(q), q % 2, lax.rem(zz + NZ, NZ)]

    def ring_copy(i, way, q, s):
        step = 1 if way == 0 else -1
        src = term(i, q, z + step * length(way, q)) if s == 1 else sring.at[i, way, q, s - 2]
        return remote(
            src, rring.at[i, way, q, s - 1], ring_s.at[i, int(s == H)], ring_r.at[i, way, q, s - 1],
            at(dd=zdev(z + step)),
        )

    gain_terms = [[], []]

    def gain_term(q, t, place):
        ch = q % 2
        part = t * wz[place, q // 2, :, ch * FH : (ch + 1) * FH].astype(F32)
        gain_terms[ch].append(jnp.sum(part.reshape(SH // SUB, SUB, FH), axis=0))

    def ring_step(i, s, q):
        for way in range(2):
            n = length(way, q)
            if s > n:
                continue
            if s > 1:
                ring_copy(i, way, q, s - 1).wait_recv()
                step = 1 if way == 0 else -1
                own = term(i, q, z + step * (n + 1 - s))[...].astype(F32)
                t = own + rring[i, way, q, s - 2].astype(F32)
                sring[i, way, q, s - 2] = t.astype(BF16)
            ring_copy(i, way, q, s).start()
            if i == 1 and s == n:
                if s == 1:
                    step = 1 if way == 0 else -1
                    t = term(i, q, z + step)[...].astype(F32)
                gain_term(q, t, 2 - way)

    def ring_steps(i, s):
        for q in CHUNKS:
            ring_step(i, s, q)

    def ring_sent(i):
        ways = len(CHUNKS) // 2
        if H > 1:
            some = rring.at[i, :, 0 : len(CHUNKS), 0 : H - 1]
            remote(some, some, ring_s.at[i, 0], ring_r.at[i, 0, 0, 0], at(dd=zdev(z + 1))).wait_send()
        some = rring.at[i, :, 0:ways, 0]
        remote(some, some, ring_s.at[i, 1], ring_r.at[i, 0, 0, 0], at(dd=zdev(z + 1))).wait_send()

    def gradient(i, terms):
        for q in CHUNKS:
            tile(i, y_of(q), q % 2, terms)
            ring_step(i, 1, q)

    def y_copy(i, ch):
        return remote(sy.at[i, ch], ry.at[i, ch], y_s.at[i], y_r.at[i, ch], at(dd=z * NY + 1 - y))

    def y_sent(i):
        remote(sy.at[i], ry.at[i], y_s.at[i], y_r.at[i, 0], at(dd=z * NY + 1 - y)).wait_send()

    def ring_end(i):
        for q in CHUNKS:
            ch = q % 2
            t = term(i, q, z)[...].astype(F32)
            for way in range(2):
                n = length(way, q)
                if n > 0:
                    ring_copy(i, way, q, n).wait_recv()
                    t = t + rring[i, way, q, n - 1].astype(F32)
            if q < 2:
                sy[i, ch] = t.astype(BF16)
                y_copy(i, ch).start()
            else:
                own_t[i, :, ch * FH : (ch + 1) * FH] = t

    def grad_end(i):
        if NY == 2:
            for ch in range(2):
                cols = slice(ch * FH, (ch + 1) * FH)
                y_copy(i, ch).wait_recv()
                own_t[i, :, cols] = own_t[i, :, cols] + ry[i, ch].astype(F32)

    def g_copy(j):
        return remote(gsend, grecv.at[d], g_s, g_r, at(dd=dpeer(j)))

    def gain_send():
        ones = [jnp.sum(own_t[0] * w_two[...], axis=0, keepdims=True)]
        ones.append(
            jnp.concatenate([jnp.sum(sum(parts), axis=0, keepdims=True) for parts in gain_terms], axis=1)
        )
        tiles = []
        for i in range(2):
            row = jnp.concatenate([ones[i][:, t * HD : (t + 1) * HD] for t in range(LT)], axis=0)
            tiles.append(row / ngn_ref[pl.ds(i, LT, stride=2), :])
        gsend[...] = jnp.concatenate(tiles, axis=0).astype(BF16)
        for j in range(DP - 1, 0, -1):
            g_copy(j).start()
        grecv[d] = gsend[...]

    def g_all():
        some = grecv.at[0 : DP - 1]
        return remote(some, some, g_s, g_r, at(dd=dpeer(1)))

    def adam(i):
        rows = pl.ds(i, SH * LT, stride=2)
        grad = own_t[i].reshape(SH, LT, HD).reshape(SH * LT, HD)
        w = wbuf[rows, :]
        a = first_beta * m1buf[rows, :] + (1.0 - first_beta) * grad
        b = second_beta * m2buf[rows, :] + (1.0 - second_beta) * grad * grad
        m1_out[rows, :] = a
        m2_out[rows, :] = b
        ca = a * (1.0 / (1.0 - first_beta**adam_steps))
        cb = b * (1.0 / (1.0 - second_beta**adam_steps))
        w_out[rows, :] = w - learn_rate * (ca / (jnp.sqrt(cb) + 1e-08) + decay_rate * w)

    scale_cot(0, inv(sums(0, 0)))
    gradient(0, ((0, None),))

    for jy in range(MY):
        yl = flipped(ml, y_bits, jy)
        some = topb.at[0, 0 : MX - 1 if jy == 0 else MX]
        remote(some, some, o_s, o_r.at[yl], at(mm=peer(1))).wait_recv()

        def stats1(x, c):
            i = yl * MX + x
            l, v, t = native_block(lob[i, g]), native_block(mib[i, g]), native_block(topb[g, i])
            gl, gv, gt = l * g0, v * g1, t * g2
            rows = pl.ds(pl.multiple_of(i * SUB, SUB), SUB)
            for n, p in enumerate((t * t, gt * gt, gl * gt, gv * gt)):
                zbuf[n, rows, :] = fold(p)
            return c

        lax.fori_loop(0, MX, stats1, 0, unroll=2)
    ssend[1] = row_sums(4)
    def s2_copy(gg, j):
        return remote(ssend.at[1], srecv2.at[g * MP + m], s_s.at[1], s_r.at[1], at(gg=gg, mm=peer(j)))

    def s2_all():
        some = srecv2.at[0 : 2 * MP - 1]
        return remote(some, some, s_s.at[1], s_r.at[1], at(mm=peer(1)))

    for j in range(MP - 1, -1, -1):
        if j:
            s2_copy(g, j).start()
        s2_copy(1 - g, j).start()
    srecv2[g * MP + m] = ssend[1]
    top_copy = remote(topb.at[g], topb.at[g], top_s, top_r, at(gg=1 - g))
    top_copy.start()
    relayout_all(3, lambda i, gg: topb[gg, i], g)
    if H >= 2:
        ring_steps(0, 2)
    if NY == 2:
        w_copy().wait_recv()
        for way in range(2):
            wz_copy(way, 0).start()
    remote(topb.at[g], topb.at[1 - g], top_s, top_r, at(gg=1 - g)).wait_recv()
    relayout_all(3, lambda i, gg: topb[gg, i], 1 - g)

    def sent(block, count, sem, r):
        some = block.at[0:count]
        remote(some, some, sem, r, at(mm=peer(1))).wait_send()

    if H >= 3:
        ring_steps(0, 3)
    sent(rxq, MP - 1, q_s, q_r.at[0])
    sent(outb, MP - 1, o_s, o_r.at[0])
    s_all().wait_send()
    sent(cbuf, MX - 1, c2_s, c2_r)

    @pl.when(sends_cot)
    def _():
        some = ax.at[0, 0, 0 : (MY - 1) * CW // SH]
        remote(some, some, c_s, c_r.at[0], at(mm=peer(1))).wait_send()

    s2_all().wait_recv()
    for gg in range(2):
        red[1, gg] = jnp.sum(srecv2[gg * MP : (gg + 1) * MP], axis=0)

    rl, rv, rt = inv(sums(0, 1)), inv(sums(0, 2)), inv(sums(1, 0))
    joined = (
        rl * rl * sums(0, 3)
        + rv * rv * sums(0, 4)
        + rt * rt * sums(1, 1)
        + 2.0 * (rl * rv * sums(0, 5) + rl * rt * sums(1, 2) + rv * rt * sums(1, 3))
    )
    rj = inv(jnp.maximum(joined, 0.0))
    scale_cot(1, rl * rj)
    scale_cot(2, rv * rj)
    scale_cot(3, rt * rj)
    for way in range(2):
        for yo in range(2 - NY, 2):
            wz_copy(way, yo).wait_recv()
    gradient(1, ((1, 0), (2, 1), (3, 2)))

    if H >= 4:
        ring_steps(0, 4)
    if H >= 2:
        ring_steps(1, 2)
    ring_end(0)
    if H >= 3:
        ring_steps(1, 3)
    for q in CHUNKS:
        gain_term(q, term(1, q, z)[...].astype(F32), 0)
    if H >= 4:
        ring_steps(1, 4)
    loads["m1"].wait()
    loads["m2"].wait()
    grad_end(0)
    gain_send()
    adam(0)
    ring_end(1)
    grad_end(1)
    adam(1)

    s2_all().wait_send()
    red_copy().wait_send()
    top_copy.wait_send()
    for i in range(2):
        ring_sent(i)
        if NY == 2:
            y_sent(i)
    if NY == 2:
        w_copy().wait_send()
    for way in range(2):
        for yo in range(2 - NY, 2):
            wz_copy(way, yo).wait_send()

    g_all().wait_recv()
    gsib_s[...] = jnp.sum(grecv[...].astype(F32), axis=0)
    g_pair = remote(gsib_s, gsib_r, gx_s, gx_r, at(gg=1 - g))
    g_pair.start()
    g_all().wait_send()
    g_pair.wait_recv()
    total = gsib_s[...] + gsib_r[...]
    for i in range(2):
        gain_out[pl.ds(i, LT, stride=2), :] = total[i * LT : (i + 1) * LT]
    g_pair.wait_send()


def hand_on(*refs):
    n = len(refs) // 2
    sems = refs[-1]
    copies = [pltpu.make_async_copy(refs[i], refs[n + i], sems.at[i]) for i in range(n)]
    for copy in copies:
        copy.start()
    for copy in copies:
        copy.wait()


def shards(
    NZ, NY, MP,
    queries, cache_keys, cache_values, slot_keys, slot_values, cache_lengths,
    embeddings, layer_low, layer_mid, accepted, join_gain, norm_gain,
    key_cotangent, key_weight, moment_first, moment_second,
):
    rows, slots, F = embeddings.shape
    D = F * MP
    KW = cache_keys.shape[2]
    KVH = KW // HD
    SH = key_weight.shape[0]
    HC = SH * NZ * NY
    T = rows * slots
    TH = T // 2
    LT = F // HD
    H = NZ // 2
    MX = 4 if MP == 16 else 2
    YH = MP // MX // 2
    cols = key_cotangent.shape[2]
    DP = NZ * NY
    FH = F // 2

    def tokens(x):
        return native(x).reshape(MP, 2, 2 * LT * slots, HD)

    hbm = pl.BlockSpec(memory_space=pl.ANY)
    vmem = pl.BlockSpec(memory_space=pltpu.VMEM)
    smem = pl.BlockSpec(memory_space=pltpu.SMEM)
    dma = pltpu.SemaphoreType.DMA
    B = 2 * LT * slots
    shape = jax.ShapeDtypeStruct
    outs = pl.pallas_call(
        functools.partial(kernel, (NZ, NY, MP, MX, KVH, F, D, HC, SH)),
        out_shape=(
            pltpu.VMEM((SH * 2 * LT, HD), F32),
            pltpu.VMEM((SH * 2 * LT, HD), F32),
            pltpu.VMEM((SH * 2 * LT, HD), F32),
            pltpu.VMEM((2 * LT, HD), F32),
        ),
        in_specs=[hbm] * 5 + [smem] + [hbm] * 11,
        out_specs=(vmem, vmem, vmem, vmem),
        scratch_shapes=[
            pltpu.VMEM((KVH * 16, HD), BF16),
            pltpu.VMEM((KVH * 16, HD), BF16),
            pltpu.VMEM(key_cotangent.shape, BF16),
            pltpu.VMEM((1, rows), jnp.int32),
            pltpu.VMEM((3, F), F32),
            pltpu.VMEM((2, F), F32),
            pltpu.VMEM((2 * LT, HD), F32),
            pltpu.VMEM((MP, B, HD), BF16),
            pltpu.VMEM((2, 64, KW), BF16),
            pltpu.VMEM((2, 64, KW), BF16),
            pltpu.VMEM((MP, B, HD), BF16),
            pltpu.VMEM((MP, 2, B, HD), BF16),
            pltpu.VMEM((MP, 2, B, HD), BF16),
            pltpu.VMEM((MP, 2, B, HD), BF16),
            pltpu.VMEM((2, MP, B, HD), BF16),
            pltpu.VMEM((cols, T), BF16),
            pltpu.VMEM((MX, YH, cols, T), BF16),
            pltpu.VMEM((SH * 2 * LT, HD), F32),
            pltpu.VMEM((SH * 2 * LT, HD), F32),
            pltpu.VMEM((SH * 2 * LT, HD), F32),
            pltpu.VMEM((3, LT // 2, SUB, HD), F32),
            pltpu.VMEM((SUB, TH, HD), F32),
            pltpu.VMEM((2, SUB, TH), F32),
            pltpu.VMEM((MP, SUB, TH), F32),
            pltpu.VMEM((2 * MP, SUB, TH), F32),
            pltpu.VMEM((2, 2, SUB, TH), F32),
            pltpu.VMEM((4, T, F), BF16),
            pltpu.VMEM((4, NY, NZ, SH, T), BF16),
            pltpu.VMEM((2, NY, 2, NZ, SH, FH), BF16),
            pltpu.VMEM((2, 2, NQ, max(H - 1, 1), SH, FH), BF16),
            pltpu.VMEM((2, 2, NQ, H, SH, FH), BF16),
            pltpu.VMEM((2, 2, SH, FH), BF16),
            pltpu.VMEM((2, 2, SH, FH), BF16),
            pltpu.VMEM((2, SH, F), F32),
            pltpu.VMEM((SH, F), F32),
            pltpu.VMEM((3, 2, SH, F), BF16),
            pltpu.VMEM((2 * LT, HD), BF16),
            pltpu.VMEM((DP, 2 * LT, HD), BF16),
            pltpu.VMEM((2 * LT, HD), F32),
            pltpu.VMEM((2 * LT, HD), F32),
            dma((16,)),
            dma, dma((MP // MX,)),
            dma, dma((YH,)), dma, dma,
            dma, dma((MP // MX,)),
            dma((2,)), dma((2,)),
            dma, dma,
            dma, dma,
            dma((2, 2)), dma((2, 2, NQ, H)),
            dma((2,)), dma((2, 2)),
            dma, dma,
            dma, dma((2, 2)),
            dma, dma,
            dma, dma,
        ],
        compiler_params=pltpu.CompilerParams(
            collective_id=0, has_side_effects=True, vmem_limit_bytes=VMEM_BYTES
        ),
        cost_estimate=pl.CostEstimate(
            flops=2 * 4 * HC * T * F, bytes_accessed=6 * 1024 * 1024, transcendentals=0
        ),
        name="draft_step",
    )(
        tokens(queries), cache_keys, cache_values, native(slot_keys), native(slot_values), cache_lengths,
        tokens(embeddings), tokens(layer_low), tokens(layer_mid), key_cotangent, accepted[None],
        join_gain, norm_gain, native(norm_gain[None]),
        native(key_weight), native(moment_first), native(moment_second),
    )
    outs = pl.pallas_call(
        hand_on,
        out_shape=[shape(x.shape, x.dtype) for x in outs],
        in_specs=[vmem] * 4,
        out_specs=[hbm] * 4,
        scratch_shapes=[dma((4,))],
        compiler_params=pltpu.CompilerParams(vmem_limit_bytes=VMEM_BYTES // 8),
        name="hand_on",
    )(*outs)
    new = [from_native(x, SH, 2, F) for x in outs[:3]]
    return (*new, from_native(outs[3], 1, 2, F)[0])


def solution(mesh, NY=2):
    NZ, MP = mesh.shape["dp"] // NY, mesh.shape["mp"]
    tokens, owners, moments = P("dp", None, "mp"), P(("dp", "mp"), None, None), P(("group", "dp"), None, "mp")
    return jax.shard_map(
        functools.partial(shards, NZ, NY, MP),
        mesh=mesh,
        in_specs=(
            tokens, owners, owners, owners, owners, P(("dp", "mp")), tokens, tokens, tokens, P("dp"),
            P(None, "mp"), P(None, "mp"), tokens, moments, moments, moments,
        ),
        out_specs=(moments, moments, moments, P(None, "mp")),
        check_vma=False,
    )
```

```python
import functools

import jax
import jax.numpy as jnp
from jax import lax
from jax.experimental import pallas as pl
from jax.experimental.pallas import tpu as pltpu
from jax.sharding import PartitionSpec as P

HD = 128
SUB = 8
VMEM_BYTES = 62 * 1024 * 1024
NQ = 4
EPS = 1e-05
first_beta = 0.9
second_beta = 0.95
learn_rate = 0.05
decay_rate = 0.1
adam_steps = 3
slot_decay = 0.8
MESH = pl.DeviceIdType.MESH
F32 = jnp.float32
BF16 = jnp.bfloat16


def native(x):
    rows, slots, width = x.shape
    x = x.reshape(rows, slots, width // HD, HD).transpose(0, 2, 1, 3)
    return x.reshape(rows * (width // HD) * slots, HD)


def from_native(y, rows, slots, width):
    y = y.reshape(rows, width // HD, slots, HD).transpose(0, 2, 1, 3)
    return y.reshape(rows, slots, width)


def dot_nt(a, b, **kw):
    return lax.dot_general(a, b, (((1,), (1,)), ((), ())), preferred_element_type=F32, **kw)


def swap_halves(x):
    return jnp.concatenate([x[:, 4:], x[:, :4]], axis=1)


def kernel(
    dims,
    q_hbm, ck_hbm, cv_hbm, sk_hbm, sv_hbm, len_ref, em_hbm, lo_hbm, mi_hbm, cot_hbm, acc_hbm,
    jg_hbm, ng_hbm, ngn_hbm, w_hbm, m1_hbm, m2_hbm,
    w_out, m1_out, m2_out, gain_out,
    sk_ref, sv_ref, cot_ref, acc_ref, jg_ref, ng_ref, ngn_ref, rxq, kbuf, vbuf, outb, emb, lob, mib, topb, csend, cbuf, wbuf, m1buf, m2buf,
    gpat, zbuf, ssend, srecv, srecv2, red, vx, ax, tb, sring, rring, sy, ry, own_t,
    w_two, wz, gsend, grecv, gsib_s, gsib_r,
    lsem, q_s, q_r, c_s, c_r, c2_s, c2_r, o_s, o_r, s_s, s_r, red_s, red_r, top_s, top_r,
    ring_s, ring_r, y_s, y_r, wx_s, wx_r, wz_s, wz_r, g_s, g_r, gx_s, gx_r,
):
    NZ, NY, MP, MX, KVH, F, D, HC, SH = dims
    MY = MP // MX
    YH = MY // 2
    LT = F // HD
    T = MP * 4 * SUB // 2
    TH = T // 2
    H = NZ // 2
    DP = NZ * NY
    FH = F // 2
    g = lax.axis_index("group")
    d = lax.axis_index("dp")
    m = lax.axis_index("mp")
    z, y = d // NY, lax.rem(d, NY)
    ml, mx = m // MX, lax.rem(m, MX)

    def at(gg=None, dd=None, mm=None):
        return (g if gg is None else gg, d if dd is None else dd, m if mm is None else mm)

    def zdev(zz):
        return lax.rem(zz + NZ, NZ) * NY + y

    def remote(src, dst, s, r, dev):
        return pltpu.make_async_remote_copy(
            src_ref=src, dst_ref=dst, send_sem=s, recv_sem=r, device_id=dev, device_id_type=MESH
        )

    def flips(a, n):
        return [(b, b * (1 - 2 * lax.rem(a // b, 2))) for b in (1, 2, 4, 8) if b < n]

    def flipped(a, bits, j):
        for b, delta in bits:
            if j & b:
                a = a + delta
        return a

    m_bits, d_bits, x_bits, y_bits = flips(m, MP), flips(d, DP), flips(mx, MX), flips(ml, MY)

    def peer(j):
        return flipped(m, m_bits, j)

    def dpeer(j):
        return flipped(d, d_bits, j)

    loads = {
        "cot": pltpu.make_async_copy(cot_hbm, cot_ref, lsem.at[9]),
        "acc": pltpu.make_async_copy(acc_hbm, acc_ref, lsem.at[10]),
        "jg": pltpu.make_async_copy(jg_hbm, jg_ref, lsem.at[11]),
        "lo": pltpu.make_async_copy(lo_hbm, lob, lsem.at[0]),
        "mi": pltpu.make_async_copy(mi_hbm, mib, lsem.at[1]),
        "em": pltpu.make_async_copy(em_hbm, emb, lsem.at[2]),
        "q": pltpu.make_async_copy(q_hbm.at[m, g], rxq.at[m], lsem.at[3]),
        "k": pltpu.make_async_copy(ck_hbm.at[pl.ds(2 * g, 2)], kbuf, lsem.at[4]),
        "v": pltpu.make_async_copy(cv_hbm.at[pl.ds(2 * g, 2)], vbuf, lsem.at[5]),
        "sk": pltpu.make_async_copy(sk_hbm, sk_ref, lsem.at[12]),
        "sv": pltpu.make_async_copy(sv_hbm, sv_ref, lsem.at[13]),
        "ng": pltpu.make_async_copy(ng_hbm, ng_ref, lsem.at[14]),
        "ngn": pltpu.make_async_copy(ngn_hbm, ngn_ref, lsem.at[15]),
        "w": pltpu.make_async_copy(w_hbm, wbuf, lsem.at[6]),
        "m1": pltpu.make_async_copy(m1_hbm, m1buf, lsem.at[7]),
        "m2": pltpu.make_async_copy(m2_hbm, m2buf, lsem.at[8]),
    }
    bar = pltpu.get_barrier_semaphore()

    greeted = [at(mm=peer(j)) for j in range(MP - 1, 0, -1)]
    greeted += [at(dd=z * NY + 1 - y)] if NY == 2 else []
    greeted += [at(dd=zdev(z + 1))] + ([at(dd=zdev(z - 1))] if NZ > 2 else []) + [at(gg=1 - g)]
    for dev in greeted:
        pl.semaphore_signal(bar, inc=1, device_id=dev, device_id_type=MESH)
    for load in loads.values():
        load.start()

    RD = 4 * MP
    loads["cot"].wait()
    loads["acc"].wait()
    ct = cot_ref[...].astype(F32).reshape(RD // 2, 2, 4, cot_ref.shape[2])
    ct = jnp.concatenate([ct[:, 0], ct[:, 1]], axis=1).reshape(MP, 2, SUB, cot_ref.shape[2])
    ct = jnp.concatenate([ct[:, 0], ct[:, 1]], axis=0).reshape(T, cot_ref.shape[2])
    token = lax.broadcasted_iota(jnp.int32, (RD, T), 1)
    quad = token // 4
    part = lax.rem(quad, RD // 2)
    row = (part // 2) * 4 + (quad // (RD // 2)) * 2 + lax.rem(part, 2)
    pick = (lax.broadcasted_iota(jnp.int32, (RD, T), 0) == row).astype(BF16)
    lengths = jnp.broadcast_to(acc_ref[...].astype(F32), (SUB, RD)).astype(BF16)
    taken = jnp.dot(lengths, pick, preferred_element_type=F32)[:1]
    slot = lax.rem(lax.broadcasted_iota(jnp.int32, (1, T), 1), 4)
    weight = jnp.zeros((1, T), F32)
    for s in range(4):
        weight = jnp.where((slot == s) & (taken > s + 0.5), jnp.float32(slot_decay**s), weight)
    csend[...] = (ct.T * weight).astype(BF16)

    sub8 = lax.broadcasted_iota(jnp.int32, (1, SUB, HD), 1) < 4
    loads["jg"].wait()
    for a in range(3):
        for lp in range(LT // 2):
            lower = jg_ref[a : a + 1, 2 * lp * HD : (2 * lp + 1) * HD]
            upper = jg_ref[a : a + 1, (2 * lp + 1) * HD : (2 * lp + 2) * HD]
            gpat[a, lp] = jnp.where(sub8[0], lower, upper)

    def native_block(x):
        return x.astype(F32).reshape(2, LT // 2, SUB, HD)

    def fold(p):
        t = jnp.sum(p, axis=1)
        t = t + swap_halves(t)
        return jnp.where(sub8[0], t[0], t[1])

    loads["lo"].wait()
    loads["mi"].wait()
    loads["em"].wait()
    g0, g1, g2 = gpat[0], gpat[1], gpat[2]

    def stats0(i, c):
        e, l, v = native_block(emb[i, g]), native_block(lob[i, g]), native_block(mib[i, g])
        gl, gv = l * g0, v * g1
        rows = pl.ds(pl.multiple_of(i * SUB, SUB), SUB)
        for n, p in enumerate((e * e, l * l, v * v, gl * gl, gv * gv, gl * gv)):
            zbuf[n, rows, :] = fold(p)
        return c

    lax.fori_loop(0, MP, stats0, 0)

    def row_sums(count):
        total = jnp.zeros((SUB, TH), F32)
        for n in range(count):
            pick = (lax.broadcasted_iota(jnp.int32, (SUB, HD), 0) == n).astype(F32)
            total = total + dot_nt(pick, zbuf[n], precision=lax.Precision.HIGHEST)
        return total

    ssend[0] = row_sums(6)

    def relayout(x):
        x = native_block(x)
        a, b = x[0], x[1]
        return jnp.where(sub8, a, swap_halves(b)), jnp.where(sub8, swap_halves(a), b)

    def relayout_all(n, load, gg):
        def two(i, c):
            parts = [relayout(load(2 * i + h, gg)) for h in range(2)]
            rows = pl.ds(pl.multiple_of(gg * TH + i * 2 * SUB, 2 * SUB), 2 * SUB)
            for lp in range(LT // 2):
                for k in range(2):
                    tile = jnp.concatenate([parts[0][k][lp], parts[1][k][lp]], axis=0)
                    lt = 2 * lp + k
                    vx[n, rows, lt * HD : (lt + 1) * HD] = tile.astype(BF16)
            return c

        lax.fori_loop(0, MP // 2, two, 0)

    for gg in range(2):
        relayout_all(0, lambda i, gg: emb[i, gg], gg)
    loads["w"].wait()
    for i in range(2):
        w = wbuf[pl.ds(i, SH * LT, stride=2), :].astype(BF16).astype(F32)
        w = w.reshape(SH, LT, HD).reshape(SH, F)
        if i == 0:
            w_two[...] = w
        else:
            wz[1] = w.astype(BF16)

    pl.semaphore_wait(bar, len(greeted))

    def q_copy(j):
        dst = peer(j)
        return remote(q_hbm.at[dst, g], rxq.at[m], q_s, q_r.at[ml], at(mm=dst))

    for j in range(MP - 1, 0, -1):
        q_copy(j).start()

    sends_cot = (ml // YH) == g
    mine = lax.rem(ml, YH)

    def c_copy(j):
        to = flipped(ml, y_bits, j) * MX + mx
        return remote(csend, cbuf.at[mx, mine], c_s, c_r.at[mine], at(mm=to))

    @pl.when(sends_cot)
    def _():
        cbuf[mx, mine] = csend[...]
        for j in range(MY - 1, 0, -1):
            c_copy(j).start()

    def c_forward(j):
        to = ml * MX + flipped(mx, x_bits, j)
        return remote(cbuf.at[mx], cbuf.at[mx], c2_s, c2_r, at(mm=to))

    def c_turn():
        for b in range(YH):

            @pl.when((YH * g + b) != ml)
            def _():
                remote(csend, cbuf.at[mx, b], c_s, c_r.at[b], at(mm=(YH * g + b) * MX + mx)).wait_recv()

        for j in range(MX - 1, 0, -1):
            c_forward(j).start()

    def c_end():
        remote(cbuf.at[0 : MX - 1], cbuf.at[0 : MX - 1], c2_s, c2_r, at(mm=peer(1))).wait_recv()

    for j in range(MP - 1, 0, -1):
        remote(ssend.at[0], srecv.at[m], s_s.at[0], s_r.at[0], at(mm=peer(j))).start()
    srecv[m] = ssend[0]

    def s_all():
        some = srecv.at[0 : MP - 1]
        return remote(some, some, s_s.at[0], s_r.at[0], at(mm=peer(1)))

    def red_copy():
        return remote(red.at[0, g], red.at[0, g], red_s, red_r, at(gg=1 - g))

    def w_copy():
        return remote(wz.at[1], wz.at[0], wx_s, wx_r, at(dd=z * NY + 1 - y))

    def wz_copy(way):
        return remote(wz.at[1], wz.at[2 + way], wz_s, wz_r.at[way], at(dd=zdev(z + 1 - 2 * way)))

    for way in range(2):
        wz_copy(way).start()

    for gg in range(2):
        relayout_all(1, lambda i, gg: lob[i, gg], gg)
        relayout_all(2, lambda i, gg: mib[i, gg], gg)

    loads["k"].wait()
    loads["v"].wait()
    loads["q"].wait()
    for key in ("sk", "sv", "ng", "ngn"):
        loads[key].wait()
    CP = 64
    SR = KVH * 4
    QR = 32
    rowi = lax.broadcasted_iota(jnp.int32, (2 * QR, HD), 0)
    coli = lax.broadcasted_iota(jnp.int32, (2 * QR, HD), 1)
    scol = coli - CP
    in_slots = (scol >= 0) & (scol < SR) & (lax.rem(scol, 4) <= lax.rem(rowi, 4))
    slot_head = scol // 4
    pad = jnp.zeros((HD - CP - SR, HD), BF16)
    slot_rows = [pl.ds(pl.multiple_of((2 * g + r) * SR, SR), SR) for r in range(2)]
    cached = [coli < jnp.minimum(len_ref[2 * g + r], CP) for r in range(2)]

    def o_copy(dst):
        return remote(outb.at[dst], topb.at[g, m], o_s, o_r.at[ml], at(mm=dst))

    def attend(k):
        cols = pl.ds(pl.multiple_of(k * HD, HD), HD)
        for r in range(2):
            qrows = slice(r * QR, (r + 1) * QR)
            qk = jnp.concatenate([rxq[2 * k, qrows, :], rxq[2 * k + 1, qrows, :]], axis=0)
            keys = jnp.concatenate([kbuf[r, :, cols], sk_ref[slot_rows[r], :], pad], axis=0)
            vals = jnp.concatenate([vbuf[r, :, cols], sv_ref[slot_rows[r], :], pad], axis=0)
            live = cached[r] | (in_slots & (slot_head == k))
            s = dot_nt(qk, keys) * (HD**-0.5)
            s = jnp.where(live, s, -1e30)
            top = jnp.max(s, axis=-1, keepdims=True)
            e = jnp.exp(s - top)
            p = (e * (1.0 / jnp.sum(e, axis=-1, keepdims=True))).astype(BF16)
            o = jnp.dot(p, vals, preferred_element_type=F32).astype(BF16)
            yield 2 * k, qrows, o[:QR]
            yield 2 * k + 1, qrows, o[QR:]

    for jy in range(MY):
        yl = flipped(ml, y_bits, jy)
        count = MX - 1 if jy == 0 else MX
        some = rxq.at[0:count]
        remote(some, some, q_s, q_r.at[yl], at(mm=peer(1))).wait_recv()
        done = []
        for h in range(MX // 2):
            done += list(attend(yl * (MX // 2) + h))
        for dst, qrows, o in done:
            outb[dst, qrows, :] = o
        for jx in range(MX):
            if jx or jy:
                o_copy(yl * MX + flipped(mx, x_bits, jx)).start()
        if jy == min(1, MY - 1):
            c_turn()
    topb[g, m] = outb[m]

    s_all().wait_recv()
    red[0, g] = jnp.sum(srecv[...], axis=0)
    red_copy().start()

    c_end()
    remote(red.at[0, g], red.at[0, 1 - g], red_s, red_r, at(gg=1 - g)).wait_recv()

    def sums(ph, n):
        return jnp.concatenate([red[ph, 0, n : n + 1, :], red[ph, 1, n : n + 1, :]], axis=1)

    def inv(total):
        return lax.rsqrt(total * (1.0 / D) + EPS)

    CW = HC // (YH * MX)

    def scale_cot(n, row, yy):
        here = pl.ds(pl.multiple_of(yy * SH, SH), SH)
        for b in range(YH):
            for x in range(MX):
                ax[n, yy, b * MX + x] = (cbuf[x, b, here, :].astype(F32) * row).astype(BF16)

    scale = (2.0 * D) ** -0.5

    def tile(i, yy, ch, terms):
        for h in range(2):
            cols = slice(ch * FH + h * FH // 2, ch * FH + (h + 1) * FH // 2)
            total = None
            for n_x, gain in terms:
                part = jnp.dot(
                    ax[n_x, yy].reshape(NZ * SH, T), vx[n_x, :, cols], preferred_element_type=F32
                )
                if gain is not None:
                    part = part * jg_ref[gain : gain + 1, cols]
                total = part if total is None else total + part
            total = (total * (ng_ref[i : i + 1, cols] * scale)).astype(BF16)
            tb[i, yy, ch, :, :, h * FH // 2 : (h + 1) * FH // 2] = total.reshape(NZ, SH, FH // 2)

    CHUNKS = [q for q in range(NQ) if NY == 2 or q >= 2]

    def y_of(q):
        return 1 - y if q < 2 else y

    def length(way, q):
        return H if (way == 0) == (q % 2 == 0) else H - 1

    def term(i, q, zz):
        return tb.at[i, y_of(q), q % 2, lax.rem(zz + NZ, NZ)]

    def ring_copy(i, way, q, s):
        step = 1 if way == 0 else -1
        src = term(i, q, z + step * length(way, q)) if s == 1 else sring.at[i, way, q, s - 2]
        return remote(
            src, rring.at[i, way, q, s - 1], ring_s.at[i, int(s == H)], ring_r.at[i, way, q, s - 1],
            at(dd=zdev(z + step)),
        )

    gain_terms = [[], []]

    def gain_term(q, t, place):
        ch = q % 2
        part = t * wz[place, :, ch * FH : (ch + 1) * FH].astype(F32)
        gain_terms[ch].append(jnp.sum(part.reshape(SH // SUB, SUB, FH), axis=0))

    def ring_step(i, s, q):
        for way in range(2):
            n = length(way, q)
            if s > n:
                continue
            if s > 1:
                ring_copy(i, way, q, s - 1).wait_recv()
                step = 1 if way == 0 else -1
                own = term(i, q, z + step * (n + 1 - s))[...].astype(F32)
                t = own + rring[i, way, q, s - 2].astype(F32)
                sring[i, way, q, s - 2] = t.astype(BF16)
            ring_copy(i, way, q, s).start()
            if i == 1 and s == n and q >= 2:
                if s == 1:
                    step = 1 if way == 0 else -1
                    t = term(i, q, z + step)[...].astype(F32)
                gain_term(q, t, 3 - way)

    def ring_steps(i, s):
        for q in CHUNKS:
            ring_step(i, s, q)

    def ring_sent(i):
        ways = len(CHUNKS) // 2
        if H > 1:
            some = rring.at[i, :, 0 : len(CHUNKS), 0 : H - 1]
            remote(some, some, ring_s.at[i, 0], ring_r.at[i, 0, 0, 0], at(dd=zdev(z + 1))).wait_send()
        some = rring.at[i, :, 0:ways, 0]
        remote(some, some, ring_s.at[i, 1], ring_r.at[i, 0, 0, 0], at(dd=zdev(z + 1))).wait_send()

    def gradient(i, terms, rows):
        for q in CHUNKS:
            if q % 2 == 0:
                for (n, _), row in zip(terms, rows):
                    scale_cot(n, row, y_of(q))
            tile(i, y_of(q), q % 2, terms)
            ring_step(i, 1, q)

    def y_copy(i, ch):
        return remote(sy.at[i, ch], ry.at[i, ch], y_s.at[i], y_r.at[i, ch], at(dd=z * NY + 1 - y))

    def y_sent(i):
        remote(sy.at[i], ry.at[i], y_s.at[i], y_r.at[i, 0], at(dd=z * NY + 1 - y)).wait_send()

    def ring_end(i):
        for q in CHUNKS:
            ch = q % 2
            if i == 1 and q == 2:
                gain_send()
            t = term(i, q, z)[...].astype(F32)
            for way in range(2):
                n = length(way, q)
                if n > 0:
                    ring_copy(i, way, q, n).wait_recv()
                    t = t + rring[i, way, q, n - 1].astype(F32)
            if q < 2:
                sy[i, ch] = t.astype(BF16)
                y_copy(i, ch).start()
                if i == 1:
                    gain_term(q, t, 0)
            else:
                own_t[i, :, ch * FH : (ch + 1) * FH] = t

    def grad_end(i):
        if NY == 2:
            for ch in range(2):
                cols = slice(ch * FH, (ch + 1) * FH)
                y_copy(i, ch).wait_recv()
                own_t[i, :, cols] = own_t[i, :, cols] + ry[i, ch].astype(F32)

    def g_copy(j):
        return remote(gsend, grecv.at[d], g_s, g_r, at(dd=dpeer(j)))

    def gain_send():
        ones = [jnp.sum(own_t[0] * w_two[...], axis=0, keepdims=True)]
        ones.append(
            jnp.concatenate([jnp.sum(sum(parts), axis=0, keepdims=True) for parts in gain_terms], axis=1)
        )
        tiles = []
        for i in range(2):
            row = jnp.concatenate([ones[i][:, t * HD : (t + 1) * HD] for t in range(LT)], axis=0)
            tiles.append(row / ngn_ref[pl.ds(i, LT, stride=2), :])
        gsend[...] = jnp.concatenate(tiles, axis=0).astype(BF16)
        for j in range(DP - 1, 0, -1):
            g_copy(j).start()
        grecv[d] = gsend[...]

    def g_all():
        some = grecv.at[0 : DP - 1]
        return remote(some, some, g_s, g_r, at(dd=dpeer(1)))

    def adam(i):
        rows = pl.ds(i, SH * LT, stride=2)
        grad = own_t[i].reshape(SH, LT, HD).reshape(SH * LT, HD)
        w = wbuf[rows, :]
        a = first_beta * m1buf[rows, :] + (1.0 - first_beta) * grad
        b = second_beta * m2buf[rows, :] + (1.0 - second_beta) * grad * grad
        m1_out[rows, :] = a
        m2_out[rows, :] = b
        ca = a * (1.0 / (1.0 - first_beta**adam_steps))
        cb = b * (1.0 / (1.0 - second_beta**adam_steps))
        w_out[rows, :] = w - learn_rate * (ca / (jnp.sqrt(cb) + 1e-08) + decay_rate * w)

    gradient(0, ((0, None),), (inv(sums(0, 0)),))

    for jy in range(MY):
        yl = flipped(ml, y_bits, jy)
        some = topb.at[0, 0 : MX - 1 if jy == 0 else MX]
        remote(some, some, o_s, o_r.at[yl], at(mm=peer(1))).wait_recv()

        def stats1(x, c):
            i = yl * MX + x
            l, v, t = native_block(lob[i, g]), native_block(mib[i, g]), native_block(topb[g, i])
            gl, gv, gt = l * g0, v * g1, t * g2
            rows = pl.ds(pl.multiple_of(i * SUB, SUB), SUB)
            for n, p in enumerate((t * t, gt * gt, gl * gt, gv * gt)):
                zbuf[n, rows, :] = fold(p)
            return c

        lax.fori_loop(0, MX, stats1, 0, unroll=4)
    ssend[1] = row_sums(4)
    def s2_copy(gg, j):
        return remote(ssend.at[1], srecv2.at[g * MP + m], s_s.at[1], s_r.at[1], at(gg=gg, mm=peer(j)))

    def s2_all():
        some = srecv2.at[0 : 2 * MP - 1]
        return remote(some, some, s_s.at[1], s_r.at[1], at(mm=peer(1)))

    for j in range(MP - 1, -1, -1):
        if j:
            s2_copy(g, j).start()
        s2_copy(1 - g, j).start()
    srecv2[g * MP + m] = ssend[1]
    top_copy = remote(topb.at[g], topb.at[g], top_s, top_r, at(gg=1 - g))
    top_copy.start()
    relayout_all(3, lambda i, gg: topb[gg, i], g)
    if H >= 2:
        ring_steps(0, 2)
    remote(topb.at[g], topb.at[1 - g], top_s, top_r, at(gg=1 - g)).wait_recv()
    relayout_all(3, lambda i, gg: topb[gg, i], 1 - g)

    def sent(block, count, sem, r):
        some = block.at[0:count]
        remote(some, some, sem, r, at(mm=peer(1))).wait_send()

    if H >= 3:
        ring_steps(0, 3)
    sent(rxq, MP - 1, q_s, q_r.at[0])
    sent(outb, MP - 1, o_s, o_r.at[0])
    s_all().wait_send()
    sent(cbuf, MX - 1, c2_s, c2_r)

    @pl.when(sends_cot)
    def _():
        some = ax.at[0, 0, 0 : (MY - 1) * CW // SH]
        remote(some, some, c_s, c_r.at[0], at(mm=peer(1))).wait_send()

    s2_all().wait_recv()
    for gg in range(2):
        red[1, gg] = jnp.sum(srecv2[gg * MP : (gg + 1) * MP], axis=0)

    rl, rv, rt = inv(sums(0, 1)), inv(sums(0, 2)), inv(sums(1, 0))
    joined = (
        rl * rl * sums(0, 3)
        + rv * rv * sums(0, 4)
        + rt * rt * sums(1, 1)
        + 2.0 * (rl * rv * sums(0, 5) + rl * rt * sums(1, 2) + rv * rt * sums(1, 3))
    )
    rj = inv(jnp.maximum(joined, 0.0))
    for way in range(2):
        wz_copy(way).wait_recv()
    gradient(1, ((1, 0), (2, 1), (3, 2)), (rl * rj, rv * rj, rt * rj))

    if NY == 2:
        w_copy().start()
    if H >= 4:
        ring_steps(0, 4)
    if H >= 2:
        ring_steps(1, 2)
    ring_end(0)
    if H >= 3:
        ring_steps(1, 3)
    for q in range(2, 4):
        gain_term(q, term(1, q, z)[...].astype(F32), 1)
    if H >= 4:
        ring_steps(1, 4)
    loads["m1"].wait()
    loads["m2"].wait()
    grad_end(0)
    adam(0)
    if NY == 2:
        w_copy().wait_recv()
    ring_end(1)
    grad_end(1)
    adam(1)

    s2_all().wait_send()
    red_copy().wait_send()
    top_copy.wait_send()
    for i in range(2):
        ring_sent(i)
        if NY == 2:
            y_sent(i)
    if NY == 2:
        w_copy().wait_send()
    for way in range(2):
        wz_copy(way).wait_send()

    g_all().wait_recv()
    gsib_s[...] = jnp.sum(grecv[...].astype(F32), axis=0)
    g_pair = remote(gsib_s, gsib_r, gx_s, gx_r, at(gg=1 - g))
    g_pair.start()
    g_all().wait_send()
    g_pair.wait_recv()
    total = gsib_s[...] + gsib_r[...]
    for i in range(2):
        gain_out[pl.ds(i, LT, stride=2), :] = total[i * LT : (i + 1) * LT]
    g_pair.wait_send()


def hand_on(*refs):
    n = len(refs) // 2
    sems = refs[-1]
    copies = [pltpu.make_async_copy(refs[i], refs[n + i], sems.at[i]) for i in range(n)]
    for copy in copies:
        copy.start()
    for copy in copies:
        copy.wait()


def shards(
    NZ, NY, MP,
    queries, cache_keys, cache_values, slot_keys, slot_values, cache_lengths,
    embeddings, layer_low, layer_mid, accepted, join_gain, norm_gain,
    key_cotangent, key_weight, moment_first, moment_second,
):
    rows, slots, F = embeddings.shape
    D = F * MP
    KW = cache_keys.shape[2]
    KVH = KW // HD
    SH = key_weight.shape[0]
    HC = SH * NZ * NY
    T = rows * slots
    TH = T // 2
    LT = F // HD
    H = NZ // 2
    MX = 4 if MP == 16 else 2
    YH = MP // MX // 2
    cols = key_cotangent.shape[2]
    DP = NZ * NY
    FH = F // 2

    def tokens(x):
        return native(x).reshape(MP, 2, 2 * LT * slots, HD)

    hbm = pl.BlockSpec(memory_space=pl.ANY)
    vmem = pl.BlockSpec(memory_space=pltpu.VMEM)
    smem = pl.BlockSpec(memory_space=pltpu.SMEM)
    dma = pltpu.SemaphoreType.DMA
    B = 2 * LT * slots
    shape = jax.ShapeDtypeStruct
    outs = pl.pallas_call(
        functools.partial(kernel, (NZ, NY, MP, MX, KVH, F, D, HC, SH)),
        out_shape=(
            pltpu.VMEM((SH * 2 * LT, HD), F32),
            pltpu.VMEM((SH * 2 * LT, HD), F32),
            pltpu.VMEM((SH * 2 * LT, HD), F32),
            pltpu.VMEM((2 * LT, HD), F32),
        ),
        in_specs=[hbm] * 5 + [smem] + [hbm] * 11,
        out_specs=(vmem, vmem, vmem, vmem),
        scratch_shapes=[
            pltpu.VMEM((KVH * 16, HD), BF16),
            pltpu.VMEM((KVH * 16, HD), BF16),
            pltpu.VMEM(key_cotangent.shape, BF16),
            pltpu.VMEM((1, rows), jnp.int32),
            pltpu.VMEM((3, F), F32),
            pltpu.VMEM((2, F), F32),
            pltpu.VMEM((2 * LT, HD), F32),
            pltpu.VMEM((MP, B, HD), BF16),
            pltpu.VMEM((2, 64, KW), BF16),
            pltpu.VMEM((2, 64, KW), BF16),
            pltpu.VMEM((MP, B, HD), BF16),
            pltpu.VMEM((MP, 2, B, HD), BF16),
            pltpu.VMEM((MP, 2, B, HD), BF16),
            pltpu.VMEM((MP, 2, B, HD), BF16),
            pltpu.VMEM((2, MP, B, HD), BF16),
            pltpu.VMEM((cols, T), BF16),
            pltpu.VMEM((MX, YH, cols, T), BF16),
            pltpu.VMEM((SH * 2 * LT, HD), F32),
            pltpu.VMEM((SH * 2 * LT, HD), F32),
            pltpu.VMEM((SH * 2 * LT, HD), F32),
            pltpu.VMEM((3, LT // 2, SUB, HD), F32),
            pltpu.VMEM((SUB, TH, HD), F32),
            pltpu.VMEM((2, SUB, TH), F32),
            pltpu.VMEM((MP, SUB, TH), F32),
            pltpu.VMEM((2 * MP, SUB, TH), F32),
            pltpu.VMEM((2, 2, SUB, TH), F32),
            pltpu.VMEM((4, T, F), BF16),
            pltpu.VMEM((4, NY, NZ, SH, T), BF16),
            pltpu.VMEM((2, NY, 2, NZ, SH, FH), BF16),
            pltpu.VMEM((2, 2, NQ, max(H - 1, 1), SH, FH), BF16),
            pltpu.VMEM((2, 2, NQ, H, SH, FH), BF16),
            pltpu.VMEM((2, 2, SH, FH), BF16),
            pltpu.VMEM((2, 2, SH, FH), BF16),
            pltpu.VMEM((2, SH, F), F32),
            pltpu.VMEM((SH, F), F32),
            pltpu.VMEM((4, SH, F), BF16),
            pltpu.VMEM((2 * LT, HD), BF16),
            pltpu.VMEM((DP, 2 * LT, HD), BF16),
            pltpu.VMEM((2 * LT, HD), F32),
            pltpu.VMEM((2 * LT, HD), F32),
            dma((16,)),
            dma, dma((MP // MX,)),
            dma, dma((YH,)), dma, dma,
            dma, dma((MP // MX,)),
            dma((2,)), dma((2,)),
            dma, dma,
            dma, dma,
            dma((2, 2)), dma((2, 2, NQ, H)),
            dma((2,)), dma((2, 2)),
            dma, dma,
            dma, dma((2,)),
            dma, dma,
            dma, dma,
        ],
        compiler_params=pltpu.CompilerParams(
            collective_id=0, has_side_effects=True, vmem_limit_bytes=VMEM_BYTES
        ),
        cost_estimate=pl.CostEstimate(
            flops=2 * 4 * HC * T * F, bytes_accessed=6 * 1024 * 1024, transcendentals=0
        ),
        name="draft_step",
    )(
        tokens(queries), cache_keys, cache_values, native(slot_keys), native(slot_values), cache_lengths,
        tokens(embeddings), tokens(layer_low), tokens(layer_mid), key_cotangent, accepted[None],
        join_gain, norm_gain, native(norm_gain[None]),
        native(key_weight), native(moment_first), native(moment_second),
    )
    outs = pl.pallas_call(
        hand_on,
        out_shape=[shape(x.shape, x.dtype) for x in outs],
        in_specs=[vmem] * 4,
        out_specs=[hbm] * 4,
        scratch_shapes=[dma((4,))],
        compiler_params=pltpu.CompilerParams(vmem_limit_bytes=VMEM_BYTES // 8),
        name="hand_on",
    )(*outs)
    new = [from_native(x, SH, 2, F) for x in outs[:3]]
    return (*new, from_native(outs[3], 1, 2, F)[0])


def solution(mesh, NY=2):
    NZ, MP = mesh.shape["dp"] // NY, mesh.shape["mp"]
    tokens, owners, moments = P("dp", None, "mp"), P(("dp", "mp"), None, None), P(("group", "dp"), None, "mp")
    return jax.shard_map(
        functools.partial(shards, NZ, NY, MP),
        mesh=mesh,
        in_specs=(
            tokens, owners, owners, owners, owners, P(("dp", "mp")), tokens, tokens, tokens, P("dp"),
            P(None, "mp"), P(None, "mp"), tokens, moments, moments, moments,
        ),
        out_specs=(moments, moments, moments, P(None, "mp")),
        check_vma=False,
    )
```

```python
import functools

import jax
import jax.numpy as jnp
from jax import lax
from jax.experimental import pallas as pl
from jax.experimental.pallas import tpu as pltpu
from jax.sharding import PartitionSpec as P

HD = 128
SUB = 8
VMEM_BYTES = 62 * 1024 * 1024
NQ = 4
EPS = 1e-05
first_beta = 0.9
second_beta = 0.95
learn_rate = 0.05
decay_rate = 0.1
adam_steps = 3
slot_decay = 0.8
MESH = pl.DeviceIdType.MESH
F32 = jnp.float32
BF16 = jnp.bfloat16


def native(x):
    rows, slots, width = x.shape
    x = x.reshape(rows, slots, width // HD, HD).transpose(0, 2, 1, 3)
    return x.reshape(rows * (width // HD) * slots, HD)


def from_native(y, rows, slots, width):
    y = y.reshape(rows, width // HD, slots, HD).transpose(0, 2, 1, 3)
    return y.reshape(rows, slots, width)


def dot_nt(a, b, **kw):
    return lax.dot_general(a, b, (((1,), (1,)), ((), ())), preferred_element_type=F32, **kw)


def swap_halves(x):
    return jnp.concatenate([x[:, 4:], x[:, :4]], axis=1)


def kernel(
    dims,
    q_hbm, ck_hbm, cv_hbm, sk_hbm, sv_hbm, len_ref, em_hbm, lo_hbm, mi_hbm, cot_hbm, acc_hbm,
    jg_hbm, ng_hbm, ngn_hbm, w_hbm, m1_hbm, m2_hbm,
    w_out, m1_out, m2_out, gain_out,
    sk_ref, sv_ref, cot_ref, acc_ref, jg_ref, ng_ref, ngn_ref, rxq, kbuf, vbuf, outb, emb, lob, mib, topb, csend, cbuf, wbuf, m1buf, m2buf,
    gpat, zbuf, ssend, srecv, srecv2, red, vx, vj, ax, aj, tb, sring, rring, sy, ry, own_t,
    w_two, wz, gsend, grecv, gsib_s, gsib_r,
    lsem, q_s, q_r, c_s, c_r, c2_s, c2_r, o_s, o_r, s_s, s_r, red_s, red_r, top_s, top_r,
    ring_s, ring_r, y_s, y_r, wx_s, wx_r, wz_s, wz_r, g_s, g_r, gx_s, gx_r,
):
    NZ, NY, MP, MX, KVH, F, D, HC, SH = dims
    MY = MP // MX
    YH = MY // 2
    LT = F // HD
    T = MP * 4 * SUB // 2
    TH = T // 2
    H = NZ // 2
    DP = NZ * NY
    FH = F // 2
    g = lax.axis_index("group")
    d = lax.axis_index("dp")
    m = lax.axis_index("mp")
    z, y = d // NY, lax.rem(d, NY)
    ml, mx = m // MX, lax.rem(m, MX)

    def at(gg=None, dd=None, mm=None):
        return (g if gg is None else gg, d if dd is None else dd, m if mm is None else mm)

    def zdev(zz):
        return lax.rem(zz + NZ, NZ) * NY + y

    def remote(src, dst, s, r, dev):
        return pltpu.make_async_remote_copy(
            src_ref=src, dst_ref=dst, send_sem=s, recv_sem=r, device_id=dev, device_id_type=MESH
        )

    def flips(a, n):
        return [(b, b * (1 - 2 * lax.rem(a // b, 2))) for b in (1, 2, 4, 8) if b < n]

    def flipped(a, bits, j):
        for b, delta in bits:
            if j & b:
                a = a + delta
        return a

    m_bits, d_bits, x_bits, y_bits = flips(m, MP), flips(d, DP), flips(mx, MX), flips(ml, MY)

    def peer(j):
        return flipped(m, m_bits, j)

    def dpeer(j):
        return flipped(d, d_bits, j)

    loads = {
        "cot": pltpu.make_async_copy(cot_hbm, cot_ref, lsem.at[9]),
        "acc": pltpu.make_async_copy(acc_hbm, acc_ref, lsem.at[10]),
        "jg": pltpu.make_async_copy(jg_hbm, jg_ref, lsem.at[11]),
        "lo": pltpu.make_async_copy(lo_hbm, lob, lsem.at[0]),
        "mi": pltpu.make_async_copy(mi_hbm, mib, lsem.at[1]),
        "em": pltpu.make_async_copy(em_hbm, emb, lsem.at[2]),
        "q": pltpu.make_async_copy(q_hbm.at[m, g], rxq.at[m], lsem.at[3]),
        "k": pltpu.make_async_copy(ck_hbm.at[pl.ds(2 * g, 2)], kbuf, lsem.at[4]),
        "v": pltpu.make_async_copy(cv_hbm.at[pl.ds(2 * g, 2)], vbuf, lsem.at[5]),
        "sk": pltpu.make_async_copy(sk_hbm, sk_ref, lsem.at[12]),
        "sv": pltpu.make_async_copy(sv_hbm, sv_ref, lsem.at[13]),
        "ng": pltpu.make_async_copy(ng_hbm, ng_ref, lsem.at[14]),
        "ngn": pltpu.make_async_copy(ngn_hbm, ngn_ref, lsem.at[15]),
        "w": pltpu.make_async_copy(w_hbm, wbuf, lsem.at[6]),
        "m1": pltpu.make_async_copy(m1_hbm, m1buf, lsem.at[7]),
        "m2": pltpu.make_async_copy(m2_hbm, m2buf, lsem.at[8]),
    }
    bar = pltpu.get_barrier_semaphore()

    greeted = [at(mm=peer(j)) for j in range(MP - 1, 0, -1)]
    greeted += [at(dd=z * NY + 1 - y)] if NY == 2 else []
    greeted += [at(dd=zdev(z + 1))] + ([at(dd=zdev(z - 1))] if NZ > 2 else []) + [at(gg=1 - g)]
    for dev in greeted:
        pl.semaphore_signal(bar, inc=1, device_id=dev, device_id_type=MESH)
    for load in loads.values():
        load.start()

    RD = 4 * MP
    loads["cot"].wait()
    loads["acc"].wait()
    ct = cot_ref[...].astype(F32).reshape(RD // 2, 2, 4, cot_ref.shape[2])
    ct = jnp.concatenate([ct[:, 0], ct[:, 1]], axis=1).reshape(MP, 2, SUB, cot_ref.shape[2])
    ct = jnp.concatenate([ct[:, 0], ct[:, 1]], axis=0).reshape(T, cot_ref.shape[2])
    token = lax.broadcasted_iota(jnp.int32, (RD, T), 1)
    quad = token // 4
    part = lax.rem(quad, RD // 2)
    row = (part // 2) * 4 + (quad // (RD // 2)) * 2 + lax.rem(part, 2)
    pick = (lax.broadcasted_iota(jnp.int32, (RD, T), 0) == row).astype(BF16)
    lengths = jnp.broadcast_to(acc_ref[...].astype(F32), (SUB, RD)).astype(BF16)
    taken = jnp.dot(lengths, pick, preferred_element_type=F32)[:1]
    slot = lax.rem(lax.broadcasted_iota(jnp.int32, (1, T), 1), 4)
    weight = jnp.zeros((1, T), F32)
    for s in range(4):
        weight = jnp.where((slot == s) & (taken > s + 0.5), jnp.float32(slot_decay**s), weight)
    csend[...] = (ct.T * weight).astype(BF16)

    sub8 = lax.broadcasted_iota(jnp.int32, (1, SUB, HD), 1) < 4
    loads["jg"].wait()
    for a in range(3):
        for lp in range(LT // 2):
            lower = jg_ref[a : a + 1, 2 * lp * HD : (2 * lp + 1) * HD]
            upper = jg_ref[a : a + 1, (2 * lp + 1) * HD : (2 * lp + 2) * HD]
            gpat[a, lp] = jnp.where(sub8[0], lower, upper)

    def native_block(x):
        return x.astype(F32).reshape(2, LT // 2, SUB, HD)

    def fold(p):
        t = jnp.sum(p, axis=1)
        t = t + swap_halves(t)
        return jnp.where(sub8[0], t[0], t[1])

    loads["lo"].wait()
    loads["mi"].wait()
    loads["em"].wait()
    g0, g1, g2 = gpat[0], gpat[1], gpat[2]

    def stats0(i, c):
        e, l, v = native_block(emb[i, g]), native_block(lob[i, g]), native_block(mib[i, g])
        gl, gv = l * g0, v * g1
        rows = pl.ds(pl.multiple_of(i * SUB, SUB), SUB)
        for n, p in enumerate((e * e, l * l, v * v, gl * gl, gv * gv, gl * gv)):
            zbuf[n, rows, :] = fold(p)
        return c

    lax.fori_loop(0, MP, stats0, 0)

    def row_sums(count):
        total = jnp.zeros((SUB, TH), F32)
        for n in range(count):
            pick = (lax.broadcasted_iota(jnp.int32, (SUB, HD), 0) == n).astype(F32)
            total = total + dot_nt(pick, zbuf[n], precision=lax.Precision.HIGHEST)
        return total

    ssend[0] = row_sums(6)

    def relayout(x, n):
        x = native_block(x)
        if n > 0:
            x = x * gpat[n - 1]
        a, b = x[0], x[1]
        return jnp.where(sub8, a, swap_halves(b)), jnp.where(sub8, swap_halves(a), b)

    def relayout_all(n, load, gg):
        def two(i, c):
            parts = [relayout(load(2 * i + h, gg), n) for h in range(2)]
            rows = pl.ds(pl.multiple_of(gg * TH + i * 2 * SUB, 2 * SUB), 2 * SUB)
            for lp in range(LT // 2):
                for k in range(2):
                    tile = jnp.concatenate([parts[0][k][lp], parts[1][k][lp]], axis=0)
                    lt = 2 * lp + k
                    if n == 0:
                        vx[rows, lt * HD : (lt + 1) * HD] = tile.astype(BF16)
                    else:
                        vj[n - 1, rows, lt * HD : (lt + 1) * HD] = tile.astype(BF16)
            return c

        lax.fori_loop(0, MP // 2, two, 0)

    for gg in range(2):
        relayout_all(0, lambda i, gg: emb[i, gg], gg)
    loads["w"].wait()
    for i in range(2):
        w = wbuf[pl.ds(i, SH * LT, stride=2), :].astype(BF16).astype(F32)
        w = w.reshape(SH, LT, HD).reshape(SH, F)
        if i == 0:
            w_two[...] = w
        else:
            wz[1] = w.astype(BF16)

    pl.semaphore_wait(bar, len(greeted))

    def q_copy(j):
        dst = peer(j)
        return remote(q_hbm.at[dst, g], rxq.at[m], q_s, q_r.at[ml], at(mm=dst))

    for j in range(MP - 1, 0, -1):
        q_copy(j).start()

    sends_cot = (ml // YH) == g
    mine = lax.rem(ml, YH)

    def c_copy(j):
        to = flipped(ml, y_bits, j) * MX + mx
        return remote(csend, cbuf.at[mx, mine], c_s, c_r.at[mine], at(mm=to))

    @pl.when(sends_cot)
    def _():
        cbuf[mx, mine] = csend[...]
        for j in range(MY - 1, 0, -1):
            c_copy(j).start()

    def c_forward(j):
        to = ml * MX + flipped(mx, x_bits, j)
        return remote(cbuf.at[mx], cbuf.at[mx], c2_s, c2_r, at(mm=to))

    def c_turn():
        for b in range(YH):

            @pl.when((YH * g + b) != ml)
            def _():
                remote(csend, cbuf.at[mx, b], c_s, c_r.at[b], at(mm=(YH * g + b) * MX + mx)).wait_recv()

        for j in range(MX - 1, 0, -1):
            c_forward(j).start()

    def c_end():
        remote(cbuf.at[0 : MX - 1], cbuf.at[0 : MX - 1], c2_s, c2_r, at(mm=peer(1))).wait_recv()

    for j in range(MP - 1, 0, -1):
        remote(ssend.at[0], srecv.at[m], s_s.at[0], s_r.at[0], at(mm=peer(j))).start()
    srecv[m] = ssend[0]

    def s_all():
        some = srecv.at[0 : MP - 1]
        return remote(some, some, s_s.at[0], s_r.at[0], at(mm=peer(1)))

    def red_copy():
        return remote(red.at[0, g], red.at[0, g], red_s, red_r, at(gg=1 - g))

    def w_copy():
        return remote(wz.at[1], wz.at[0], wx_s, wx_r, at(dd=z * NY + 1 - y))

    def wz_copy(way):
        return remote(wz.at[1], wz.at[2 + way], wz_s, wz_r.at[way], at(dd=zdev(z + 1 - 2 * way)))

    for way in range(2):
        wz_copy(way).start()

    for gg in range(2):
        relayout_all(1, lambda i, gg: lob[i, gg], gg)
        relayout_all(2, lambda i, gg: mib[i, gg], gg)

    loads["k"].wait()
    loads["v"].wait()
    loads["q"].wait()
    for key in ("sk", "sv", "ng", "ngn"):
        loads[key].wait()
    CP = 64
    SR = KVH * 4
    QR = 32
    rowi = lax.broadcasted_iota(jnp.int32, (2 * QR, HD), 0)
    coli = lax.broadcasted_iota(jnp.int32, (2 * QR, HD), 1)
    scol = coli - CP
    in_slots = (scol >= 0) & (scol < SR) & (lax.rem(scol, 4) <= lax.rem(rowi, 4))
    slot_head = scol // 4
    pad = jnp.zeros((HD - CP - SR, HD), BF16)
    slot_rows = [pl.ds(pl.multiple_of((2 * g + r) * SR, SR), SR) for r in range(2)]
    cached = [coli < jnp.minimum(len_ref[2 * g + r], CP) for r in range(2)]

    def o_copy(dst):
        return remote(outb.at[dst], topb.at[g, m], o_s, o_r.at[ml], at(mm=dst))

    def attend(k):
        cols = pl.ds(pl.multiple_of(k * HD, HD), HD)
        for r in range(2):
            qrows = slice(r * QR, (r + 1) * QR)
            qk = jnp.concatenate([rxq[2 * k, qrows, :], rxq[2 * k + 1, qrows, :]], axis=0)
            keys = jnp.concatenate([kbuf[r, :, cols], sk_ref[slot_rows[r], :], pad], axis=0)
            vals = jnp.concatenate([vbuf[r, :, cols], sv_ref[slot_rows[r], :], pad], axis=0)
            live = cached[r] | (in_slots & (slot_head == k))
            s = dot_nt(qk, keys) * (HD**-0.5)
            s = jnp.where(live, s, -1e30)
            top = jnp.max(s, axis=-1, keepdims=True)
            e = jnp.exp(s - top)
            p = (e * (1.0 / jnp.sum(e, axis=-1, keepdims=True))).astype(BF16)
            o = jnp.dot(p, vals, preferred_element_type=F32).astype(BF16)
            yield 2 * k, qrows, o[:QR]
            yield 2 * k + 1, qrows, o[QR:]

    for jy in range(MY):
        yl = flipped(ml, y_bits, jy)
        count = MX - 1 if jy == 0 else MX
        some = rxq.at[0:count]
        remote(some, some, q_s, q_r.at[yl], at(mm=peer(1))).wait_recv()
        done = []
        for h in range(MX // 2):
            done += list(attend(yl * (MX // 2) + h))
        for dst, qrows, o in done:
            outb[dst, qrows, :] = o
        for jx in range(MX):
            if jx or jy:
                o_copy(yl * MX + flipped(mx, x_bits, jx)).start()
        if jy == min(1, MY - 1):
            c_turn()
    topb[g, m] = outb[m]

    s_all().wait_recv()
    red[0, g] = jnp.sum(srecv[...], axis=0)
    red_copy().start()

    c_end()
    remote(red.at[0, g], red.at[0, 1 - g], red_s, red_r, at(gg=1 - g)).wait_recv()

    def sums(ph, n):
        return jnp.concatenate([red[ph, 0, n : n + 1, :], red[ph, 1, n : n + 1, :]], axis=1)

    def inv(total):
        return lax.rsqrt(total * (1.0 / D) + EPS)

    CW = HC // (YH * MX)

    def scale_cot(n, row, yy):
        here = pl.ds(pl.multiple_of(yy * SH, SH), SH)
        for b in range(YH):
            for x in range(MX):
                scaled = (cbuf[x, b, here, :].astype(F32) * row).astype(BF16)
                if n == 0:
                    ax[yy, b * MX + x] = scaled
                else:
                    aj[yy, b * MX + x, :, (n - 1) * T : n * T] = scaled

    scale = (2.0 * D) ** -0.5

    def tile(i, yy, ch):
        for h in range(2):
            cols = slice(ch * FH + h * FH // 2, ch * FH + (h + 1) * FH // 2)
            if i == 0:
                total = jnp.dot(ax[yy].reshape(NZ * SH, T), vx[:, cols], preferred_element_type=F32)
            else:
                gained = vj[:, :, cols].reshape(3 * T, FH // 2)
                total = jnp.dot(aj[yy].reshape(NZ * SH, 3 * T), gained, preferred_element_type=F32)
            total = (total * (ng_ref[i : i + 1, cols] * scale)).astype(BF16)
            tb[i, yy, ch, :, :, h * FH // 2 : (h + 1) * FH // 2] = total.reshape(NZ, SH, FH // 2)

    CHUNKS = [q for q in range(NQ) if NY == 2 or q >= 2]

    def y_of(q):
        return 1 - y if q < 2 else y

    def length(way, q):
        return H if (way == 0) == (q % 2 == 0) else H - 1

    def term(i, q, zz):
        return tb.at[i, y_of(q), q % 2, lax.rem(zz + NZ, NZ)]

    def ring_copy(i, way, q, s):
        step = 1 if way == 0 else -1
        src = term(i, q, z + step * length(way, q)) if s == 1 else sring.at[i, way, q, s - 2]
        return remote(
            src, rring.at[i, way, q, s - 1], ring_s.at[i, int(s == H)], ring_r.at[i, way, q, s - 1],
            at(dd=zdev(z + step)),
        )

    gain_terms = [[], []]

    def gain_term(q, t, place):
        ch = q % 2
        part = t * wz[place, :, ch * FH : (ch + 1) * FH].astype(F32)
        gain_terms[ch].append(jnp.sum(part.reshape(SH // SUB, SUB, FH), axis=0))

    def ring_step(i, s, q):
        for way in range(2):
            n = length(way, q)
            if s > n:
                continue
            if s > 1:
                ring_copy(i, way, q, s - 1).wait_recv()
                step = 1 if way == 0 else -1
                own = term(i, q, z + step * (n + 1 - s))[...].astype(F32)
                t = own + rring[i, way, q, s - 2].astype(F32)
                sring[i, way, q, s - 2] = t.astype(BF16)
            ring_copy(i, way, q, s).start()
            if i == 1 and s == n and q >= 2:
                if s == 1:
                    step = 1 if way == 0 else -1
                    t = term(i, q, z + step)[...].astype(F32)
                gain_term(q, t, 3 - way)

    def ring_steps(i, s):
        for q in CHUNKS:
            ring_step(i, s, q)

    def ring_sent(i):
        ways = len(CHUNKS) // 2
        if H > 1:
            some = rring.at[i, :, 0 : len(CHUNKS), 0 : H - 1]
            remote(some, some, ring_s.at[i, 0], ring_r.at[i, 0, 0, 0], at(dd=zdev(z + 1))).wait_send()
        some = rring.at[i, :, 0:ways, 0]
        remote(some, some, ring_s.at[i, 1], ring_r.at[i, 0, 0, 0], at(dd=zdev(z + 1))).wait_send()

    def gradient(i, terms, rows):
        for q in CHUNKS:
            if q % 2 == 0:
                for n, row in zip(terms, rows):
                    scale_cot(n, row, y_of(q))
            tile(i, y_of(q), q % 2)
            ring_step(i, 1, q)

    def y_copy(i, ch):
        return remote(sy.at[i, ch], ry.at[i, ch], y_s.at[i], y_r.at[i, ch], at(dd=z * NY + 1 - y))

    def y_sent(i):
        remote(sy.at[i], ry.at[i], y_s.at[i], y_r.at[i, 0], at(dd=z * NY + 1 - y)).wait_send()

    def ring_end(i):
        for q in CHUNKS:
            ch = q % 2
            if i == 1 and q == 2:
                gain_send()
            t = term(i, q, z)[...].astype(F32)
            for way in range(2):
                n = length(way, q)
                if n > 0:
                    ring_copy(i, way, q, n).wait_recv()
                    t = t + rring[i, way, q, n - 1].astype(F32)
            if q < 2:
                sy[i, ch] = t.astype(BF16)
                y_copy(i, ch).start()
                if i == 1:
                    gain_term(q, t, 0)
            else:
                own_t[i, :, ch * FH : (ch + 1) * FH] = t

    def grad_end(i):
        if NY == 2:
            for ch in range(2):
                cols = slice(ch * FH, (ch + 1) * FH)
                y_copy(i, ch).wait_recv()
                own_t[i, :, cols] = own_t[i, :, cols] + ry[i, ch].astype(F32)

    def g_copy(j):
        return remote(gsend, grecv.at[d], g_s, g_r, at(dd=dpeer(j)))

    def gain_send():
        ones = [jnp.sum(own_t[0] * w_two[...], axis=0, keepdims=True)]
        ones.append(
            jnp.concatenate([jnp.sum(sum(parts), axis=0, keepdims=True) for parts in gain_terms], axis=1)
        )
        tiles = []
        for i in range(2):
            row = jnp.concatenate([ones[i][:, t * HD : (t + 1) * HD] for t in range(LT)], axis=0)
            tiles.append(row / ngn_ref[pl.ds(i, LT, stride=2), :])
        gsend[...] = jnp.concatenate(tiles, axis=0).astype(BF16)
        for j in range(DP - 1, 0, -1):
            g_copy(j).start()
        grecv[d] = gsend[...]

    def g_all():
        some = grecv.at[0 : DP - 1]
        return remote(some, some, g_s, g_r, at(dd=dpeer(1)))

    def adam(i):
        rows = pl.ds(i, SH * LT, stride=2)
        grad = own_t[i].reshape(SH, LT, HD).reshape(SH * LT, HD)
        w = wbuf[rows, :]
        a = first_beta * m1buf[rows, :] + (1.0 - first_beta) * grad
        b = second_beta * m2buf[rows, :] + (1.0 - second_beta) * grad * grad
        m1_out[rows, :] = a
        m2_out[rows, :] = b
        ca = a * (1.0 / (1.0 - first_beta**adam_steps))
        cb = b * (1.0 / (1.0 - second_beta**adam_steps))
        w_out[rows, :] = w - learn_rate * (ca / (jnp.sqrt(cb) + 1e-08) + decay_rate * w)

    gradient(0, (0,), (inv(sums(0, 0)),))

    for jy in range(MY):
        yl = flipped(ml, y_bits, jy)
        some = topb.at[0, 0 : MX - 1 if jy == 0 else MX]
        remote(some, some, o_s, o_r.at[yl], at(mm=peer(1))).wait_recv()

        def stats1(x, c):
            i = yl * MX + x
            l, v, t = native_block(lob[i, g]), native_block(mib[i, g]), native_block(topb[g, i])
            gl, gv, gt = l * g0, v * g1, t * g2
            rows = pl.ds(pl.multiple_of(i * SUB, SUB), SUB)
            for n, p in enumerate((t * t, gt * gt, gl * gt, gv * gt)):
                zbuf[n, rows, :] = fold(p)
            return c

        lax.fori_loop(0, MX, stats1, 0, unroll=4)
    ssend[1] = row_sums(4)
    def s2_copy(gg, j):
        return remote(ssend.at[1], srecv2.at[g * MP + m], s_s.at[1], s_r.at[1], at(gg=gg, mm=peer(j)))

    def s2_all():
        some = srecv2.at[0 : 2 * MP - 1]
        return remote(some, some, s_s.at[1], s_r.at[1], at(mm=peer(1)))

    for j in range(MP - 1, -1, -1):
        if j:
            s2_copy(g, j).start()
        s2_copy(1 - g, j).start()
    srecv2[g * MP + m] = ssend[1]
    top_copy = remote(topb.at[g], topb.at[g], top_s, top_r, at(gg=1 - g))
    top_copy.start()
    relayout_all(3, lambda i, gg: topb[gg, i], g)
    if H >= 2:
        ring_steps(0, 2)
    remote(topb.at[g], topb.at[1 - g], top_s, top_r, at(gg=1 - g)).wait_recv()
    relayout_all(3, lambda i, gg: topb[gg, i], 1 - g)

    def sent(block, count, sem, r):
        some = block.at[0:count]
        remote(some, some, sem, r, at(mm=peer(1))).wait_send()

    if H >= 3:
        ring_steps(0, 3)
    sent(rxq, MP - 1, q_s, q_r.at[0])
    sent(outb, MP - 1, o_s, o_r.at[0])
    s_all().wait_send()
    sent(cbuf, MX - 1, c2_s, c2_r)

    @pl.when(sends_cot)
    def _():
        some = ax.at[0, 0 : (MY - 1) * CW // SH]
        remote(some, some, c_s, c_r.at[0], at(mm=peer(1))).wait_send()

    s2_all().wait_recv()
    for gg in range(2):
        red[1, gg] = jnp.sum(srecv2[gg * MP : (gg + 1) * MP], axis=0)

    rl, rv, rt = inv(sums(0, 1)), inv(sums(0, 2)), inv(sums(1, 0))
    joined = (
        rl * rl * sums(0, 3)
        + rv * rv * sums(0, 4)
        + rt * rt * sums(1, 1)
        + 2.0 * (rl * rv * sums(0, 5) + rl * rt * sums(1, 2) + rv * rt * sums(1, 3))
    )
    rj = inv(jnp.maximum(joined, 0.0))
    for way in range(2):
        wz_copy(way).wait_recv()
    gradient(1, (1, 2, 3), (rl * rj, rv * rj, rt * rj))

    if NY == 2:
        w_copy().start()
    if H >= 4:
        ring_steps(0, 4)
    if H >= 2:
        ring_steps(1, 2)
    ring_end(0)
    if H >= 3:
        ring_steps(1, 3)
    for q in range(2, 4):
        gain_term(q, term(1, q, z)[...].astype(F32), 1)
    if H >= 4:
        ring_steps(1, 4)
    loads["m1"].wait()
    loads["m2"].wait()
    grad_end(0)
    adam(0)
    if NY == 2:
        w_copy().wait_recv()
    ring_end(1)
    grad_end(1)
    adam(1)

    s2_all().wait_send()
    red_copy().wait_send()
    top_copy.wait_send()
    for i in range(2):
        ring_sent(i)
        if NY == 2:
            y_sent(i)
    if NY == 2:
        w_copy().wait_send()
    for way in range(2):
        wz_copy(way).wait_send()

    g_all().wait_recv()
    gsib_s[...] = jnp.sum(grecv[...].astype(F32), axis=0)
    g_pair = remote(gsib_s, gsib_r, gx_s, gx_r, at(gg=1 - g))
    g_pair.start()
    g_all().wait_send()
    g_pair.wait_recv()
    total = gsib_s[...] + gsib_r[...]
    for i in range(2):
        gain_out[pl.ds(i, LT, stride=2), :] = total[i * LT : (i + 1) * LT]
    g_pair.wait_send()


def hand_on(*refs):
    n = len(refs) // 2
    sems = refs[-1]
    copies = [pltpu.make_async_copy(refs[i], refs[n + i], sems.at[i]) for i in range(n)]
    for copy in copies:
        copy.start()
    for copy in copies:
        copy.wait()


def shards(
    NZ, NY, MP,
    queries, cache_keys, cache_values, slot_keys, slot_values, cache_lengths,
    embeddings, layer_low, layer_mid, accepted, join_gain, norm_gain,
    key_cotangent, key_weight, moment_first, moment_second,
):
    rows, slots, F = embeddings.shape
    D = F * MP
    KW = cache_keys.shape[2]
    KVH = KW // HD
    SH = key_weight.shape[0]
    HC = SH * NZ * NY
    T = rows * slots
    TH = T // 2
    LT = F // HD
    H = NZ // 2
    MX = 4 if MP == 16 else 2
    YH = MP // MX // 2
    cols = key_cotangent.shape[2]
    DP = NZ * NY
    FH = F // 2

    def tokens(x):
        return native(x).reshape(MP, 2, 2 * LT * slots, HD)

    hbm = pl.BlockSpec(memory_space=pl.ANY)
    vmem = pl.BlockSpec(memory_space=pltpu.VMEM)
    smem = pl.BlockSpec(memory_space=pltpu.SMEM)
    dma = pltpu.SemaphoreType.DMA
    B = 2 * LT * slots
    shape = jax.ShapeDtypeStruct
    outs = pl.pallas_call(
        functools.partial(kernel, (NZ, NY, MP, MX, KVH, F, D, HC, SH)),
        out_shape=(
            pltpu.VMEM((SH * 2 * LT, HD), F32),
            pltpu.VMEM((SH * 2 * LT, HD), F32),
            pltpu.VMEM((SH * 2 * LT, HD), F32),
            pltpu.VMEM((2 * LT, HD), F32),
        ),
        in_specs=[hbm] * 5 + [smem] + [hbm] * 11,
        out_specs=(vmem, vmem, vmem, vmem),
        scratch_shapes=[
            pltpu.VMEM((KVH * 16, HD), BF16),
            pltpu.VMEM((KVH * 16, HD), BF16),
            pltpu.VMEM(key_cotangent.shape, BF16),
            pltpu.VMEM((1, rows), jnp.int32),
            pltpu.VMEM((3, F), F32),
            pltpu.VMEM((2, F), F32),
            pltpu.VMEM((2 * LT, HD), F32),
            pltpu.VMEM((MP, B, HD), BF16),
            pltpu.VMEM((2, 64, KW), BF16),
            pltpu.VMEM((2, 64, KW), BF16),
            pltpu.VMEM((MP, B, HD), BF16),
            pltpu.VMEM((MP, 2, B, HD), BF16),
            pltpu.VMEM((MP, 2, B, HD), BF16),
            pltpu.VMEM((MP, 2, B, HD), BF16),
            pltpu.VMEM((2, MP, B, HD), BF16),
            pltpu.VMEM((cols, T), BF16),
            pltpu.VMEM((MX, YH, cols, T), BF16),
            pltpu.VMEM((SH * 2 * LT, HD), F32),
            pltpu.VMEM((SH * 2 * LT, HD), F32),
            pltpu.VMEM((SH * 2 * LT, HD), F32),
            pltpu.VMEM((3, LT // 2, SUB, HD), F32),
            pltpu.VMEM((SUB, TH, HD), F32),
            pltpu.VMEM((2, SUB, TH), F32),
            pltpu.VMEM((MP, SUB, TH), F32),
            pltpu.VMEM((2 * MP, SUB, TH), F32),
            pltpu.VMEM((2, 2, SUB, TH), F32),
            pltpu.VMEM((T, F), BF16),
            pltpu.VMEM((3, T, F), BF16),
            pltpu.VMEM((NY, NZ, SH, T), BF16),
            pltpu.VMEM((NY, NZ, SH, 3 * T), BF16),
            pltpu.VMEM((2, NY, 2, NZ, SH, FH), BF16),
            pltpu.VMEM((2, 2, NQ, max(H - 1, 1), SH, FH), BF16),
            pltpu.VMEM((2, 2, NQ, H, SH, FH), BF16),
            pltpu.VMEM((2, 2, SH, FH), BF16),
            pltpu.VMEM((2, 2, SH, FH), BF16),
            pltpu.VMEM((2, SH, F), F32),
            pltpu.VMEM((SH, F), F32),
            pltpu.VMEM((4, SH, F), BF16),
            pltpu.VMEM((2 * LT, HD), BF16),
            pltpu.VMEM((DP, 2 * LT, HD), BF16),
            pltpu.VMEM((2 * LT, HD), F32),
            pltpu.VMEM((2 * LT, HD), F32),
            dma((16,)),
            dma, dma((MP // MX,)),
            dma, dma((YH,)), dma, dma,
            dma, dma((MP // MX,)),
            dma((2,)), dma((2,)),
            dma, dma,
            dma, dma,
            dma((2, 2)), dma((2, 2, NQ, H)),
            dma((2,)), dma((2, 2)),
            dma, dma,
            dma, dma((2,)),
            dma, dma,
            dma, dma,
        ],
        compiler_params=pltpu.CompilerParams(
            collective_id=0, has_side_effects=True, vmem_limit_bytes=VMEM_BYTES
        ),
        cost_estimate=pl.CostEstimate(
            flops=2 * 4 * HC * T * F, bytes_accessed=6 * 1024 * 1024, transcendentals=0
        ),
        name="draft_step",
    )(
        tokens(queries), cache_keys, cache_values, native(slot_keys), native(slot_values), cache_lengths,
        tokens(embeddings), tokens(layer_low), tokens(layer_mid), key_cotangent, accepted[None],
        join_gain, norm_gain, native(norm_gain[None]),
        native(key_weight), native(moment_first), native(moment_second),
    )
    outs = pl.pallas_call(
        hand_on,
        out_shape=[shape(x.shape, x.dtype) for x in outs],
        in_specs=[vmem] * 4,
        out_specs=[hbm] * 4,
        scratch_shapes=[dma((4,))],
        compiler_params=pltpu.CompilerParams(vmem_limit_bytes=VMEM_BYTES // 8),
        name="hand_on",
    )(*outs)
    new = [from_native(x, SH, 2, F) for x in outs[:3]]
    return (*new, from_native(outs[3], 1, 2, F)[0])


def solution(mesh, NY=2):
    NZ, MP = mesh.shape["dp"] // NY, mesh.shape["mp"]
    tokens, owners, moments = P("dp", None, "mp"), P(("dp", "mp"), None, None), P(("group", "dp"), None, "mp")
    return jax.shard_map(
        functools.partial(shards, NZ, NY, MP),
        mesh=mesh,
        in_specs=(
            tokens, owners, owners, owners, owners, P(("dp", "mp")), tokens, tokens, tokens, P("dp"),
            P(None, "mp"), P(None, "mp"), tokens, moments, moments, moments,
        ),
        out_specs=(moments, moments, moments, P(None, "mp")),
        check_vma=False,
    )
```
